32 devices in a mesh: section: 2 (over x), ctx: 16 (over z, y, core).
Axes of the slice: x: 2, y: 2, z: 4, core: 2. Of those that a mesh axis runs over, the one named last changes fastest.
Arguments:
- inputs: bfloat16 [2048, 2048], P('ctx', 'section'), may hold values from -8 to 8
- out_grads: bfloat16 [2048, 2048], P('ctx', 'section'), may hold values from -6 to 6
- conv_weight: float32 [3, 4, 2048], P(None, None, 'section'), may hold values from -3 to 3
- log_decay: float32 [2048, 2048], P('ctx', 'section'), may hold values from -1 to 0
- beta: float32 [2048, 16], P('ctx', 'section'), may hold values from 0 to 1
Outputs:
- stream_out: bfloat16 [2048, 2048], P('ctx', 'section')
- input_grad: bfloat16 [2048, 2048], P('ctx', 'section')
The draws below stay inside these ranges and needn't reach their ends.
All inputs are finite; a program needn't handle non-finite values.
Results may differ from the reference program's by a relative error of at most 0.001.
Values sent between devices are 32-bit elements; how exact they have to be, the bound alone decides.
No kernel may reach another device: no remote copies, remote signals or barrier semaphores. Data moves between devices by JAX's collectives and lax.ppermute only.
A program may use at most 128 MiB of HBM per device.

```python
import math
import jax
import jax.numpy as jnp
from jax import lax

HEADS = 16
HEAD_DIM = 128
KERNEL = 4
TOK_DEV = 128
CHANNELS = 2048
TOKENS = 2048


def head_kinds(key):
    base = jax.random.fold_in(key, 11)
    share = 0.5
    return jax.random.uniform(base, (HEADS,)) < share


def draw_inputs(key, part):
    keys_all = jax.random.split(jax.random.fold_in(key, 41), 1)
    position = jnp.arange(CHANNELS).astype(jnp.float32) / CHANNELS
    rise = jnp.exp(0.5 * math.log(4.0) * position)
    values = jax.random.normal(keys_all[0], (TOKENS, CHANNELS), jnp.float32) * rise[None, :]
    return jnp.clip(values, -8.0, 8.0).astype(jnp.bfloat16)


def draw_log_decay(key, part):
    slow_factor = head_kinds(key)
    keys_all = jax.random.split(jax.random.fold_in(key, 23), 6)
    shape_rate = (1, HEADS, HEAD_DIM)
    slow_rate = math.log(10.0) / TOKENS * jnp.exp(jax.random.uniform(keys_all[0], shape_rate, jnp.float32, math.log(0.02), math.log(0.3)))
    fast_rate = jnp.exp(jax.random.uniform(keys_all[1], shape_rate, jnp.float32, math.log(1.0 / 50.0), math.log(1.0 / 20.0)))
    learning_rate = jnp.where(slow_factor[None, :, None], slow_rate, fast_rate)
    random_noise = jax.random.uniform(keys_all[2], (TOKENS, HEADS, HEAD_DIM), jnp.float32, 0.5, 1.5)
    block_count = TOKENS // TOK_DEV
    block_scale = jnp.exp(jax.random.uniform(keys_all[3], (block_count, 1, HEADS, 1), jnp.float32, math.log(0.5), math.log(2.0)))
    random_noise = (random_noise.reshape(block_count, TOK_DEV, HEADS, HEAD_DIM) * block_scale).reshape(TOKENS, HEADS, HEAD_DIM)
    spots = jax.random.randint(keys_all[4], (4,), 0, TOKENS)
    match_flag = jnp.any(jnp.arange(TOKENS)[:, None] == spots[None, :], axis=-1)
    stack_depth = jax.random.uniform(keys_all[5], (TOKENS, HEADS, 1), jnp.float32, 0.2, 0.5)
    spike_factor = jnp.where(match_flag[:, None, None] & slow_factor[None, :, None], jnp.log(1.0 - stack_depth), 0.0)
    final_result = -learning_rate * random_noise + spike_factor
    return final_result.reshape(TOKENS, HEADS * HEAD_DIM).astype(jnp.float32)


def draw_beta(key, part):
    slow_factor = head_kinds(key)
    keys_all = jax.random.split(jax.random.fold_in(key, 31), 2)
    limit = min(0.9, HEAD_DIM * math.log(10.0) / TOKENS)
    slow_beta = jax.random.uniform(keys_all[0], (TOKENS, HEADS), jnp.float32, 0.2, 1.0) * limit
    fast_beta = jax.random.uniform(keys_all[1], (TOKENS, HEADS), jnp.float32, 0.2, 0.9)
    return jnp.where(slow_factor[None, :], slow_beta, fast_beta).astype(jnp.float32)


def steps_of(rng, shape, cuts, smallest, high):
    gain = 1.0
    for axis_at, shards_of in cuts:
        draws = jax.random.uniform(jax.random.fold_in(jax.random.fold_in(rng, 6), axis_at), (shards_of,), jnp.float32, smallest / len(cuts), high / len(cuts))
        gain = gain * jnp.repeat(jnp.exp(draws), shape[axis_at] // shards_of).reshape((-1,) + (1,) * (len(shape) - 1 - axis_at))
    return gain


def bell_draw(own_key, shape, deviation, bound, pieces=(), kind=jnp.bfloat16):
    drawn = jax.random.normal(own_key, shape, jnp.float32) * deviation
    if len(pieces) > 0:
        drawn = steps_of(own_key, shape, pieces, -0.22, 0.18) * drawn
    return jnp.clip(drawn, min=-bound, max=bound).astype(kind)


def setup_inputs(seed: int = 0) -> dict:
    seeds = jax.random.split(jax.random.key(seed), 6)
    return {
        "inputs": draw_inputs(jax.random.fold_in(seeds[5], 71), 0),
        "out_grads": bell_draw(seeds[1], (TOKENS, CHANNELS), 1.0, 6.0, ((0, 16), (1, 2))),
        "conv_weight": bell_draw(seeds[2], (3, KERNEL, CHANNELS), KERNEL ** -0.5, 3.0, ((2, 2),), jnp.float32),
        "log_decay": draw_log_decay(jax.random.fold_in(seeds[5], 71), 0),
        "beta": draw_beta(jax.random.fold_in(seeds[5], 71), 0),
    }


epsilon = 1e-06
norm_eps = 1e-05
highest = lax.Precision.HIGHEST

def unit_rows(mixed):
    act = jax.nn.silu(mixed).reshape(mixed.shape[0], -1, HEAD_DIM)
    return act / jnp.sqrt(lax.optimization_barrier(jnp.sum(act * act, axis=-1, keepdims=True)) + epsilon)

def features(padded, kern):
    taps_count = kern.shape[1]
    length = padded.shape[0] - taps_count + 1
    mixes = [sum((kern[j, i] * padded[i:i + length] for i in range(taps_count))) for j in range(3)]
    queries = unit_rows(mixes[0])
    keys = unit_rows(mixes[1])
    values = jax.nn.silu(mixes[2]).reshape(length, -1, HEAD_DIM)
    return (queries, keys, values)

def solve_block(keys, values, cumulative, rates):
    length = keys.shape[0]
    middle = cumulative[length // 2]
    key_fwd = keys * jnp.exp(cumulative - middle)
    key_back = keys * jnp.exp(middle - cumulative)
    products = jnp.einsum('thc,shc->hts', key_fwd, key_back, precision=highest)
    strict_mask = jnp.tril(jnp.ones((length, length), jnp.float32), -1)
    rate_col = jnp.swapaxes(rates, 0, 1)[:, :, None]
    system = jnp.eye(length, dtype=jnp.float32) + rate_col * products * strict_mask
    rhs_keys = rate_col * jnp.swapaxes(keys * jnp.exp(cumulative), 0, 1)
    rhs_values = rate_col * jnp.swapaxes(values, 0, 1)
    solved = lax.linalg.triangular_solve(system, jnp.concatenate([rhs_keys, rhs_values], axis=-1), left_side=True, lower=True, unit_diagonal=True)
    return (solved[..., :HEAD_DIM], solved[..., HEAD_DIM:])

def transition(keys, cumulative, w_rows, u_rows):
    final_decay = cumulative[-1]
    key_end = keys * jnp.exp(final_decay - cumulative)
    retained = jnp.exp(final_decay)[:, :, None] * jnp.eye(HEAD_DIM, dtype=jnp.float32)
    transit = retained - jnp.einsum('thd,hte->hde', key_end, w_rows, precision=highest)
    inject = jnp.einsum('thd,hte->hde', key_end, u_rows, precision=highest)
    return (transit, inject)

def block_out(queries, keys, cumulative, w_rows, u_rows, start):
    length = queries.shape[0]
    middle = cumulative[length // 2]
    query_fwd = queries * jnp.exp(cumulative - middle)
    key_back = keys * jnp.exp(middle - cumulative)
    full_mask = jnp.tril(jnp.ones((length, length), jnp.float32))
    scores = jnp.einsum('thc,shc->hts', query_fwd, key_back, precision=highest) * full_mask
    fresh = u_rows - jnp.einsum('htd,hde->hte', w_rows, start, precision=highest)
    output = jnp.einsum('thd,hde->the', queries * jnp.exp(cumulative), start, precision=highest)
    output = output + jnp.einsum('hts,hse->the', scores, fresh, precision=highest)
    return output.reshape(length, -1)

def layer(stream_in, kern, decay, rates):
    stream = stream_in.astype(jnp.float32)
    scale = 1.0 / jnp.sqrt(lax.optimization_barrier(jnp.mean(stream * stream, axis=1, keepdims=True)) + norm_eps)
    normed = stream * scale
    padded = jnp.concatenate([jnp.zeros((KERNEL - 1, stream.shape[1]), jnp.float32), normed], axis=0)
    queries, keys, values = features(padded, kern)
    blocks = TOKENS // TOK_DEV
    parts = (queries.reshape(blocks, TOK_DEV, HEADS, HEAD_DIM), keys.reshape(blocks, TOK_DEV, HEADS, HEAD_DIM), values.reshape(blocks, TOK_DEV, HEADS, HEAD_DIM), decay.reshape(blocks, TOK_DEV, HEADS, HEAD_DIM), rates.reshape(blocks, TOK_DEV, HEADS))

    def advance(state, piece):
        query_b, key_b, value_b, decay_b, rate_b = piece
        cumulative = jnp.cumsum(decay_b, axis=0)
        w_rows, u_rows = solve_block(key_b, value_b, cumulative, rate_b)
        transit, inject = transition(key_b, cumulative, w_rows, u_rows)
        output = block_out(query_b, key_b, cumulative, w_rows, u_rows, state)
        following = jnp.einsum('hde,hef->hdf', transit, state, precision=highest) + inject
        return (following, output)
    initial = jnp.zeros((HEADS, HEAD_DIM, HEAD_DIM), jnp.float32)
    _, outputs = lax.scan(advance, initial, parts)
    return (stream + outputs.reshape(TOKENS, -1)).astype(jnp.bfloat16)

def reference(inputs, out_grads, conv_weight, log_decay, beta):
    stream_out, pull = jax.vjp(lambda a: layer(a, conv_weight, log_decay, beta), inputs)
    input_grad = pull(out_grads)[0].astype(jnp.bfloat16)
    return (stream_out, input_grad)
```

```python
import functools

import jax
import jax.numpy as jnp
from jax import lax
from jax.experimental import pallas as pl
from jax.experimental.pallas import tpu as pltpu
from jax.sharding import PartitionSpec as P

HEAD_DIM = 128
RIM = 8
epsilon = 1e-06
norm_eps = 1e-05
f32 = jnp.float32
bf16 = jnp.bfloat16
VMEM_LIMIT = 56 * 1024 * 1024

DIMS = {
    "nn": (((1,), (0,)), ((), ())),
    "nt": (((1,), (1,)), ((), ())),
    "tn": (((0,), (0,)), ((), ())),
}


def split(a):
    high = a.astype(bf16)
    return high, (a - high.astype(f32)).astype(bf16)


def exact(a):
    return a, None


def rows_of(*parts):
    highs = jnp.concatenate([p[0] for p in parts], axis=0)
    lows = [jnp.zeros_like(p[0]) if p[1] is None else p[1] for p in parts]
    return highs, jnp.concatenate(lows, axis=0)


def cols_of(*parts):
    return tuple(jnp.concatenate([p[i] for p in parts], axis=1) for i in range(2))


def mm(a, b, form):
    pairs = [(a[0], b[0])]
    if a[1] is not None:
        pairs.append((a[1], b[0]))
    if b[1] is not None:
        pairs.append((a[0], b[1]))
    left = jnp.concatenate([p[0] for p in pairs], axis=0 if form == "tn" else 1)
    right = jnp.concatenate([p[1] for p in pairs], axis=1 if form == "nt" else 0)
    return lax.dot_general(left, right, DIMS[form], preferred_element_type=f32)


def row_sums(a):
    high = a.astype(bf16)
    rest = a - high.astype(f32)
    mid = rest.astype(bf16)
    low = (rest - mid.astype(f32)).astype(bf16)
    terms = jnp.concatenate([high, mid, low], axis=1)
    ones = jnp.ones((RIM, terms.shape[1]), bf16)
    return lax.dot_general(ones, terms, DIMS["nt"], preferred_element_type=f32)


def down_rows(row):
    return jnp.transpose(jnp.broadcast_to(row[0:1], (HEAD_DIM, row.shape[1])))


def iotas(n=HEAD_DIM):
    return (
        lax.broadcasted_iota(jnp.int32, (n, n), 0),
        lax.broadcasted_iota(jnp.int32, (n, n), 1),
    )


def lane_slice(place):
    return pl.ds(pl.multiple_of(place * HEAD_DIM, HEAD_DIM), HEAD_DIM)


def prelude_kernel(x_ref, payload_ref, sums_ref):
    x = x_ref[...].astype(f32)
    channels = x.shape[1]
    sums = row_sums(x * x)
    sums_ref[...] = sums
    payload_ref[:, :channels] = x[x.shape[0] - RIM :]
    payload_ref[:, channels:] = sums


def inverse_all(systems):
    row, col = iotas()
    found = [jnp.where(row == col, 1.0, 0.0) - jnp.where((row >> 1 == col >> 1), n, 0.0) for n in systems]
    level = 1
    while (2 << level) <= HEAD_DIM:
        mask = (row >> (level + 1) == col >> (level + 1)) & (row >> level != col >> level)
        parts = [split(a) for a in found]
        cross = [split(jnp.where(mask, n, 0.0)) for n in systems]
        right = [split(mm(c, p, "nn")) for c, p in zip(cross, parts)]
        found = [a - mm(p, r, "nn") for a, p, r in zip(found, parts, right)]
        level += 1
    return found


def mixes_of(normed, rim, kern):
    row8 = lax.broadcasted_iota(jnp.int32, (RIM, HEAD_DIM), 0)
    taps = kern.shape[1]
    shifted = [normed]
    for s in range(1, taps):
        moved = pltpu.roll(normed, s, 0)
        first = jnp.where(row8 < s, pltpu.roll(rim, s, 0), moved[:RIM])
        shifted.append(jnp.concatenate([first, moved[RIM:]], axis=0))
    return [
        sum(kern[j, i : i + 1] * shifted[taps - 1 - i] for i in range(taps)) for j in range(3)
    ]


def local_kernel(
    heads, base, flags, x_ref, go_ref, kern_ref, decay_ref, beta_ref, rim_ref, scale_ref, rim_scale_ref,
    comp_ref, saved_ref,
):
    mask = flags[0]
    length = x_ref.shape[0]
    row, col = iotas()
    strict, full = row > col, row >= col
    scale = down_rows(scale_ref[...])
    rim_scale = down_rows(rim_scale_ref[...])[length - RIM :]
    lane8 = lax.broadcasted_iota(jnp.int32, beta_ref.shape, 1)
    tril = jnp.where(full, 1.0, 0.0).astype(bf16)
    tril = jnp.concatenate([tril] * 3, axis=1)
    data = []
    for j in range(heads):
        place = (j ^ mask) & (heads - 1)
        at = lane_slice(place)
        head = (base + j) ^ mask
        x = x_ref[:, at].astype(f32)
        kern = kern_ref[:, :, at]
        mixes = mixes_of(x * scale, rim_ref[:, at] * rim_scale, kern)
        sig = [1.0 / (1.0 + jnp.exp(-m)) for m in mixes]
        act = [m * s for m, s in zip(mixes, sig)]
        slope = [s * (1.0 + m * (1.0 - s)) for m, s in zip(mixes, sig)]
        inv = [lax.rsqrt(jnp.sum(a * a, axis=1, keepdims=True) + epsilon) for a in act[:2]]
        q, k = act[0] * inv[0], act[1] * inv[1]
        gq, gk = slope[0] * inv[0], slope[1] * inv[1]
        beta = jnp.sum(jnp.where(lane8 == head, beta_ref[...], 0.0), axis=1, keepdims=True)
        decay = decay_ref[:, at]
        high = decay.astype(bf16)
        rest = decay - high.astype(f32)
        mid = rest.astype(bf16)
        low = (rest - mid.astype(f32)).astype(bf16)
        cumulative = lax.dot_general(
            tril, jnp.concatenate([high, mid, low], axis=0), DIMS["nn"], preferred_element_type=f32
        )
        middle = cumulative[length // 2 : length // 2 + 1]
        final = cumulative[length - 1 : length]
        e1 = jnp.exp(cumulative - middle)
        e2 = jnp.exp(middle - cumulative)
        em = jnp.exp(middle)
        ecm = jnp.exp(final - middle)
        kf, qf, kb = k * e1, q * e1, k * e2
        data.append(
            dict(q=q, gq=gq, k=k, gk=gk, v=act[2], gv=slope[2], beta=beta, e1=e1, e2=e2, em=em, ecm=ecm,
                 ef=jnp.exp(final), kf=kf, qf=qf, kb=kb, at=at)
        )
    for d in data:
        d["skb"] = split(d["kb"])
        products = mm(rows_of(split(d["kf"]), split(d["qf"])), d["skb"], "nt")
        d["system"] = jnp.where(strict, d["beta"] * products[:length], 0.0)
        d["scores"] = split(jnp.where(full, products[length:], 0.0))
    inverses = inverse_all([d["system"] for d in data])
    for d, inverse in zip(data, inverses):
        d["inv"] = split(inverse)
        rhs = cols_of(split(d["beta"] * d["kf"] * d["em"]), split(d["beta"] * d["v"]))
        d["wu"] = mm(d["inv"], rhs, "nn")
        d["swu"] = split(d["wu"])
    for j, d in enumerate(data):
        ke = split(d["kb"] * d["ecm"])
        d["ke"] = ke
        maps = mm(ke, d["swu"], "tn")
        comp_ref[j, 0:128] = jnp.where(row == col, d["ef"], 0.0) - maps[:, :HEAD_DIM]
        comp_ref[j, 128:256] = maps[:, HEAD_DIM:]
        swu = mm(d["scores"], d["swu"], "nn")
        qs = d["qf"] * d["em"] - swu[:, :HEAD_DIM]
        go = exact(go_ref[:, d["at"]])
        comp_ref[j, 256:384] = mm(split(qs), go, "tn")
        fresh_grad = split(mm(d["scores"], go, "tn"))
        back = mm(d["inv"], cols_of(fresh_grad, ke), "tn")
        saved = [
            d["q"], d["gq"], d["k"], d["gk"], d["gv"], d["e1"], d["e2"], qs, d["wu"][:, :HEAD_DIM],
            swu[:, HEAD_DIM:], d["wu"][:, HEAD_DIM:], back[:, :HEAD_DIM], back[:, HEAD_DIM:],
        ]
        for n, a in enumerate(saved):
            saved_ref[j, n] = a
        saved_ref[j, len(saved), 0:8] = jnp.broadcast_to(d["em"], (8, HEAD_DIM))
        saved_ref[j, len(saved), 8:16] = jnp.broadcast_to(d["ecm"], (8, HEAD_DIM))


N_SAVED = 14


def compose_kernel(heads, bit, flags, keep_ref, recv_ref, *outs):
    later = flags[bit] != 0
    half = outs[0].shape[0]
    for j in range(heads):
        keep, recv = keep_ref[j], recv_ref[j]
        lo = jnp.where(later, recv, keep)
        hi = jnp.where(later, keep, recv)
        lo_map, hi_map = split(lo[0:128]), split(hi[0:128])
        forward = mm(hi_map, cols_of(lo_map, split(lo[128:256])), "nn")
        back = mm(lo_map, split(hi[256:384]), "tn")
        out, at = outs[j // half], j % half
        out[at, 0:128] = forward[:, :HEAD_DIM]
        out[at, 128:256] = forward[:, HEAD_DIM:] + hi[128:256]
        out[at, 256:384] = back + lo[256:384]


def last_compose_kernel(heads, bit, flags, keep_ref, recv_ref, t_ref, u_ref, g_ref):
    later = flags[bit] != 0
    for j in range(heads):
        keep, recv = keep_ref[j], recv_ref[j]
        lo = jnp.where(later, recv, keep)
        hi = jnp.where(later, keep, recv)
        lo_map, hi_map = split(lo[0:128]), split(hi[0:128])
        forward = mm(hi_map, cols_of(lo_map, split(lo[128:256])), "nn")
        back = mm(lo_map, split(hi[256:384]), "tn")
        t_ref[j] = forward[:, :HEAD_DIM]
        u_ref[j] = forward[:, HEAD_DIM:] + hi[128:256]
        g_ref[j] = back + lo[256:384]


def hop_kernel(t_ref, u_ref, g_ref, s_ref, e_ref, s_out, e_out):
    for j in range(t_ref.shape[0]):
        t = split(t_ref[j])
        s_out[j] = mm(t, split(s_ref[j]), "nn") + u_ref[j]
        e_out[j] = mm(t, split(e_ref[j]), "tn") + g_ref[j]


def down_kernel(bit, n_in, flags, keep_ref, recv_ref, *refs):
    ins, (mine_ref, send_ref) = refs[:n_in], refs[n_in:]
    later = flags[bit] != 0
    heads = keep_ref.shape[0]
    for j in range(heads):
        half = ins[0].shape[0]
        at = j % half
        if ins[0].shape[1] == HEAD_DIM:
            start, end = ins[0][at], ins[1][at]
        else:
            both = ins[j // half][at]
            start, end = both[:HEAD_DIM], both[HEAD_DIM:]
        keep, recv = keep_ref[j], recv_ref[j]
        lo = jnp.where(later, recv, keep)
        hi = jnp.where(later, keep, recv)
        start_hi = mm(split(lo[0:128]), split(start), "nn") + lo[128:256]
        end_lo = mm(split(hi[0:128]), split(end), "tn") + hi[256:384]
        mine_ref[j, 0:128] = jnp.where(later, start_hi, start)
        mine_ref[j, 128:256] = jnp.where(later, end, end_lo)
        send_ref[j, 0:128] = jnp.where(later, start, start_hi)
        send_ref[j, 128:256] = jnp.where(later, end_lo, end)


def back_kernel(
    heads, base, chained, flags, x_ref, go_ref, kern_ref, beta_ref, rim_ref, saved_ref, state_ref, *rest
):
    if chained:
        rest = rest[1:]
    out_ref, grad_ref, rim_grad_ref, sums_ref, rim_sums_ref = rest
    mask = flags[0]
    length = x_ref.shape[0]
    row, col = iotas()
    strict, full = row > col, row >= col
    lane8 = lax.broadcasted_iota(jnp.int32, beta_ref.shape, 1)
    taps = kern_ref.shape[1]
    dot_all = rim_dot = 0.0
    data = []
    for j in range(heads):
        place = (j ^ mask) & (heads - 1)
        at = lane_slice(place)
        head = (base + j) ^ mask
        start, end = split(state_ref[j, 0:128]), split(state_ref[j, 128:256])
        qs, w, o0, u, z0, kea = [saved_ref[j, 7 + n] for n in range(6)]
        first = mm(rows_of(split(qs), split(w)), start, "nn")
        z = z0 + mm(split(kea), end, "nn")
        x = x_ref[:, at].astype(f32)
        out_ref[:, at] = (x + (o0 + first[:length])).astype(bf16)
        data.append(
            dict(at=at, head=head, x=x, start=start, end=end, z=z, fresh=split(u - first[length:]))
        )
    for j, d in enumerate(data):
        q, gq, k, gk, gv, e1, e2 = [saved_ref[j, n] for n in range(7)]
        em, ecm = saved_ref[j, 13, 0:1], saved_ref[j, 13, 8:9]
        at = d["at"]
        beta = jnp.sum(jnp.where(lane8 == d["head"], beta_ref[...], 0.0), axis=1, keepdims=True)
        go = exact(go_ref[:, at])
        second = mm(rows_of(go, split(d["z"])), rows_of(d["fresh"], d["start"]), "nt")
        score_grad = split(jnp.where(full, second[:length, :HEAD_DIM], 0.0))
        product_grad = split(jnp.where(strict, -beta * second[length:, :HEAD_DIM], 0.0))
        qg_grad = second[:length, HEAD_DIM:]
        kg_grad = -beta * second[length:, HEAD_DIM:]
        ke_grad = mm(d["fresh"], d["end"], "nt")
        pair = rows_of(score_grad, product_grad)
        third = mm(pair, split(k * e2), "nn")
        kb_grad = mm(pair, rows_of(split(q * e1), split(k * e1)), "tn")
        q_grad = e1 * (third[:length] + em * qg_grad)
        k_grad = e1 * (third[length:] + em * kg_grad) + e2 * (kb_grad + ecm * ke_grad)
        mix_grads = [
            gq * (q_grad - q * jnp.sum(q * q_grad, axis=1, keepdims=True)),
            gk * (k_grad - k * jnp.sum(k * k_grad, axis=1, keepdims=True)),
            gv * (beta * d["z"]),
        ]
        kern = kern_ref[:, :, at]
        normed_grad = rim_grad = 0.0
        for i in range(taps):
            each = sum(kern[n, i : i + 1] * mix_grads[n] for n in range(3))
            s = taps - 1 - i
            if s == 0:
                normed_grad = normed_grad + each
            else:
                moved = pltpu.roll(each, length - s, 0)
                normed_grad = normed_grad + jnp.where(row < length - s, moved, 0.0)
                row8 = lax.broadcasted_iota(jnp.int32, (RIM, HEAD_DIM), 0)
                rim_grad = rim_grad + jnp.where(row8 >= RIM - s, moved[length - RIM :], 0.0)
        grad_ref[:, at] = normed_grad
        rim_grad_ref[:, at] = rim_grad
        dot_all = dot_all + normed_grad * d["x"]
        rim_dot = rim_dot + rim_grad * rim_ref[:, at]
    sums_ref[...] = row_sums(dot_all)
    rim_sums_ref[...] = jnp.broadcast_to(jnp.sum(rim_dot, axis=1, keepdims=True), rim_dot.shape)


def finish_kernel(
    groups, width, flags, x_ref, go_ref, scale_ref, inner_ref, next_sums_ref, *refs
):
    grads, next_rims, out_ref = refs[:groups], refs[groups : 2 * groups], refs[2 * groups]
    length = x_ref.shape[0]
    mask = flags[0]
    scale = down_rows(scale_ref[...])
    inner = down_rows(inner_ref[...])
    inner = jnp.concatenate([inner[: length - RIM], inner[length - RIM :] + next_sums_ref[...]], axis=0)
    cubed = scale * scale * scale * inner * (1.0 / width)
    span = grads[0].shape[1]
    per = span // HEAD_DIM
    for g in range(groups):
        grad_ref, next_ref = grads[g], next_rims[g]
        place = ((g * per) ^ mask) // per if groups > 1 else 0
        for n in range(per):
            here = slice(n * HEAD_DIM, (n + 1) * HEAD_DIM)
            at = lane_slice(place * per + n)
            grad = grad_ref[:, here]
            grad = jnp.concatenate([grad[: length - RIM], grad[length - RIM :] + next_ref[:, here]], axis=0)
            total = go_ref[:, at].astype(f32) + grad * scale - x_ref[:, at].astype(f32) * cubed
            out_ref[:, at] = total.astype(bf16)


def whole_call(kernel, outs, flags, *args, name=None, aliases=None, scalar=True):
    params = pltpu.CompilerParams(vmem_limit_bytes=VMEM_LIMIT)
    if not scalar:
        return pl.pallas_call(kernel, out_shape=outs, compiler_params=params, name=name)(*args)
    spec = pl.BlockSpec(memory_space=pltpu.VMEM)
    return pl.pallas_call(
        kernel,
        out_shape=outs,
        in_specs=[pl.BlockSpec(memory_space=pltpu.SMEM)] + [spec] * len(args),
        out_specs=jax.tree.map(lambda _: spec, outs),
        compiler_params=params,
        name=name,
    )(flags, *args)


def array(*shape, dtype=f32):
    return jax.ShapeDtypeStruct(shape, dtype)


def shards(inputs, out_grads, conv_weight, log_decay, beta):
    length, channels = inputs.shape
    heads = channels // HEAD_DIM
    sections, spots = lax.axis_size("section"), lax.axis_size("ctx")
    width = channels * sections
    me = lax.axis_index("ctx")
    levels = 0
    while (heads >> (levels + 1)) >= 1 and spots % (2 << levels) == 0:
        levels += 1
    slabs = spots >> levels
    bits = [(me >> n) & 1 for n in range(levels)]
    mask = sum(b * (heads >> (n + 1)) for n, b in enumerate(bits))
    flags = jnp.stack([mask] + bits).astype(jnp.int32)

    def turned(value, sec, shift):
        route = []
        for s in range(sections):
            for c in range(spots):
                if 0 <= c + shift < spots:
                    route.append((s * spots + c, ((s + sec) % sections) * spots + c + shift))
        return lax.ppermute(value, ("section", "ctx"), route)

    def swapped(value, level):
        return lax.ppermute(value, "ctx", [(i, i ^ (1 << level)) for i in range(spots)])

    def moved(value, shift):
        return lax.ppermute(
            value, "ctx", [(i, i + shift) for i in range(spots) if 0 <= i + shift < spots]
        )

    payload, sums = whole_call(
        prelude_kernel, (array(RIM, channels + length), array(RIM, length)), None, inputs,
        name="prelude", scalar=False,
    )
    rim = turned(payload, 0, 1)
    total = sums
    rim_total = rim[:, channels:]
    for sec in range(1, sections):
        total = total + turned(sums, sec, 0)
        rim_total = rim_total + turned(sums, sec, 1)
    scale = lax.rsqrt(total / width + norm_eps)
    rim_scale = lax.rsqrt(rim_total / width + norm_eps)

    groups = 2 if levels > 0 else 1
    per = heads // groups
    span = per * HEAD_DIM

    def block(shape, at, wide):
        lead = (0,) * (len(shape) - 1)
        return pl.BlockSpec(
            shape[:-1] + (span,), lambda i, f, lead=lead: lead + (((at * per) ^ f[0]) // per,)
        )

    def fixed(shape):
        return pl.BlockSpec(shape, lambda i, f, n=len(shape): (0,) * n)

    def grid_call(kernel, in_specs, out_specs, outs, args, name, aliases=None):
        return pl.pallas_call(
            kernel,
            grid_spec=pltpu.PrefetchScalarGridSpec(
                num_scalar_prefetch=1, grid=(1,), in_specs=in_specs, out_specs=out_specs
            ),
            out_shape=outs,
            input_output_aliases=aliases or {},
            compiler_params=pltpu.CompilerParams(vmem_limit_bytes=VMEM_LIMIT),
            name=name,
        )(flags, *args)

    rim_raw = rim[:, :channels]
    comps, saves = [None] * groups, [None] * groups
    for g in reversed(range(groups)):
        comps[g], saves[g] = grid_call(
            functools.partial(local_kernel, per, g * per),
            [
                block(inputs.shape, g, span), block(out_grads.shape, g, span), block(conv_weight.shape, g, span),
                block(log_decay.shape, g, span), fixed(beta.shape), block(rim_raw.shape, g, span),
                fixed(scale.shape), fixed(rim_scale.shape),
            ],
            [fixed((per, 384, HEAD_DIM)), fixed((per, N_SAVED, HEAD_DIM, HEAD_DIM))],
            [array(per, 384, HEAD_DIM), array(per, N_SAVED, HEAD_DIM, HEAD_DIM)],
            (inputs, out_grads, conv_weight, log_decay, beta, rim_raw, scale, rim_scale),
            name=f"local{g}",
        )

    history = []
    keep, send = comps[0], comps[-1]
    for level in range(levels):
        recv = swapped(send, level)
        history.append((keep, recv))
        n = keep.shape[0]
        if level + 1 < levels:
            keep, send = whole_call(
                functools.partial(compose_kernel, n, level + 1),
                (array(n // 2, 384, HEAD_DIM), array(n // 2, 384, HEAD_DIM)),
                flags, keep, recv, name=f"compose{level}",
            )
        else:
            t, u, g = whole_call(
                functools.partial(last_compose_kernel, n, level + 1),
                (array(n, HEAD_DIM, HEAD_DIM),) * 3,
                flags, keep, recv, name=f"compose{level}",
            )
    if levels == 0:
        t, u, g = keep[:, :128], keep[:, 128:256], keep[:, 256:]
    step = 1 << levels
    start, end = jnp.zeros_like(u), jnp.zeros_like(g)
    for hop in range(slabs - 1):
        if hop == 0:
            start, end = u, g
        else:
            start, end = whole_call(
                lambda flags, *refs: hop_kernel(*refs), (array(*u.shape),) * 2, flags, t, u, g, start, end,
                name=f"hop{hop}",
            )
        start, end = moved(start, step), moved(end, -step)
    states = (start, end)
    for level in reversed(range(levels)):
        keep, recv = history[level]
        n = keep.shape[0]
        mine, send = whole_call(
            functools.partial(down_kernel, level + 1, len(states)),
            (array(n, 256, HEAD_DIM),) * 2,
            flags, keep, recv, *states, name=f"down{level}",
        )
        states = (mine, swapped(send, level))
    if levels == 0:
        states = (jnp.concatenate([start, end], axis=1),)

    stream_out = None
    grads, rim_grads, inner, rim_sums = [], [], 0.0, 0.0
    for g in range(groups):
        args = [inputs, out_grads, conv_weight, beta, rim_raw, saves[g], states[g]]
        specs = [
            block(inputs.shape, g, span), block(out_grads.shape, g, span), block(conv_weight.shape, g, span),
            fixed(beta.shape), block(rim_raw.shape, g, span), fixed(saves[g].shape), fixed(states[g].shape),
        ]
        aliases = None
        if g > 0:
            args.append(stream_out)
            specs.append(pl.BlockSpec(memory_space=pl.ANY))
            aliases = {len(args): 0}
        stream_out, grad, rim_grad, part, rim_part = grid_call(
            functools.partial(back_kernel, per, g * per, g > 0),
            specs,
            [
                block(inputs.shape, g, span), fixed((length, span)), fixed((RIM, span)),
                fixed((RIM, length)), fixed((RIM, HEAD_DIM)),
            ],
            [
                array(*inputs.shape, dtype=bf16), array(length, span), array(RIM, span),
                array(RIM, length), array(RIM, HEAD_DIM),
            ],
            args, name=f"back{g}", aliases=aliases,
        )
        grads.append(grad)
        rim_grads.append(rim_grad)
        inner = inner + part
        rim_sums = rim_sums + rim_part

    next_rims = [turned(a, 0, -1) for a in reversed(rim_grads)]
    inner_total = inner
    next_sums = turned(rim_sums, 0, -1)
    for sec in range(1, sections):
        inner_total = inner_total + turned(inner, sec, 0)
        next_sums = next_sums + turned(rim_sums, sec, -1)
    input_grad = finish(
        flags, groups, width, inputs, out_grads, scale, inner_total, next_sums, grads, next_rims
    )
    return (stream_out, input_grad)


def finish(flags, groups, width, inputs, out_grads, scale, inner_total, next_sums, grads, next_rims):
    return whole_call(
        functools.partial(finish_kernel, groups, width),
        array(*inputs.shape, dtype=bf16),
        flags, inputs, out_grads, scale, inner_total, next_sums, *grads, *next_rims, name="finish",
    )


def solution(mesh):
    in_specs = (
        P("ctx", "section"),
        P("ctx", "section"),
        P(None, None, "section"),
        P("ctx", "section"),
        P("ctx", "section"),
    )
    out_specs = (P("ctx", "section"), P("ctx", "section"))
    return jax.shard_map(shards, mesh=mesh, in_specs=in_specs, out_specs=out_specs, check_vma=False)
```

```python
import functools

import jax
import jax.numpy as jnp
from jax import lax
from jax.experimental import pallas as pl
from jax.experimental.pallas import tpu as pltpu
from jax.sharding import PartitionSpec as P

HEAD_DIM = 128
RIM = 8
epsilon = 1e-06
norm_eps = 1e-05
f32 = jnp.float32
bf16 = jnp.bfloat16
VMEM_LIMIT = 24 * 1024 * 1024

DIMS = {
    "nn": (((1,), (0,)), ((), ())),
    "nt": (((1,), (1,)), ((), ())),
    "tn": (((0,), (0,)), ((), ())),
}


def split(a):
    high = a.astype(bf16)
    return high, (a - high.astype(f32)).astype(bf16)


def exact(a):
    return a, None


def rows_of(*parts):
    highs = jnp.concatenate([p[0] for p in parts], axis=0)
    lows = [jnp.zeros_like(p[0]) if p[1] is None else p[1] for p in parts]
    return highs, jnp.concatenate(lows, axis=0)


def cols_of(*parts):
    return tuple(jnp.concatenate([p[i] for p in parts], axis=1) for i in range(2))


def mm(a, b, form):
    pairs = [(a[0], b[0])]
    if a[1] is not None:
        pairs.append((a[1], b[0]))
    if b[1] is not None:
        pairs.append((a[0], b[1]))
    left = jnp.concatenate([p[0] for p in pairs], axis=0 if form == "tn" else 1)
    right = jnp.concatenate([p[1] for p in pairs], axis=1 if form == "nt" else 0)
    return lax.dot_general(left, right, DIMS[form], preferred_element_type=f32)


def row_sums(a):
    high = a.astype(bf16)
    rest = a - high.astype(f32)
    mid = rest.astype(bf16)
    low = (rest - mid.astype(f32)).astype(bf16)
    terms = jnp.concatenate([high, mid, low], axis=1)
    ones = jnp.ones((RIM, terms.shape[1]), bf16)
    return lax.dot_general(ones, terms, DIMS["nt"], preferred_element_type=f32)


def down_rows(row):
    return jnp.transpose(jnp.broadcast_to(row[0:1], (HEAD_DIM, row.shape[1])))


def iotas(n=HEAD_DIM):
    return (
        lax.broadcasted_iota(jnp.int32, (n, n), 0),
        lax.broadcasted_iota(jnp.int32, (n, n), 1),
    )


def lane_slice(place):
    return pl.ds(pl.multiple_of(place * HEAD_DIM, HEAD_DIM), HEAD_DIM)


def prelude_kernel(x_ref, payload_ref, sums_ref):
    x = x_ref[...].astype(f32)
    channels = x.shape[1]
    sums = row_sums(x * x)
    sums_ref[...] = sums
    payload_ref[:, :channels] = x[x.shape[0] - RIM :]
    payload_ref[:, channels:] = sums


def inverse_all(systems):
    row, col = iotas()
    found = [jnp.where(row == col, 1.0, 0.0) - jnp.where((row >> 1 == col >> 1), n, 0.0) for n in systems]
    level = 1
    while (2 << level) <= HEAD_DIM:
        mask = (row >> (level + 1) == col >> (level + 1)) & (row >> level != col >> level)
        parts = [split(a) for a in found]
        cross = [split(jnp.where(mask, n, 0.0)) for n in systems]
        right = [split(mm(c, p, "nn")) for c, p in zip(cross, parts)]
        found = [a - mm(p, r, "nn") for a, p, r in zip(found, parts, right)]
        level += 1
    return found


def mixes_of(normed, rim, kern):
    row8 = lax.broadcasted_iota(jnp.int32, (RIM, HEAD_DIM), 0)
    taps = kern.shape[1]
    shifted = [normed]
    for s in range(1, taps):
        moved = pltpu.roll(normed, s, 0)
        first = jnp.where(row8 < s, pltpu.roll(rim, s, 0), moved[:RIM])
        shifted.append(jnp.concatenate([first, moved[RIM:]], axis=0))
    return [
        sum(kern[j, i : i + 1] * shifted[taps - 1 - i] for i in range(taps)) for j in range(3)
    ]


def local_kernel(
    heads, base, flags, x_ref, go_ref, kern_ref, decay_ref, beta_ref, rim_ref, scale_ref, rim_scale_ref,
    comp_ref, saved_ref,
):
    mask = flags[0]
    length = x_ref.shape[0]
    row, col = iotas()
    strict, full = row > col, row >= col
    scale = down_rows(scale_ref[...])
    rim_scale = down_rows(rim_scale_ref[...])[length - RIM :]
    lane8 = lax.broadcasted_iota(jnp.int32, beta_ref.shape, 1)
    tril = jnp.where(full, 1.0, 0.0).astype(bf16)
    tril = jnp.concatenate([tril] * 3, axis=1)
    data = []
    for j in range(heads):
        place = (j ^ mask) & (heads - 1)
        at = lane_slice(place)
        head = (base + j) ^ mask
        x = x_ref[:, at].astype(f32)
        kern = kern_ref[:, :, at]
        mixes = mixes_of(x * scale, rim_ref[:, at] * rim_scale, kern)
        sig = [1.0 / (1.0 + jnp.exp(-m)) for m in mixes]
        act = [m * s for m, s in zip(mixes, sig)]
        slope = [s * (1.0 + m * (1.0 - s)) for m, s in zip(mixes, sig)]
        inv = [lax.rsqrt(jnp.sum(a * a, axis=1, keepdims=True) + epsilon) for a in act[:2]]
        q, k = act[0] * inv[0], act[1] * inv[1]
        gq, gk = slope[0] * inv[0], slope[1] * inv[1]
        beta = jnp.sum(jnp.where(lane8 == head, beta_ref[...], 0.0), axis=1, keepdims=True)
        decay = decay_ref[:, at]
        high = decay.astype(bf16)
        rest = decay - high.astype(f32)
        mid = rest.astype(bf16)
        low = (rest - mid.astype(f32)).astype(bf16)
        cumulative = lax.dot_general(
            tril, jnp.concatenate([high, mid, low], axis=0), DIMS["nn"], preferred_element_type=f32
        )
        middle = cumulative[length // 2 : length // 2 + 1]
        final = cumulative[length - 1 : length]
        e1 = jnp.exp(cumulative - middle)
        e2 = jnp.exp(middle - cumulative)
        em = jnp.exp(middle)
        ecm = jnp.exp(final - middle)
        kf, qf, kb = k * e1, q * e1, k * e2
        data.append(
            dict(q=q, gq=gq, k=k, gk=gk, v=act[2], gv=slope[2], beta=beta, e1=e1, e2=e2, em=em, ecm=ecm,
                 ef=jnp.exp(final), kf=kf, qf=qf, kb=kb, at=at)
        )
    for d in data:
        d["skb"] = split(d["kb"])
        products = mm(rows_of(split(d["kf"]), split(d["qf"])), d["skb"], "nt")
        d["system"] = jnp.where(strict, d["beta"] * products[:length], 0.0)
        d["scores"] = split(jnp.where(full, products[length:], 0.0))
    inverses = inverse_all([d["system"] for d in data])
    for d, inverse in zip(data, inverses):
        d["inv"] = split(inverse)
        rhs = cols_of(split(d["beta"] * d["kf"] * d["em"]), split(d["beta"] * d["v"]))
        d["wu"] = mm(d["inv"], rhs, "nn")
        d["swu"] = split(d["wu"])
    for j, d in enumerate(data):
        ke = split(d["kb"] * d["ecm"])
        d["ke"] = ke
        maps = mm(ke, d["swu"], "tn")
        comp_ref[j, 0:128] = jnp.where(row == col, d["ef"], 0.0) - maps[:, :HEAD_DIM]
        comp_ref[j, 128:256] = maps[:, HEAD_DIM:]
        swu = mm(d["scores"], d["swu"], "nn")
        qs = d["qf"] * d["em"] - swu[:, :HEAD_DIM]
        go = exact(go_ref[:, d["at"]])
        comp_ref[j, 256:384] = mm(split(qs), go, "tn")
        fresh_grad = split(mm(d["scores"], go, "tn"))
        back = mm(d["inv"], cols_of(fresh_grad, ke), "tn")
        saved = [
            d["q"], d["gq"], d["k"], d["gk"], d["gv"], d["e1"], d["e2"], qs, d["wu"][:, :HEAD_DIM],
            swu[:, HEAD_DIM:], d["wu"][:, HEAD_DIM:], back[:, :HEAD_DIM], back[:, HEAD_DIM:],
        ]
        for n, a in enumerate(saved):
            saved_ref[j, n] = a
        saved_ref[j, len(saved), 0:8] = jnp.broadcast_to(d["em"], (8, HEAD_DIM))
        saved_ref[j, len(saved), 8:16] = jnp.broadcast_to(d["ecm"], (8, HEAD_DIM))


N_SAVED = 14


def compose_kernel(heads, bit, flags, keep_ref, recv_ref, *outs):
    later = flags[bit] != 0
    half = outs[0].shape[0]
    for j in range(heads):
        keep, recv = keep_ref[j], recv_ref[j]
        lo = jnp.where(later, recv, keep)
        hi = jnp.where(later, keep, recv)
        lo_map, hi_map = split(lo[0:128]), split(hi[0:128])
        forward = mm(hi_map, cols_of(lo_map, split(lo[128:256])), "nn")
        back = mm(lo_map, split(hi[256:384]), "tn")
        out, at = outs[j // half], j % half
        out[at, 0:128] = forward[:, :HEAD_DIM]
        out[at, 128:256] = forward[:, HEAD_DIM:] + hi[128:256]
        out[at, 256:384] = back + lo[256:384]


def last_compose_kernel(heads, bit, flags, keep_ref, recv_ref, t_ref, u_ref, g_ref):
    later = flags[bit] != 0
    for j in range(heads):
        keep, recv = keep_ref[j], recv_ref[j]
        lo = jnp.where(later, recv, keep)
        hi = jnp.where(later, keep, recv)
        lo_map, hi_map = split(lo[0:128]), split(hi[0:128])
        forward = mm(hi_map, cols_of(lo_map, split(lo[128:256])), "nn")
        back = mm(lo_map, split(hi[256:384]), "tn")
        t_ref[j] = forward[:, :HEAD_DIM]
        u_ref[j] = forward[:, HEAD_DIM:] + hi[128:256]
        g_ref[j] = back + lo[256:384]


def hop_kernel(t_ref, u_ref, g_ref, s_ref, e_ref, s_out, e_out):
    for j in range(t_ref.shape[0]):
        t = split(t_ref[j])
        s_out[j] = mm(t, split(s_ref[j]), "nn") + u_ref[j]
        e_out[j] = mm(t, split(e_ref[j]), "tn") + g_ref[j]


def down_kernel(bit, n_in, flags, keep_ref, recv_ref, *refs):
    ins, (mine_ref, send_ref) = refs[:n_in], refs[n_in:]
    later = flags[bit] != 0
    heads = keep_ref.shape[0]
    for j in range(heads):
        half = ins[0].shape[0]
        at = j % half
        if ins[0].shape[1] == HEAD_DIM:
            start, end = ins[0][at], ins[1][at]
        else:
            both = ins[j // half][at]
            start, end = both[:HEAD_DIM], both[HEAD_DIM:]
        keep, recv = keep_ref[j], recv_ref[j]
        lo = jnp.where(later, recv, keep)
        hi = jnp.where(later, keep, recv)
        start_hi = mm(split(lo[0:128]), split(start), "nn") + lo[128:256]
        end_lo = mm(split(hi[0:128]), split(end), "tn") + hi[256:384]
        mine_ref[j, 0:128] = jnp.where(later, start_hi, start)
        mine_ref[j, 128:256] = jnp.where(later, end, end_lo)
        send_ref[j, 0:128] = jnp.where(later, start, start_hi)
        send_ref[j, 128:256] = jnp.where(later, end_lo, end)


def back_kernel(
    heads, base, chained, flags, x_ref, go_ref, kern_ref, beta_ref, rim_ref, saved_ref, state_ref, *rest
):
    if chained:
        rest = rest[1:]
    out_ref, grad_ref, rim_grad_ref, sums_ref, rim_sums_ref = rest
    mask = flags[0]
    length = x_ref.shape[0]
    row, col = iotas()
    strict, full = row > col, row >= col
    lane8 = lax.broadcasted_iota(jnp.int32, beta_ref.shape, 1)
    taps = kern_ref.shape[1]
    dot_all = rim_dot = 0.0
    data = []
    for j in range(heads):
        place = (j ^ mask) & (heads - 1)
        at = lane_slice(place)
        head = (base + j) ^ mask
        start, end = split(state_ref[j, 0:128]), split(state_ref[j, 128:256])
        qs, w, o0, u, z0, kea = [saved_ref[j, 7 + n] for n in range(6)]
        first = mm(rows_of(split(qs), split(w)), start, "nn")
        z = z0 + mm(split(kea), end, "nn")
        x = x_ref[:, at].astype(f32)
        out_ref[:, at] = (x + (o0 + first[:length])).astype(bf16)
        data.append(
            dict(at=at, head=head, x=x, start=start, end=end, z=z, fresh=split(u - first[length:]))
        )
    for j, d in enumerate(data):
        q, gq, k, gk, gv, e1, e2 = [saved_ref[j, n] for n in range(7)]
        em, ecm = saved_ref[j, 13, 0:1], saved_ref[j, 13, 8:9]
        at = d["at"]
        beta = jnp.sum(jnp.where(lane8 == d["head"], beta_ref[...], 0.0), axis=1, keepdims=True)
        go = exact(go_ref[:, at])
        second = mm(rows_of(go, split(d["z"])), rows_of(d["fresh"], d["start"]), "nt")
        score_grad = split(jnp.where(full, second[:length, :HEAD_DIM], 0.0))
        product_grad = split(jnp.where(strict, -beta * second[length:, :HEAD_DIM], 0.0))
        qg_grad = second[:length, HEAD_DIM:]
        kg_grad = -beta * second[length:, HEAD_DIM:]
        ke_grad = mm(d["fresh"], d["end"], "nt")
        pair = rows_of(score_grad, product_grad)
        third = mm(pair, split(k * e2), "nn")
        kb_grad = mm(pair, rows_of(split(q * e1), split(k * e1)), "tn")
        q_grad = e1 * (third[:length] + em * qg_grad)
        k_grad = e1 * (third[length:] + em * kg_grad) + e2 * (kb_grad + ecm * ke_grad)
        mix_grads = [
            gq * (q_grad - q * jnp.sum(q * q_grad, axis=1, keepdims=True)),
            gk * (k_grad - k * jnp.sum(k * k_grad, axis=1, keepdims=True)),
            gv * (beta * d["z"]),
        ]
        kern = kern_ref[:, :, at]
        normed_grad = rim_grad = 0.0
        for i in range(taps):
            each = sum(kern[n, i : i + 1] * mix_grads[n] for n in range(3))
            s = taps - 1 - i
            if s == 0:
                normed_grad = normed_grad + each
            else:
                moved = pltpu.roll(each, length - s, 0)
                normed_grad = normed_grad + jnp.where(row < length - s, moved, 0.0)
                row8 = lax.broadcasted_iota(jnp.int32, (RIM, HEAD_DIM), 0)
                rim_grad = rim_grad + jnp.where(row8 >= RIM - s, moved[length - RIM :], 0.0)
        grad_ref[:, at] = normed_grad
        rim_grad_ref[:, at] = rim_grad
        dot_all = dot_all + normed_grad * d["x"]
        rim_dot = rim_dot + rim_grad * rim_ref[:, at]
    sums_ref[...] = row_sums(dot_all)
    rim_sums_ref[...] = jnp.broadcast_to(jnp.sum(rim_dot, axis=1, keepdims=True), rim_dot.shape)


def finish_kernel(
    groups, width, flags, x_ref, go_ref, scale_ref, inner_ref, next_sums_ref, *refs
):
    grads, next_rims, out_ref = refs[:groups], refs[groups : 2 * groups], refs[2 * groups]
    length = x_ref.shape[0]
    mask = flags[0]
    scale = down_rows(scale_ref[...])
    inner = down_rows(inner_ref[...])
    inner = jnp.concatenate([inner[: length - RIM], inner[length - RIM :] + next_sums_ref[...]], axis=0)
    cubed = scale * scale * scale * inner * (1.0 / width)
    span = grads[0].shape[1]
    per = span // HEAD_DIM
    for g in range(groups):
        grad_ref, next_ref = grads[g], next_rims[g]
        place = ((g * per) ^ mask) // per if groups > 1 else 0
        for n in range(per):
            here = slice(n * HEAD_DIM, (n + 1) * HEAD_DIM)
            at = lane_slice(place * per + n)
            grad = grad_ref[:, here]
            grad = jnp.concatenate([grad[: length - RIM], grad[length - RIM :] + next_ref[:, here]], axis=0)
            total = go_ref[:, at].astype(f32) + grad * scale - x_ref[:, at].astype(f32) * cubed
            out_ref[:, at] = total.astype(bf16)


def whole_call(kernel, outs, flags, *args, name=None, aliases=None, scalar=True):
    params = pltpu.CompilerParams(vmem_limit_bytes=VMEM_LIMIT)
    if not scalar:
        return pl.pallas_call(kernel, out_shape=outs, compiler_params=params, name=name)(*args)
    spec = pl.BlockSpec(memory_space=pltpu.VMEM)
    return pl.pallas_call(
        kernel,
        out_shape=outs,
        in_specs=[pl.BlockSpec(memory_space=pltpu.SMEM)] + [spec] * len(args),
        out_specs=jax.tree.map(lambda _: spec, outs),
        compiler_params=params,
        name=name,
    )(flags, *args)


def array(*shape, dtype=f32):
    return jax.ShapeDtypeStruct(shape, dtype)


def shards(inputs, out_grads, conv_weight, log_decay, beta):
    length, channels = inputs.shape
    heads = channels // HEAD_DIM
    sections, spots = lax.axis_size("section"), lax.axis_size("ctx")
    width = channels * sections
    me = lax.axis_index("ctx")
    levels = 0
    while (heads >> (levels + 1)) >= 1 and spots % (2 << levels) == 0:
        levels += 1
    slabs = spots >> levels
    bits = [(me >> n) & 1 for n in range(levels)]
    mask = sum(b * (heads >> (n + 1)) for n, b in enumerate(bits))
    flags = jnp.stack([mask] + bits).astype(jnp.int32)

    def turned(value, sec, shift):
        route = []
        for s in range(sections):
            for c in range(spots):
                if 0 <= c + shift < spots:
                    route.append((s * spots + c, ((s + sec) % sections) * spots + c + shift))
        return lax.ppermute(value, ("section", "ctx"), route)

    def swapped(value, level):
        return lax.ppermute(value, "ctx", [(i, i ^ (1 << level)) for i in range(spots)])

    def moved(value, shift):
        return lax.ppermute(
            value, "ctx", [(i, i + shift) for i in range(spots) if 0 <= i + shift < spots]
        )

    payload, sums = whole_call(
        prelude_kernel, (array(RIM, channels + length), array(RIM, length)), None, inputs,
        name="prelude", scalar=False,
    )
    rim = turned(payload, 0, 1)
    total = sums
    rim_total = rim[:, channels:]
    for sec in range(1, sections):
        total = total + turned(sums, sec, 0)
        rim_total = rim_total + turned(sums, sec, 1)
    scale = lax.rsqrt(total / width + norm_eps)
    rim_scale = lax.rsqrt(rim_total / width + norm_eps)

    groups = 2 if levels > 0 else 1
    per = heads // groups
    span = per * HEAD_DIM

    def block(shape, at, wide):
        lead = (0,) * (len(shape) - 1)
        return pl.BlockSpec(
            shape[:-1] + (span,), lambda i, f, lead=lead: lead + (((at * per) ^ f[0]) // per,)
        )

    def fixed(shape):
        return pl.BlockSpec(shape, lambda i, f, n=len(shape): (0,) * n)

    def grid_call(kernel, in_specs, out_specs, outs, args, name, aliases=None):
        return pl.pallas_call(
            kernel,
            grid_spec=pltpu.PrefetchScalarGridSpec(
                num_scalar_prefetch=1, grid=(1,), in_specs=in_specs, out_specs=out_specs
            ),
            out_shape=outs,
            input_output_aliases=aliases or {},
            compiler_params=pltpu.CompilerParams(vmem_limit_bytes=VMEM_LIMIT),
            name=name,
        )(flags, *args)

    rim_raw = rim[:, :channels]
    comps, saves = [None] * groups, [None] * groups
    for g in reversed(range(groups)):
        comps[g], saves[g] = grid_call(
            functools.partial(local_kernel, per, g * per),
            [
                block(inputs.shape, g, span), block(out_grads.shape, g, span), block(conv_weight.shape, g, span),
                block(log_decay.shape, g, span), fixed(beta.shape), block(rim_raw.shape, g, span),
                fixed(scale.shape), fixed(rim_scale.shape),
            ],
            [fixed((per, 384, HEAD_DIM)), fixed((per, N_SAVED, HEAD_DIM, HEAD_DIM))],
            [array(per, 384, HEAD_DIM), array(per, N_SAVED, HEAD_DIM, HEAD_DIM)],
            (inputs, out_grads, conv_weight, log_decay, beta, rim_raw, scale, rim_scale),
            name=f"local{g}",
        )

    history = []
    keep, send = comps[0], comps[-1]
    for level in range(levels):
        recv = swapped(send, level)
        history.append((keep, recv))
        n = keep.shape[0]
        if level + 1 < levels:
            keep, send = whole_call(
                functools.partial(compose_kernel, n, level + 1),
                (array(n // 2, 384, HEAD_DIM), array(n // 2, 384, HEAD_DIM)),
                flags, keep, recv, name=f"compose{level}",
            )
        else:
            t, u, g = whole_call(
                functools.partial(last_compose_kernel, n, level + 1),
                (array(n, HEAD_DIM, HEAD_DIM),) * 3,
                flags, keep, recv, name=f"compose{level}",
            )
    if levels == 0:
        t, u, g = keep[:, :128], keep[:, 128:256], keep[:, 256:]
    step = 1 << levels
    start, end = jnp.zeros_like(u), jnp.zeros_like(g)
    for hop in range(slabs - 1):
        if hop == 0:
            start, end = u, g
        else:
            start, end = whole_call(
                lambda flags, *refs: hop_kernel(*refs), (array(*u.shape),) * 2, flags, t, u, g, start, end,
                name=f"hop{hop}",
            )
        start, end = moved(start, step), moved(end, -step)
    states = (start, end)
    for level in reversed(range(levels)):
        keep, recv = history[level]
        n = keep.shape[0]
        mine, send = whole_call(
            functools.partial(down_kernel, level + 1, len(states)),
            (array(n, 256, HEAD_DIM),) * 2,
            flags, keep, recv, *states, name=f"down{level}",
        )
        states = (mine, swapped(send, level))
    if levels == 0:
        states = (jnp.concatenate([start, end], axis=1),)

    stream_out = None
    grads, rim_grads, inner, rim_sums = [], [], 0.0, 0.0
    for g in range(groups):
        args = [inputs, out_grads, conv_weight, beta, rim_raw, saves[g], states[g]]
        specs = [
            block(inputs.shape, g, span), block(out_grads.shape, g, span), block(conv_weight.shape, g, span),
            fixed(beta.shape), block(rim_raw.shape, g, span), fixed(saves[g].shape), fixed(states[g].shape),
        ]
        aliases = None
        if g > 0:
            args.append(stream_out)
            specs.append(pl.BlockSpec(memory_space=pl.ANY))
            aliases = {len(args): 0}
        stream_out, grad, rim_grad, part, rim_part = grid_call(
            functools.partial(back_kernel, per, g * per, g > 0),
            specs,
            [
                block(inputs.shape, g, span), fixed((length, span)), fixed((RIM, span)),
                fixed((RIM, length)), fixed((RIM, HEAD_DIM)),
            ],
            [
                array(*inputs.shape, dtype=bf16), array(length, span), array(RIM, span),
                array(RIM, length), array(RIM, HEAD_DIM),
            ],
            args, name=f"back{g}", aliases=aliases,
        )
        grads.append(grad)
        rim_grads.append(rim_grad)
        inner = inner + part
        rim_sums = rim_sums + rim_part

    next_rims = [turned(a, 0, -1) for a in reversed(rim_grads)]
    inner_total = inner
    next_sums = turned(rim_sums, 0, -1)
    for sec in range(1, sections):
        inner_total = inner_total + turned(inner, sec, 0)
        next_sums = next_sums + turned(rim_sums, sec, -1)
    input_grad = finish(
        flags, groups, width, inputs, out_grads, scale, inner_total, next_sums, grads, next_rims
    )
    return (stream_out, input_grad)


def finish(flags, groups, width, inputs, out_grads, scale, inner_total, next_sums, grads, next_rims):
    return whole_call(
        functools.partial(finish_kernel, groups, width),
        array(*inputs.shape, dtype=bf16),
        flags, inputs, out_grads, scale, inner_total, next_sums, *grads, *next_rims, name="finish",
    )


def solution(mesh):
    in_specs = (
        P("ctx", "section"),
        P("ctx", "section"),
        P(None, None, "section"),
        P("ctx", "section"),
        P("ctx", "section"),
    )
    out_specs = (P("ctx", "section"), P("ctx", "section"))
    return jax.shard_map(shards, mesh=mesh, in_specs=in_specs, out_specs=out_specs, check_vma=False)
```

```python
import functools

import jax
import jax.numpy as jnp
from jax import lax
from jax.experimental import pallas as pl
from jax.experimental.pallas import tpu as pltpu
from jax.sharding import PartitionSpec as P

HEAD_DIM = 128
RIM = 8
epsilon = 1e-06
norm_eps = 1e-05
f32 = jnp.float32
bf16 = jnp.bfloat16
VMEM_LIMIT = 24 * 1024 * 1024

DIMS = {
    "nn": (((1,), (0,)), ((), ())),
    "nt": (((1,), (1,)), ((), ())),
    "tn": (((0,), (0,)), ((), ())),
}


def split(a):
    high = a.astype(bf16)
    return high, (a - high.astype(f32)).astype(bf16)


def exact(a):
    return a, None


def rows_of(*parts):
    highs = jnp.concatenate([p[0] for p in parts], axis=0)
    lows = [jnp.zeros_like(p[0]) if p[1] is None else p[1] for p in parts]
    return highs, jnp.concatenate(lows, axis=0)


def cols_of(*parts):
    return tuple(jnp.concatenate([p[i] for p in parts], axis=1) for i in range(2))


def mm(a, b, form):
    pairs = [(a[0], b[0])]
    if a[1] is not None:
        pairs.append((a[1], b[0]))
    if b[1] is not None:
        pairs.append((a[0], b[1]))
    left = jnp.concatenate([p[0] for p in pairs], axis=0 if form == "tn" else 1)
    right = jnp.concatenate([p[1] for p in pairs], axis=1 if form == "nt" else 0)
    return lax.dot_general(left, right, DIMS[form], preferred_element_type=f32)


def row_sums(a):
    high = a.astype(bf16)
    rest = a - high.astype(f32)
    mid = rest.astype(bf16)
    low = (rest - mid.astype(f32)).astype(bf16)
    terms = jnp.concatenate([high, mid, low], axis=1)
    ones = jnp.ones((RIM, terms.shape[1]), bf16)
    return lax.dot_general(ones, terms, DIMS["nt"], preferred_element_type=f32)


def down_rows(row):
    return jnp.transpose(jnp.broadcast_to(row[0:1], (HEAD_DIM, row.shape[1])))


def iotas(n=HEAD_DIM):
    return (
        lax.broadcasted_iota(jnp.int32, (n, n), 0),
        lax.broadcasted_iota(jnp.int32, (n, n), 1),
    )


def lane_slice(place):
    return pl.ds(pl.multiple_of(place * HEAD_DIM, HEAD_DIM), HEAD_DIM)


def prelude_kernel(x_hbm, go_hbm, kern_hbm, decay_hbm, payload_ref, sums_ref, x_ref, go_ref, kern_ref, decay_ref, sems):
    pairs = ((x_hbm, x_ref), (go_hbm, go_ref), (kern_hbm, kern_ref), (decay_hbm, decay_ref))
    copies = [pltpu.make_async_copy(src, dst, sems.at[n]) for n, (src, dst) in enumerate(pairs)]
    for copy in copies:
        copy.start()
    copies[0].wait()
    x = x_ref[...].astype(f32)
    channels = x.shape[1]
    sums = row_sums(x * x)
    sums_ref[...] = sums
    payload_ref[:, :channels] = x[x.shape[0] - RIM :]
    payload_ref[:, channels:] = sums
    for copy in copies[1:]:
        copy.wait()


def inverse_all(systems):
    row, col = iotas()
    own = row >> 3 == col >> 3
    row8 = lax.broadcasted_iota(jnp.int32, (RIM, HEAD_DIM), 0)
    col8 = lax.broadcasted_iota(jnp.int32, (RIM, HEAD_DIM), 1)
    found = []
    for n in systems:
        blocks = jnp.sum(jnp.where(own, n, 0.0).reshape(-1, RIM, HEAD_DIM), axis=0)
        rows = jnp.where(row8 == (col8 & 7), 1.0, 0.0)
        for s in range(RIM - 1):
            column = jnp.take_along_axis(blocks, ((col8 >> 3) << 3) + s, axis=1, mode="promise_in_bounds")
            rows = rows - column * rows[s : s + 1]
        found.append(jnp.where(own, jnp.concatenate([rows] * (HEAD_DIM // RIM), axis=0), 0.0))
    level = 3
    while (1 << level) < HEAD_DIM:
        mask = (row >> (level + 2) == col >> (level + 2)) & (row >> level != col >> level)
        parts = [split(d) for d in found]
        cross = [split(jnp.where(mask, n, 0.0)) for n in systems]
        maps = [split(mm(p, c, "nn")) for p, c in zip(parts, cross)]
        twice = [mm(m, cols_of(m, p), "nn") for m, p in zip(maps, parts)]
        less = [d - t[:, HEAD_DIM:] for d, t in zip(found, twice)]
        found = [y + mm(split(t[:, :HEAD_DIM]), split(y), "nn") for y, t in zip(less, twice)]
        level += 2
    return found


def mixes_of(normed, rim, kern):
    row8 = lax.broadcasted_iota(jnp.int32, (RIM, HEAD_DIM), 0)
    taps = kern.shape[1]
    shifted = [normed]
    for s in range(1, taps):
        moved = pltpu.roll(normed, s, 0)
        first = jnp.where(row8 < s, pltpu.roll(rim, s, 0), moved[:RIM])
        shifted.append(jnp.concatenate([first, moved[RIM:]], axis=0))
    return [
        sum(kern[j, i : i + 1] * shifted[taps - 1 - i] for i in range(taps)) for j in range(3)
    ]


def gates_kernel(decay_ref, beta_ref, e1_ref, e2_ref, edge_ref, rate_ref):
    length = decay_ref.shape[0]
    row, col = iotas()
    tril = jnp.where(row >= col, 1.0, 0.0).astype(bf16)
    tril = jnp.concatenate([tril] * 3, axis=1)
    for head in range(decay_ref.shape[1] // HEAD_DIM):
        here = slice(head * HEAD_DIM, (head + 1) * HEAD_DIM)
        decay = decay_ref[:, here]
        high = decay.astype(bf16)
        rest = decay - high.astype(f32)
        mid = rest.astype(bf16)
        low = (rest - mid.astype(f32)).astype(bf16)
        cumulative = lax.dot_general(
            tril, jnp.concatenate([high, mid, low], axis=0), DIMS["nn"], preferred_element_type=f32
        )
        middle = cumulative[length // 2 : length // 2 + 1]
        final = cumulative[length - 1 : length]
        e1_ref[:, here] = jnp.exp(cumulative - middle)
        e2_ref[:, here] = jnp.exp(middle - cumulative)
        edge_ref[0:8, here] = jnp.broadcast_to(jnp.exp(middle), (8, HEAD_DIM))
        edge_ref[8:16, here] = jnp.broadcast_to(jnp.exp(final - middle), (8, HEAD_DIM))
        edge_ref[16:24, here] = jnp.broadcast_to(jnp.exp(final), (8, HEAD_DIM))
        rate_ref[:, here] = down_rows(beta_ref[head : head + 1])


def scaled(x_ref, rim_ref, kern_ref, scale, rim_scale, at):
    x = x_ref[:, at].astype(f32)
    return mixes_of(x * scale, rim_ref[:, at] * rim_scale, kern_ref[:, :, at])


def scales(flags, scale_ref, rim_scale_ref):
    rim_scale = down_rows(rim_scale_ref[...])
    rim_scale = jnp.where(flags[4] != 0, rim_scale[rim_scale.shape[0] - RIM :], 0.0)
    return down_rows(scale_ref[...]), rim_scale


def keep_split(ref, j, n, parts):
    ref[j, n] = parts[0]
    ref[j, n + 1] = parts[1]


def kept(ref, j, n):
    return ref[j, n], ref[j, n + 1]


def local_kernel(
    heads, flags, x_ref, go_ref, kern_ref, e1_ref, e2_ref, edge_ref, rate_ref, rim_ref, scale_ref, rim_scale_ref,
    comp_ref, wide_ref, narrow_ref,
):
    mask = flags[0]
    length = x_ref.shape[0]
    row, col = iotas()
    strict, full = row > col, row >= col
    scale, rim_scale = scales(flags, scale_ref, rim_scale_ref)
    data = []
    for j in range(heads):
        at = lane_slice((j ^ mask) & (heads - 1))
        mixes = scaled(x_ref, rim_ref, kern_ref, scale, rim_scale, at)
        act = [m / (1.0 + jnp.exp(-m)) for m in mixes]
        q, k = [a * lax.rsqrt(jnp.sum(a * a, axis=1, keepdims=True) + epsilon) for a in act[:2]]
        rate, e1, e2 = rate_ref[:, at], e1_ref[:, at], e2_ref[:, at]
        em, ecm, ef = [edge_ref[n : n + 1, at] for n in (0, 8, 16)]
        qf, kf, kb = q * e1, k * e1, k * e2
        skf, sqf, skb = split(kf), split(qf), split(kb)
        products = mm(rows_of(skf, sqf), skb, "nt")
        system = jnp.where(strict, rate * products[:length], 0.0)
        scores = split(jnp.where(full, products[length:], 0.0))
        go = exact(go_ref[:, at])
        fresh_grad = split(mm(scores, go, "tn"))
        wide_ref[j, 0], wide_ref[j, 1] = q, k
        for n, parts in enumerate((skf, sqf, skb, scores, fresh_grad)):
            keep_split(narrow_ref, j, 2 * n, parts)
        data.append(
            dict(system=system, go=go, rhs=cols_of(split(rate * kf * em), split(rate * act[2])), ke=split(kb * ecm),
                 qg=qf * em, fresh_grad=fresh_grad, ef=ef)
        )
    inverses = inverse_all([d["system"] for d in data])
    for j, (d, inverse) in enumerate(zip(data, inverses)):
        inverse = split(inverse)
        keep_split(narrow_ref, j, 10, inverse)
        solved = mm(inverse, d["rhs"], "nn")
        wide_ref[j, 2] = solved[:, HEAD_DIM:]
        d["solved"] = split(solved)
    for j, d in enumerate(data):
        solved = d["solved"]
        keep_split(narrow_ref, j, 12, (solved[0][:, :HEAD_DIM], solved[1][:, :HEAD_DIM]))
        keep_split(narrow_ref, j, 14, (solved[0][:, HEAD_DIM:], solved[1][:, HEAD_DIM:]))
        maps = mm(d["ke"], solved, "tn")
        comp_ref[j, 0:128] = jnp.where(row == col, d["ef"], 0.0) - maps[:, :HEAD_DIM]
        comp_ref[j, 128:256] = maps[:, HEAD_DIM:]
        w = (solved[0][:, :HEAD_DIM], solved[1][:, :HEAD_DIM])
        comp_ref[j, 256:384] = mm(split(d["qg"]), d["go"], "tn") - mm(w, d["fresh_grad"], "tn")


WIDE, NARROW = 3, 16


def ready_kernel(
    heads, flags, x_ref, kern_ref, e2_ref, edge_ref, rim_ref, scale_ref, rim_scale_ref, wide_ref, narrow_ref,
    more_ref, pairs_ref,
):
    mask = flags[0]
    scale, rim_scale = scales(flags, scale_ref, rim_scale_ref)
    for j in range(heads):
        at = lane_slice((j ^ mask) & (heads - 1))
        mixes = scaled(x_ref, rim_ref, kern_ref, scale, rim_scale, at)
        sig = [1.0 / (1.0 + jnp.exp(-m)) for m in mixes]
        slope = [s * (1.0 + m * (1.0 - s)) for m, s in zip(mixes, sig)]
        act = [m * s for m, s in zip(mixes[:2], sig)]
        inv = [lax.rsqrt(jnp.sum(a * a, axis=1, keepdims=True) + epsilon) for a in act]
        em, ecm = edge_ref[0:1, at], edge_ref[8:9, at]
        scores, fresh_grad, inverse = [kept(narrow_ref, j, n) for n in (6, 8, 10)]
        solved = cols_of(kept(narrow_ref, j, 12), kept(narrow_ref, j, 14))
        seen = mm(scores, solved, "nn")
        ke = split(wide_ref[j, 1] * e2_ref[:, at] * ecm)
        back = mm(inverse, cols_of(fresh_grad, ke), "tn")
        more_ref[j, 0] = slope[0] * inv[0]
        more_ref[j, 1] = slope[1] * inv[1]
        more_ref[j, 2] = slope[2]
        more_ref[j, 3] = seen[:, HEAD_DIM:]
        more_ref[j, 4] = back[:, :HEAD_DIM]
        qf = narrow_ref[j, 2].astype(f32) + narrow_ref[j, 3].astype(f32)
        keep_split(pairs_ref, j, 0, split(qf * em - seen[:, :HEAD_DIM]))
        keep_split(pairs_ref, j, 2, split(back[:, HEAD_DIM:]))


MORE, PAIRS = 5, 4


def join_kernel(flags, keep_ref, recv_ref, *outs):
    later = flags[1] != 0
    for j, out in enumerate(outs):
        keep, recv = keep_ref[j], recv_ref[j]
        lo = jnp.where(later, recv, keep)
        hi = jnp.where(later, keep, recv)
        lo_map, hi_map = split(lo[0:128]), split(hi[0:128])
        forward = mm(hi_map, cols_of(lo_map, split(lo[128:256])), "nn")
        back = mm(lo_map, split(hi[256:384]), "tn")
        out[0:128] = forward[:, :HEAD_DIM]
        out[128:256] = forward[:, HEAD_DIM:] + hi[128:256]
        out[256:384] = back + lo[256:384]


def collect(place, parts, held):
    for n, part in enumerate(parts):
        held[place ^ n] = part[...]


def gather_kernel(count, waits, with_map, flags, *refs):
    parts, outs, held = refs[:count], refs[count + waits : -1], refs[-1]
    collect(flags[2], parts, held)
    maps = [split(held[p, 0:128]) for p in range(count)]
    state, grad = held[0, 128:256], held[count - 1, 256:384]
    whole = held[0, 0:128]
    for p in range(1, count):
        state = mm(maps[p], split(state), "nn") + held[p, 128:256]
        grad = mm(maps[count - 1 - p], split(grad), "tn") + held[count - 1 - p, 256:384]
        if with_map:
            whole = mm(maps[p], split(whole), "nn")
    if with_map:
        outs[0][...], outs[1][...], outs[2][...] = whole, state, grad
    else:
        outs[0][...] = jnp.where(flags[3] != 0, grad, state)


def hop_kernel(flags, t_ref, u_ref, g_ref, s_ref, e_ref, s_out, e_out):
    t = split(t_ref[...])
    s_out[...] = mm(t, split(s_ref[...]), "nn") + u_ref[...]
    e_out[...] = mm(t, split(e_ref[...]), "tn") + g_ref[...]


def spread_kernel(count, single, flags, *refs):
    parts, ins, outs, held, found = refs[:count], refs[count : -2 - count], refs[-2 - count : -2], refs[-2], refs[-1]
    collect(flags[2], parts, held)
    if single:
        upper = flags[3] != 0
        state = jnp.where(upper, ins[0][...], 0.0)
        grad = jnp.where(upper, 0.0, ins[0][...])
    else:
        state, grad = ins[0][...], ins[1][...]
    for p in range(count):
        back = count - 1 - p
        found[p, 0:128] = state
        found[back, 128:256] = grad
        if p + 1 < count:
            state = mm(split(held[p, 0:128]), split(state), "nn") + held[p, 128:256]
            grad = mm(split(held[back, 0:128]), split(grad), "tn") + held[back, 256:384]
    for n, out in enumerate(outs):
        out[...] = found[flags[2] ^ n]


def part_kernel(flags, keep_ref, recv_ref, *refs):
    ins, (mine_ref, send_ref) = refs[:-2], refs[-2:]
    later = flags[1] != 0
    for j, ref in enumerate(ins):
        start, end = ref[0:128], ref[128:256]
        keep, recv = keep_ref[j], recv_ref[j]
        lo = jnp.where(later, recv, keep)
        hi = jnp.where(later, keep, recv)
        start_hi = mm(split(lo[0:128]), split(start), "nn") + lo[128:256]
        end_lo = mm(split(hi[0:128]), split(end), "tn") + hi[256:384]
        mine_ref[j, 0:128] = jnp.where(later, start_hi, start)
        mine_ref[j, 128:256] = jnp.where(later, end, end_lo)
        send_ref[j, 0:128] = jnp.where(later, start, start_hi)
        send_ref[j, 128:256] = jnp.where(later, end_lo, end)


def back_kernel(
    heads, chained, flags, x_ref, go_ref, kern_ref, e1_ref, e2_ref, edge_ref, rate_ref, rim_ref, wide_ref, narrow_ref,
    more_ref, pairs_ref, state_ref, *rest,
):
    if chained:
        sums_in, rim_sums_in, rim_grad_in, rest = rest[0], rest[1], rest[2], rest[4:]
    out_hbm, rim_grad_ref, grad_ref, sums_ref, rim_sums_ref, out_ref, sems = rest
    mask = flags[0]
    length = x_ref.shape[0]
    row, col = iotas()
    row8 = lax.broadcasted_iota(jnp.int32, (RIM, HEAD_DIM), 0)
    strict, full = row > col, row >= col
    taps = kern_ref.shape[1]
    first_head = (heads if chained else 0) ^ (mask & heads)
    dot_all = rim_dot = 0.0
    data, copies = [], []
    for j in range(heads):
        near = (j ^ mask) & (heads - 1)
        at = lane_slice(near)
        start, end = split(state_ref[j, 0:128]), split(state_ref[j, 128:256])
        first = mm(rows_of(kept(pairs_ref, j, 0), kept(narrow_ref, j, 12)), start, "nn")
        z = more_ref[j, 4] + mm(kept(pairs_ref, j, 2), end, "nn")
        x = x_ref[:, at].astype(f32)
        out_ref[j] = (x + (more_ref[j, 3] + first[:length])).astype(bf16)
        copies.append(
            pltpu.make_async_copy(out_ref.at[j], out_hbm.at[:, lane_slice(first_head + near)], sems.at[j])
        )
        copies[-1].start()
        data.append(dict(at=at, x=x, start=start, end=end, z=z, fresh=split(wide_ref[j, 2] - first[length:])))
    for j, d in enumerate(data):
        at = d["at"]
        q, k = wide_ref[j, 0], wide_ref[j, 1]
        gq, gk, gv = [more_ref[j, n] for n in range(3)]
        skf, sqf, skb = [kept(narrow_ref, j, n) for n in (0, 2, 4)]
        e1, e2, rate = e1_ref[:, at], e2_ref[:, at], rate_ref[:, at]
        em, ecm = edge_ref[0:1, at], edge_ref[8:9, at]
        go = exact(go_ref[:, at])
        second = mm(rows_of(go, split(d["z"])), rows_of(d["fresh"], d["start"]), "nt")
        score_grad = split(jnp.where(full, second[:length, :HEAD_DIM], 0.0))
        product_grad = split(jnp.where(strict, -rate * second[length:, :HEAD_DIM], 0.0))
        qg_grad = second[:length, HEAD_DIM:]
        kg_grad = -rate * second[length:, HEAD_DIM:]
        ke_grad = mm(d["fresh"], d["end"], "nt")
        pair = rows_of(score_grad, product_grad)
        third = mm(pair, skb, "nn")
        kb_grad = mm(pair, rows_of(sqf, skf), "tn")
        q_grad = e1 * (third[:length] + em * qg_grad)
        k_grad = e1 * (third[length:] + em * kg_grad) + e2 * (kb_grad + ecm * ke_grad)
        mix_grads = [
            gq * (q_grad - q * jnp.sum(q * q_grad, axis=1, keepdims=True)),
            gk * (k_grad - k * jnp.sum(k * k_grad, axis=1, keepdims=True)),
            gv * (rate * d["z"]),
        ]
        kern = kern_ref[:, :, at]
        normed_grad = rim_grad = 0.0
        for i in range(taps):
            each = sum(kern[n, i : i + 1] * mix_grads[n] for n in range(3))
            s = taps - 1 - i
            if s == 0:
                normed_grad = normed_grad + each
            else:
                moved = pltpu.roll(each, length - s, 0)
                normed_grad = normed_grad + jnp.where(row < length - s, moved, 0.0)
                rim_grad = rim_grad + jnp.where(row8 >= RIM - s, moved[length - RIM :], 0.0)
        grad_ref[:, at] = normed_grad
        if chained:
            rim_grad_ref[:, lane_slice(first_head + ((j ^ mask) & (heads - 1)))] = rim_grad
        else:
            rim_grad_ref[:, at] = rim_grad
        dot_all = dot_all + normed_grad * d["x"]
        rim_dot = rim_dot + rim_grad * rim_ref[:, at]
    sums = row_sums(dot_all)
    rim_sums = jnp.broadcast_to(jnp.sum(rim_dot, axis=1, keepdims=True), rim_dot.shape)
    if chained:
        sums, rim_sums = sums + sums_in[...], rim_sums + rim_sums_in[...]
        for n in range(heads):
            here = slice(n * HEAD_DIM, (n + 1) * HEAD_DIM)
            rim_grad_ref[:, lane_slice((first_head ^ heads) + n)] = rim_grad_in[:, here]
        rim_grad_ref[:, 2 * heads * HEAD_DIM :] = rim_sums
    sums_ref[...] = sums
    rim_sums_ref[...] = rim_sums
    for copy in copies:
        copy.wait()


def finish_kernel(groups, width, flags, x_ref, go_ref, scale_ref, inner_ref, next_sums_ref, next_ref, *refs):
    grads, (out_hbm, out_ref, sems) = refs[:groups], refs[groups:]
    length = x_ref.shape[0]
    scale = down_rows(scale_ref[...])
    inner = down_rows(inner_ref[...])
    last = flags[5] == 0
    next_sums = jnp.where(last, 0.0, next_sums_ref[...])
    inner = jnp.concatenate([inner[: length - RIM], inner[length - RIM :] + next_sums], axis=0)
    cubed = scale * scale * scale * inner * (1.0 / width)
    per = grads[0].shape[1] // HEAD_DIM
    copies = []
    for g, grad_ref in enumerate(grads):
        place = ((g * per) ^ flags[0]) // per
        for n in range(per):
            at = lane_slice(place * per + n)
            grad = grad_ref[:, n * HEAD_DIM : (n + 1) * HEAD_DIM]
            next_grad = jnp.where(last, 0.0, next_ref[:, at])
            grad = jnp.concatenate([grad[: length - RIM], grad[length - RIM :] + next_grad], axis=0)
            total = go_ref[:, at].astype(f32) + grad * scale - x_ref[:, at].astype(f32) * cubed
            out_ref[g * per + n] = total.astype(bf16)
            copies.append(
                pltpu.make_async_copy(out_ref.at[g * per + n], out_hbm.at[:, at], sems.at[g * per + n])
            )
            copies[-1].start()
    for copy in copies:
        copy.wait()


def whole_call(kernel, outs, *args, name=None, scratch=(), scalar=True, cost=None, far=False, unread=0):
    spec = pl.BlockSpec(memory_space=pltpu.VMEM)
    hbm = pl.BlockSpec(memory_space=pltpu.HBM)
    first = [pl.BlockSpec(memory_space=pltpu.SMEM)] if scalar else []
    return pl.pallas_call(
        kernel,
        out_shape=outs,
        in_specs=first + [hbm if far == "in" else spec] * (len(args) - len(first) - unread)
        + [pl.BlockSpec(memory_space=pl.ANY)] * unread,
        out_specs=jax.tree.map(lambda _: hbm if far == "out" else spec, outs),
        scratch_shapes=scratch,
        compiler_params=pltpu.CompilerParams(vmem_limit_bytes=VMEM_LIMIT),
        cost_estimate=cost,
        name=name,
    )(*args)


BESIDE = pl.CostEstimate(flops=10**9, bytes_accessed=10**7, transcendentals=0)


def array(*shape, dtype=f32):
    return jax.ShapeDtypeStruct(shape, dtype)


def shards(inputs, out_grads, conv_weight, log_decay, beta):
    length, channels = inputs.shape
    heads = channels // HEAD_DIM
    sections, spots = lax.axis_size("section"), lax.axis_size("ctx")
    width = channels * sections
    groups, per = 2, heads // 2
    count = per
    slabs = spots // (2 * count)
    me = lax.axis_index("ctx")
    place = (me >> 1) % count
    later = me & 1
    mask = later * per + place
    flags = [mask, later, place, (me // (2 * count)) % 2, me != 0, me != spots - 1]
    flags = jnp.stack([jnp.asarray(f, jnp.int32) for f in flags])

    def turned(value, sec, shift):
        route = [
            (s * spots + c, ((s + sec) % sections) * spots + (c + shift) % spots)
            for s in range(sections)
            for c in range(spots)
        ]
        return lax.ppermute(value, ("section", "ctx"), route)

    def swapped(value, distance):
        return lax.ppermute(value, "ctx", [(i, i ^ distance) for i in range(spots)])

    def moved(value, shift):
        return lax.ppermute(
            value, "ctx", [(i, i + shift) for i in range(spots) if 0 <= i + shift < spots]
        )

    payload, sums, x, go, kern, decay = whole_call(
        prelude_kernel,
        (
            array(RIM, channels + length), array(RIM, length), array(*inputs.shape, dtype=bf16),
            array(*inputs.shape, dtype=bf16), array(*conv_weight.shape), array(*inputs.shape),
        ),
        *[pltpu.with_memory_space_constraint(a, pltpu.HBM) for a in (inputs, out_grads, conv_weight, log_decay)],
        name="prelude", scalar=False, far="in", scratch=[pltpu.SemaphoreType.DMA((4,))],
    )
    total = sums
    rim_total = 0.0
    for sec in range(1, sections):
        total = total + turned(sums, sec, 0)
        rim_total = rim_total + turned(sums, sec, 1)
    rim = turned(payload, 0, 1)
    e1, e2, edge, rate = whole_call(
        gates_kernel,
        (array(length, channels), array(length, channels), array(24, channels), array(length, channels)),
        decay, beta.T, name="gates", scalar=False, cost=BESIDE,
    )
    scale = lax.rsqrt(total / width + norm_eps)
    rim_scale = lax.rsqrt((rim_total + rim[:, channels:]) / width + norm_eps)
    rim_raw = rim[:, :channels]

    span = per * HEAD_DIM

    def block(a, g):
        lead = (0,) * (len(a.shape) - 1)
        return pl.BlockSpec(a.shape[:-1] + (span,), lambda i, f: lead + (((g * per) ^ f[0]) // per,))

    def fixed(a):
        return pl.BlockSpec(a.shape, lambda i, f: (0,) * len(a.shape))

    def grid_call(kernel, in_specs, out_specs, outs, args, name, aliases=None, scratch=(), cost=None):
        return pl.pallas_call(
            kernel,
            grid_spec=pltpu.PrefetchScalarGridSpec(
                num_scalar_prefetch=1, grid=(1,), in_specs=in_specs, out_specs=out_specs, scratch_shapes=scratch
            ),
            out_shape=outs,
            input_output_aliases=aliases or {},
            compiler_params=pltpu.CompilerParams(vmem_limit_bytes=VMEM_LIMIT),
            cost_estimate=cost,
            name=name,
        )(flags, *args)

    square = (HEAD_DIM, HEAD_DIM)
    sliced = (x, go, kern, e1, e2, edge, rate, rim_raw)
    comps, saves = [None] * groups, [None] * groups
    for g in reversed(range(groups)):
        outs = [array(per, 384, HEAD_DIM), array(per, WIDE, *square), array(per, NARROW, *square, dtype=bf16)]
        comps[g], *saves[g] = grid_call(
            functools.partial(local_kernel, per),
            [block(a, g) for a in sliced] + [fixed(scale), fixed(rim_scale)],
            [fixed(a) for a in outs], outs, sliced + (scale, rim_scale), name=f"local{g}",
        )

    keep, recv = comps[0], swapped(comps[1], 1)
    joined = whole_call(join_kernel, (array(384, HEAD_DIM),) * per, flags, keep, recv, name="join")
    parts = [joined[0]] + [swapped(joined[n], 2 * n) for n in range(1, count)]
    for g in range(groups):
        outs = [array(per, MORE, HEAD_DIM, HEAD_DIM), array(per, PAIRS, HEAD_DIM, HEAD_DIM, dtype=bf16)]
        some = (x, kern, e2, edge, rim_raw)
        rest = (scale, rim_scale, *saves[g])
        saves[g] += grid_call(
            functools.partial(ready_kernel, per),
            [block(a, g) for a in some] + [fixed(a) for a in rest],
            [fixed(a) for a in outs], outs, some + rest, name=f"ready{g}", cost=BESIDE,
        )
    held = pltpu.VMEM((count, 384, HEAD_DIM), f32)
    square = array(*square)
    single = slabs == 2
    gathered = whole_call(
        functools.partial(gather_kernel, count, groups, not single), (square,) if single else (square,) * 3,
        flags, *parts, *[saves[g][2] for g in range(groups)], name="gather", scratch=[held], unread=groups,
    )
    step = 2 * count
    if single:
        states = (swapped(gathered[0], step),)
    else:
        states = (jnp.zeros(square.shape, f32),) * 2
        for hop in range(slabs - 1):
            if hop == 0:
                states = gathered[1:]
            else:
                states = whole_call(hop_kernel, (square,) * 2, flags, *gathered, *states, name=f"hop{hop}")
            states = (moved(states[0], step), moved(states[1], -step))
    spread = whole_call(
        functools.partial(spread_kernel, count, single), (array(256, HEAD_DIM),) * count,
        flags, *parts, *states, name="spread", scratch=[held, pltpu.VMEM((count, 256, HEAD_DIM), f32)],
    )
    spread = [spread[0]] + [swapped(spread[n], 2 * n) for n in range(1, count)]
    mine, send = whole_call(
        part_kernel, (array(per, 256, HEAD_DIM),) * 2, flags, keep, recv, *spread, name="part"
    )
    states = (mine, swapped(send, 1))

    chain = None
    grads = []
    far = pl.BlockSpec(memory_space=pltpu.HBM)
    for g in range(groups):
        rest = (*saves[g], states[g])
        aliases = None
        if chain is not None:
            rest = rest + (chain[3], chain[4], chain[1])
        args = sliced + rest
        specs = [block(a, g) for a in sliced] + [fixed(a) for a in rest]
        if chain is not None:
            args = args + (chain[0],)
            specs = specs + [far]
            aliases = {len(args): 0}
        rim_width = span if chain is None else channels + HEAD_DIM
        outs = [
            array(*inputs.shape, dtype=bf16), array(RIM, rim_width), array(length, span),
            array(RIM, length), array(RIM, HEAD_DIM),
        ]
        chain = grid_call(
            functools.partial(back_kernel, per, chain is not None),
            specs, [far] + [fixed(a) for a in outs[1:]], outs, args, name=f"back{g}", aliases=aliases,
            scratch=[pltpu.VMEM((per, length, HEAD_DIM), bf16), pltpu.SemaphoreType.DMA((per,))],
        )
        grads.append(chain[2])
    stream_out, rim_grad, _, inner, rim_sums = chain

    inner_total, next_sums = inner, 0.0
    for sec in range(1, sections):
        inner_total = inner_total + turned(inner, sec, 0)
        next_sums = next_sums + turned(rim_sums, sec, -1)
    next_rim = turned(rim_grad, 0, -1)
    input_grad = whole_call(
        functools.partial(finish_kernel, groups, width), array(*inputs.shape, dtype=bf16),
        flags, x, go, scale, inner_total, next_sums + next_rim[:, channels:], next_rim, *grads, name="finish",
        far="out", scratch=[pltpu.VMEM((heads, length, HEAD_DIM), bf16), pltpu.SemaphoreType.DMA((heads,))],
    )
    return (stream_out, input_grad)


def solution(mesh):
    in_specs = (
        P("ctx", "section"),
        P("ctx", "section"),
        P(None, None, "section"),
        P("ctx", "section"),
        P("ctx", "section"),
    )
    out_specs = (P("ctx", "section"), P("ctx", "section"))
    return jax.shard_map(shards, mesh=mesh, in_specs=in_specs, out_specs=out_specs, check_vma=False)
```

```python
import functools

import jax
import jax.numpy as jnp
from jax import lax
from jax.experimental import pallas as pl
from jax.experimental.pallas import tpu as pltpu
from jax.sharding import PartitionSpec as P

HEAD_DIM = 128
RIM = 8
epsilon = 1e-06
norm_eps = 1e-05
f32 = jnp.float32
bf16 = jnp.bfloat16
VMEM_LIMIT = 24 * 1024 * 1024

DIMS = {
    "nn": (((1,), (0,)), ((), ())),
    "nt": (((1,), (1,)), ((), ())),
    "tn": (((0,), (0,)), ((), ())),
}


def split(a):
    high = a.astype(bf16)
    return high, (a - high.astype(f32)).astype(bf16)


def exact(a):
    return a, None


def rows_of(*parts):
    highs = jnp.concatenate([p[0] for p in parts], axis=0)
    lows = [jnp.zeros_like(p[0]) if p[1] is None else p[1] for p in parts]
    return highs, jnp.concatenate(lows, axis=0)


def cols_of(*parts):
    return tuple(jnp.concatenate([p[i] for p in parts], axis=1) for i in range(2))


def mm(a, b, form):
    width = b[0].shape[1]
    if form != "nt" and a[1] is not None and b[1] is not None and width == HEAD_DIM:
        right = jnp.concatenate(b, axis=1)
        left = jnp.concatenate(a, axis=0 if form == "tn" else 1)
        out = lax.dot_general(left, jnp.concatenate([right, right], axis=0), DIMS[form], preferred_element_type=f32)
        return out[:, :width] + out[:, width:]
    pairs = [(a[0], b[0])]
    if a[1] is not None:
        pairs.append((a[1], b[0]))
    if b[1] is not None:
        pairs.append((a[0], b[1]))
    left = jnp.concatenate([p[0] for p in pairs], axis=0 if form == "tn" else 1)
    right = jnp.concatenate([p[1] for p in pairs], axis=1 if form == "nt" else 0)
    return lax.dot_general(left, right, DIMS[form], preferred_element_type=f32)


def row_sums(a):
    high = a.astype(bf16)
    rest = a - high.astype(f32)
    mid = rest.astype(bf16)
    low = (rest - mid.astype(f32)).astype(bf16)
    terms = jnp.concatenate([high, mid, low], axis=1)
    ones = jnp.ones((RIM, terms.shape[1]), bf16)
    return lax.dot_general(ones, terms, DIMS["nt"], preferred_element_type=f32)


def down_rows(row):
    return jnp.transpose(jnp.broadcast_to(row[0:1], (HEAD_DIM, row.shape[1])))


def iotas(n=HEAD_DIM):
    return (
        lax.broadcasted_iota(jnp.int32, (n, n), 0),
        lax.broadcasted_iota(jnp.int32, (n, n), 1),
    )


def lane_slice(place):
    return pl.ds(pl.multiple_of(place * HEAD_DIM, HEAD_DIM), HEAD_DIM)


def prelude_kernel(
    x_hbm, go_hbm, kern_hbm, decay_hbm, beta_hbm, payload_ref, sums_ref, x_ref, go_ref, kern_ref, decay_ref, beta_ref, sems
):
    pairs = ((x_hbm, x_ref), (go_hbm, go_ref), (kern_hbm, kern_ref), (decay_hbm, decay_ref), (beta_hbm, beta_ref))
    copies = [pltpu.make_async_copy(src, dst, sems.at[n]) for n, (src, dst) in enumerate(pairs)]
    for copy in copies:
        copy.start()
    copies[0].wait()
    x = x_ref[...].astype(f32)
    channels = x.shape[1]
    sums = row_sums(x * x)
    sums_ref[...] = sums
    payload_ref[:, :channels] = x[x.shape[0] - RIM :]
    payload_ref[:, channels:] = sums
    for copy in copies[1:]:
        copy.wait()


def inverse_all(systems):
    row, col = iotas()
    own = row >> 3 == col >> 3
    row8 = lax.broadcasted_iota(jnp.int32, (RIM, HEAD_DIM), 0)
    col8 = lax.broadcasted_iota(jnp.int32, (RIM, HEAD_DIM), 1)
    found = []
    for n in systems:
        blocks = jnp.sum(jnp.where(own, n, 0.0).reshape(-1, RIM, HEAD_DIM), axis=0)
        rows = jnp.where(row8 == (col8 & 7), 1.0, 0.0)
        for s in range(RIM - 1):
            column = jnp.take_along_axis(blocks, ((col8 >> 3) << 3) + s, axis=1, mode="promise_in_bounds")
            rows = rows - column * rows[s : s + 1]
        found.append(jnp.where(own, jnp.concatenate([rows] * (HEAD_DIM // RIM), axis=0), 0.0))
    level = 3
    while (1 << level) < HEAD_DIM:
        mask = (row >> (level + 2) == col >> (level + 2)) & (row >> level != col >> level)
        parts = [split(d) for d in found]
        cross = [split(jnp.where(mask, n, 0.0)) for n in systems]
        maps = [split(mm(p, c, "nn")) for p, c in zip(parts, cross)]
        twice = [mm(m, cols_of(m, p), "nn") for m, p in zip(maps, parts)]
        less = [d - t[:, HEAD_DIM:] for d, t in zip(found, twice)]
        found = [y + mm(split(t[:, :HEAD_DIM]), split(y), "nn") for y, t in zip(less, twice)]
        level += 2
    return found


def mixes_of(normed, rim, kern):
    row8 = lax.broadcasted_iota(jnp.int32, (RIM, HEAD_DIM), 0)
    taps = kern.shape[1]
    shifted = [normed]
    for s in range(1, taps):
        moved = pltpu.roll(normed, s, 0)
        first = jnp.where(row8 < s, pltpu.roll(rim, s, 0), moved[:RIM])
        shifted.append(jnp.concatenate([first, moved[RIM:]], axis=0))
    return [
        sum(kern[j, i : i + 1] * shifted[taps - 1 - i] for i in range(taps)) for j in range(3)
    ]


def gates_kernel(decay_ref, beta_ref, e1_ref, e2_ref, edge_ref, rate_ref):
    length = decay_ref.shape[0]
    row, col = iotas()
    tril = jnp.where(row >= col, 1.0, 0.0).astype(bf16)
    tril = jnp.concatenate([tril] * 3, axis=1)
    for head in range(decay_ref.shape[1] // HEAD_DIM):
        here = slice(head * HEAD_DIM, (head + 1) * HEAD_DIM)
        decay = decay_ref[:, here]
        high = decay.astype(bf16)
        rest = decay - high.astype(f32)
        mid = rest.astype(bf16)
        low = (rest - mid.astype(f32)).astype(bf16)
        cumulative = lax.dot_general(
            tril, jnp.concatenate([high, mid, low], axis=0), DIMS["nn"], preferred_element_type=f32
        )
        middle = cumulative[length // 2 : length // 2 + 1]
        final = cumulative[length - 1 : length]
        e1_ref[:, here] = jnp.exp(cumulative - middle)
        e2_ref[:, here] = jnp.exp(middle - cumulative)
        edge_ref[0:8, here] = jnp.broadcast_to(jnp.exp(middle), (8, HEAD_DIM))
        edge_ref[8:16, here] = jnp.broadcast_to(jnp.exp(final - middle), (8, HEAD_DIM))
        edge_ref[16:24, here] = jnp.broadcast_to(jnp.exp(final), (8, HEAD_DIM))
        rate_ref[:, here] = down_rows(beta_ref[head : head + 1])


def scaled(x_ref, rim_ref, kern_ref, scale, rim_scale, at):
    x = x_ref[:, at].astype(f32)
    return mixes_of(x * scale, rim_ref[:, at] * rim_scale, kern_ref[:, :, at])


def scales(flags, scale_ref, rim_scale_ref):
    rim_scale = down_rows(rim_scale_ref[...])
    rim_scale = jnp.where(flags[4] != 0, rim_scale[rim_scale.shape[0] - RIM :], 0.0)
    return down_rows(scale_ref[...]), rim_scale


def keep_split(ref, j, n, parts):
    ref[j, n] = parts[0]
    ref[j, n + 1] = parts[1]


def kept(ref, j, n):
    return ref[j, n], ref[j, n + 1]


def local_kernel(
    slots, flags, x_ref, go_ref, kern_ref, e1_ref, e2_ref, edge_ref, rate_ref, rim_ref, scale_ref, rim_scale_ref,
    comp_ref, wide_ref, narrow_ref,
):
    length = x_ref.shape[0]
    row, col = iotas()
    strict, full = row > col, row >= col
    scale, rim_scale = scales(flags, scale_ref, rim_scale_ref)
    data = []
    for j, slot in enumerate(slots):
        at = lane_slice(slot ^ flags[0])
        mixes = scaled(x_ref, rim_ref, kern_ref, scale, rim_scale, at)
        act = [m / (1.0 + jnp.exp(-m)) for m in mixes]
        q, k = [a * lax.rsqrt(jnp.sum(a * a, axis=1, keepdims=True) + epsilon) for a in act[:2]]
        rate, e1, e2 = rate_ref[:, at], e1_ref[:, at], e2_ref[:, at]
        em, ecm, ef = [edge_ref[n : n + 1, at] for n in (0, 8, 16)]
        qf, kf, kb = q * e1, k * e1, k * e2
        skf, sqf, skb = split(kf), split(qf), split(kb)
        products = mm(rows_of(skf, sqf), skb, "nt")
        system = jnp.where(strict, rate * products[:length], 0.0)
        scores = split(jnp.where(full, products[length:], 0.0))
        go = exact(go_ref[:, at])
        fresh_grad = split(mm(scores, go, "tn"))
        wide_ref[j, 0], wide_ref[j, 1] = q, k
        for n, parts in enumerate((skf, sqf, skb, scores, fresh_grad)):
            keep_split(narrow_ref, j, 2 * n, parts)
        data.append(
            dict(system=system, go=go, rhs=cols_of(split(rate * kf * em), split(rate * act[2])), ke=split(kb * ecm),
                 qg=qf * em, fresh_grad=fresh_grad, ef=ef)
        )
    inverses = inverse_all([d["system"] for d in data])
    for j, (d, inverse) in enumerate(zip(data, inverses)):
        inverse = split(inverse)
        keep_split(narrow_ref, j, 14, inverse)
        solved = mm(inverse, d["rhs"], "nn")
        wide_ref[j, 2] = solved[:, HEAD_DIM:]
        d["solved"] = split(solved)
    for j, d in enumerate(data):
        solved = d["solved"]
        keep_split(narrow_ref, j, 10, (solved[0][:, :HEAD_DIM], solved[1][:, :HEAD_DIM]))
        keep_split(narrow_ref, j, 12, (solved[0][:, HEAD_DIM:], solved[1][:, HEAD_DIM:]))
        maps = mm(d["ke"], solved, "tn")
        comp_ref[j, 0:128] = jnp.where(row == col, d["ef"], 0.0) - maps[:, :HEAD_DIM]
        comp_ref[j, 128:256] = maps[:, HEAD_DIM:]
        w = (solved[0][:, :HEAD_DIM], solved[1][:, :HEAD_DIM])
        comp_ref[j, 256:384] = mm(split(d["qg"]), d["go"], "tn") - mm(w, d["fresh_grad"], "tn")


WIDE, NARROW = 3, 16


def ready_kernel(
    slots, flags, x_ref, kern_ref, e2_ref, edge_ref, rim_ref, scale_ref, rim_scale_ref, wide_ref, narrow_ref,
    more_ref, pairs_ref,
):
    scale, rim_scale = scales(flags, scale_ref, rim_scale_ref)
    for j, slot in enumerate(slots):
        at = lane_slice(slot ^ flags[0])
        mixes = scaled(x_ref, rim_ref, kern_ref, scale, rim_scale, at)
        sig = [1.0 / (1.0 + jnp.exp(-m)) for m in mixes]
        slope = [s * (1.0 + m * (1.0 - s)) for m, s in zip(mixes, sig)]
        act = [m * s for m, s in zip(mixes[:2], sig)]
        inv = [lax.rsqrt(jnp.sum(a * a, axis=1, keepdims=True) + epsilon) for a in act]
        em, ecm = edge_ref[0:1, at], edge_ref[8:9, at]
        scores, fresh_grad, inverse = [kept(narrow_ref, j, n) for n in (6, 8, 14)]
        solved = cols_of(kept(narrow_ref, j, 10), kept(narrow_ref, j, 12))
        seen = mm(scores, solved, "nn")
        ke = split(wide_ref[j, 1] * e2_ref[:, at] * ecm)
        back = mm(inverse, cols_of(fresh_grad, ke), "tn")
        more_ref[j, 0] = slope[0] * inv[0]
        more_ref[j, 1] = slope[1] * inv[1]
        more_ref[j, 2] = slope[2]
        more_ref[j, 3] = seen[:, HEAD_DIM:]
        more_ref[j, 4] = back[:, :HEAD_DIM]
        qf = narrow_ref[j, 2].astype(f32) + narrow_ref[j, 3].astype(f32)
        keep_split(pairs_ref, j, 0, split(qf * em - seen[:, :HEAD_DIM]))
        keep_split(pairs_ref, j, 2, split(back[:, HEAD_DIM:]))


MORE, PAIRS = 5, 4


def join_kernel(flags, keep_ref, recv_ref, *outs):
    later = flags[1] != 0
    outs = outs[-keep_ref.shape[0] :]
    for j, out in enumerate(outs):
        keep, recv = keep_ref[j], recv_ref[j]
        lo = jnp.where(later, recv, keep)
        hi = jnp.where(later, keep, recv)
        lo_map, hi_map = split(lo[0:128]), split(hi[0:128])
        forward = mm(hi_map, cols_of(lo_map, split(lo[128:256])), "nn")
        back = mm(lo_map, split(hi[256:384]), "tn")
        out[0:128] = forward[:, :HEAD_DIM]
        out[128:256] = forward[:, HEAD_DIM:] + hi[128:256]
        out[256:384] = back + lo[256:384]


def collect(place, parts, held):
    for n, part in enumerate(parts):
        held[place ^ n] = part[...]


def gather_kernel(count, waits, flags, *refs):
    parts, outs, held = refs[:count], refs[count + waits : -1], refs[-1]
    collect(flags[2], parts, held)
    maps = [split(held[p, 0:128]) for p in range(count)]
    state, grad = held[0, 128:256], held[count - 1, 256:384]
    whole = held[0, 0:128]
    for p in range(1, count):
        state = mm(maps[p], split(state), "nn") + held[p, 128:256]
        grad = mm(maps[count - 1 - p], split(grad), "tn") + held[count - 1 - p, 256:384]
        whole = mm(maps[p], split(whole), "nn")
    outs[0][...], outs[1][...], outs[2][...] = whole, state, grad


def hop_kernel(flags, t_ref, u_ref, g_ref, s_ref, e_ref, s_out, e_out):
    t = split(t_ref[...])
    s_out[...] = mm(t, split(s_ref[...]), "nn") + u_ref[...]
    e_out[...] = mm(t, split(e_ref[...]), "tn") + g_ref[...]


def spread_kernel(count, flags, *refs):
    parts, ins, outs, held, found = refs[:count], refs[count : -2 - count], refs[-2 - count : -2], refs[-2], refs[-1]
    collect(flags[2], parts, held)
    state, grad = ins[0][...], ins[1][...]
    for p in range(count):
        back = count - 1 - p
        found[p, 0:128] = state
        found[back, 128:256] = grad
        if p + 1 < count:
            state = mm(split(held[p, 0:128]), split(state), "nn") + held[p, 128:256]
            grad = mm(split(held[back, 0:128]), split(grad), "tn") + held[back, 256:384]
    for n, out in enumerate(outs):
        out[...] = found[flags[2] ^ n]


def two_gather_kernel(waits, flags, *refs):
    parts, outs = refs[:4], refs[4 + waits : -1]
    held = refs[-1]
    total_ref, known_ref, pairs_ref, found_ref = outs
    upper = flags[3] != 0
    collect(flags[2], parts, held)
    t = [split(held[p, 0:128]) for p in range(4)]
    u = [held[p, 128:256] for p in range(4)]
    g = [held[p, 256:384] for p in range(4)]
    last = mm(t[3], cols_of(t[2], split(u[2])), "nn")
    first = mm(t[1], cols_of(t[0], split(u[0])), "nn")
    second = first[:, HEAD_DIM:] + u[1]
    first, last, last_u = first[:, :HEAD_DIM], last[:, :HEAD_DIM], last[:, HEAD_DIM:]
    third = mm(t[2], split(g[3]), "tn") + g[2]
    low = mm(t[0], split(g[1]), "tn")
    s_second, s_third = split(second), split(third)
    forward = [jnp.zeros_like(second), u[0], second, mm(t[2], s_second, "nn") + u[2]]
    back = [mm(t[1], s_third, "tn") + g[1], third, g[3], jnp.zeros_like(third)]
    state = mm(split(last), s_second, "nn") + (last_u + u[3])
    grad = mm(split(first), s_third, "tn") + (low + g[0])
    total_ref[...] = jnp.where(upper, grad, state)
    pairs_ref[0], pairs_ref[1] = first, last
    for p in range(4):
        found_ref[p] = jnp.where(upper, back[p], forward[p])
        known_ref[p] = jnp.where(upper, forward[p], back[3 - p])


def reach_kernel(flags, *refs):
    parts, pairs_ref, found_ref, out_ref, early, held = refs[:4], refs[4], refs[5], refs[6], refs[7:11], refs[11]
    for n, out in enumerate(early):
        out[...] = found_ref[flags[2] ^ n]
    upper = flags[3] != 0
    collect(flags[2], parts, held)
    first, last = pairs_ref[0], pairs_ref[1]
    far_up = mm(split(held[2, 0:128]), split(first), "nn")
    far_down = mm(split(last), split(held[1, 0:128]), "nn")
    ups, downs = (held[0, 0:128], first, far_up), (held[3, 0:128], last, far_down)
    for n in range(3):
        high, low = split(jnp.where(upper, ups[n], jnp.transpose(downs[n])))
        out_ref[2 * n], out_ref[2 * n + 1] = high, low


def late_kernel(flags, recv_ref, known_ref, reach_ref, *refs):
    outs, found = refs[:-1], refs[-1]
    from_end = jnp.where(flags[3] != 0, 0, 3)
    recv = recv_ref[...]
    parts = split(recv)
    found[from_end] = recv
    for n in range(3):
        found[from_end ^ (n + 1)] = mm((reach_ref[2 * n], reach_ref[2 * n + 1]), parts, "nn") + known_ref[n + 1]
    for n, out in enumerate(outs):
        out[...] = found[flags[2] ^ n]


def part_kernel(flags, keep_ref, recv_ref, *refs):
    heads = keep_ref.shape[0]
    ins, (mine_ref, send_ref) = refs[:-2], refs[-2:]
    later, upper = flags[1] != 0, flags[3] != 0
    for j in range(heads):
        if len(ins) == heads:
            start, end = ins[j][0:128], ins[j][128:256]
        else:
            early, late = ins[j][...], ins[heads + j][...]
            start, end = jnp.where(upper, late, early), jnp.where(upper, early, late)
        keep, recv = keep_ref[j], recv_ref[j]
        lo = jnp.where(later, recv, keep)
        hi = jnp.where(later, keep, recv)
        start_hi = mm(split(lo[0:128]), split(start), "nn") + lo[128:256]
        end_lo = mm(split(hi[0:128]), split(end), "tn") + hi[256:384]
        mine_ref[j, 0:128] = jnp.where(later, start_hi, start)
        mine_ref[j, 128:256] = jnp.where(later, end, end_lo)
        send_ref[j, 0:128] = jnp.where(later, start, start_hi)
        send_ref[j, 128:256] = jnp.where(later, end_lo, end)


def back_kernel(
    slots, n_states, chained, last, flags, x_ref, go_ref, kern_ref, e1_ref, e2_ref, edge_ref, rate_ref, rim_ref, wide_ref,
    narrow_ref, more_ref, pairs_ref, *rest,
):
    state_refs, rest = rest[:n_states], rest[n_states:]
    if chained:
        sums_in, rim_grad_in, rest = rest[0], rest[1], rest[3:]
    out_hbm, grad_ref, sums_ref, rim_grad_ref, out_ref, sems = rest[:4] + rest[-2:]
    length = x_ref.shape[0]
    channels = x_ref.shape[1]
    row, col = iotas()
    row8 = lax.broadcasted_iota(jnp.int32, (RIM, HEAD_DIM), 0)
    strict, full = row > col, row >= col
    taps = kern_ref.shape[1]
    if chained:
        rim_grad_ref[...] = rim_grad_in[...]
    dot_all = rim_dot = 0.0
    data, copies = [], []
    states = [(ref, n) for ref in state_refs for n in range(ref.shape[0])]
    for j, slot in enumerate(slots):
        at = lane_slice(slot ^ flags[0])
        state_ref, n = states[j]
        start, end = split(state_ref[n, 0:128]), split(state_ref[n, 128:256])
        first = mm(rows_of(kept(pairs_ref, j, 0), kept(narrow_ref, j, 10)), start, "nn")
        z = more_ref[j, 4] + mm(kept(pairs_ref, j, 2), end, "nn")
        x = x_ref[:, at].astype(f32)
        out_ref[j] = (x + (more_ref[j, 3] + first[:length])).astype(bf16)
        copies.append(pltpu.make_async_copy(out_ref.at[j], out_hbm.at[:, at], sems.at[j]))
        copies[-1].start()
        data.append(dict(at=at, x=x, start=start, end=end, z=z, fresh=split(wide_ref[j, 2] - first[length:])))
    for j, d in enumerate(data):
        at = d["at"]
        q, k = wide_ref[j, 0], wide_ref[j, 1]
        gq, gk, gv = [more_ref[j, n] for n in range(3)]
        skf, sqf, skb = [kept(narrow_ref, j, n) for n in (0, 2, 4)]
        e1, e2, rate = e1_ref[:, at], e2_ref[:, at], rate_ref[:, at]
        em, ecm = edge_ref[0:1, at], edge_ref[8:9, at]
        go = exact(go_ref[:, at])
        second = mm(rows_of(go, split(d["z"])), rows_of(d["fresh"], d["start"]), "nt")
        score_grad = split(jnp.where(full, second[:length, :HEAD_DIM], 0.0))
        product_grad = split(jnp.where(strict, -rate * second[length:, :HEAD_DIM], 0.0))
        qg_grad = second[:length, HEAD_DIM:]
        kg_grad = -rate * second[length:, HEAD_DIM:]
        ke_grad = mm(d["fresh"], d["end"], "nt")
        pair = rows_of(score_grad, product_grad)
        third = mm(pair, skb, "nn")
        kb_grad = mm(pair, rows_of(sqf, skf), "tn")
        q_grad = e1 * (third[:length] + em * qg_grad)
        k_grad = e1 * (third[length:] + em * kg_grad) + e2 * (kb_grad + ecm * ke_grad)
        mix_grads = [
            gq * (q_grad - q * jnp.sum(q * q_grad, axis=1, keepdims=True)),
            gk * (k_grad - k * jnp.sum(k * k_grad, axis=1, keepdims=True)),
            gv * (rate * d["z"]),
        ]
        kern = kern_ref[:, :, at]
        normed_grad = rim_grad = 0.0
        for i in range(taps):
            each = sum(kern[n, i : i + 1] * mix_grads[n] for n in range(3))
            s = taps - 1 - i
            if s == 0:
                normed_grad = normed_grad + each
            else:
                moved = pltpu.roll(each, length - s, 0)
                normed_grad = normed_grad + jnp.where(row < length - s, moved, 0.0)
                rim_grad = rim_grad + jnp.where(row8 >= RIM - s, moved[length - RIM :], 0.0)
        grad_ref[j] = normed_grad
        rim_grad_ref[:, at] = rim_grad
        dot_all = dot_all + normed_grad * d["x"]
        rim_dot = rim_dot + rim_grad * rim_ref[:, at]
    sums = row_sums(dot_all)
    rim_sums = jnp.broadcast_to(jnp.sum(rim_dot, axis=1, keepdims=True), rim_dot.shape)
    if chained:
        sums, rim_sums = sums + sums_in[...], rim_sums + rim_grad_in[:, channels:]
    sums_ref[...] = sums
    rim_grad_ref[:, channels:] = rim_sums
    if last:
        rest[4][...] = rim_sums
    for copy in copies:
        copy.wait()


def finish_kernel(slots, width, flags, x_ref, go_ref, scale_ref, inner_ref, next_sums_ref, next_ref, *refs):
    grads, (out_hbm, out_ref, sems) = refs[:-3], refs[-3:]
    length = x_ref.shape[0]
    scale = down_rows(scale_ref[...])
    inner = down_rows(inner_ref[...])
    last = flags[5] == 0
    next_sums = jnp.where(last, 0.0, next_sums_ref[...])
    inner = jnp.concatenate([inner[: length - RIM], inner[length - RIM :] + next_sums], axis=0)
    cubed = scale * scale * scale * inner * (1.0 / width)
    copies = []
    places = [(ref, n) for ref in grads for n in range(ref.shape[0])]
    for j, (slot, (grad_ref, n)) in enumerate(zip(slots, places)):
        at = lane_slice(slot ^ flags[0])
        grad = grad_ref[n]
        next_grad = jnp.where(last, 0.0, next_ref[:, at])
        grad = jnp.concatenate([grad[: length - RIM], grad[length - RIM :] + next_grad], axis=0)
        total = go_ref[:, at].astype(f32) + grad * scale - x_ref[:, at].astype(f32) * cubed
        out_ref[j] = total.astype(bf16)
        copies.append(pltpu.make_async_copy(out_ref.at[j], out_hbm.at[:, at], sems.at[j]))
        copies[-1].start()
    for copy in copies:
        copy.wait()


def call(kernel, outs, *args, name=None, scratch=(), scalar=(), cost=None, far_in=False, far_out=(), unread=(), alias=None):
    spec, hbm = pl.BlockSpec(memory_space=pltpu.VMEM), pl.BlockSpec(memory_space=pltpu.HBM)
    in_specs = [hbm if far_in else spec] * len(args)
    in_specs += [pl.BlockSpec(memory_space=pl.ANY)] * len(unread)
    args = args + tuple(unread)
    aliases = {}
    if alias is not None:
        args, in_specs, aliases = args + (alias,), in_specs + [hbm], {len(args): 0}
    return pl.pallas_call(
        (lambda *refs: kernel(placed(*scalar), *refs)) if scalar else kernel,
        out_shape=list(outs),
        in_specs=in_specs,
        out_specs=[hbm if n in far_out else spec for n in range(len(outs))],
        scratch_shapes=scratch,
        input_output_aliases=aliases,
        compiler_params=pltpu.CompilerParams(vmem_limit_bytes=VMEM_LIMIT),
        cost_estimate=cost,
        name=name,
    )(*args)


BESIDE = pl.CostEstimate(flops=10**9, bytes_accessed=10**7, transcendentals=0)


def array(*shape, dtype=f32):
    return jax.ShapeDtypeStruct(shape, dtype)


def placed(per, spots):
    me = lax.axis_index("ctx")
    place, later = lax.rem(lax.shift_right_logical(me, 1), per), lax.rem(me, 2)
    row = lax.rem(lax.div(me, 2 * per), 2)
    return [later * per + place, later, place, row, me, spots - 1 - me]


def shards(inputs, out_grads, conv_weight, log_decay, beta):
    length, channels = inputs.shape
    heads = channels // HEAD_DIM
    sections, spots = lax.axis_size("section"), lax.axis_size("ctx")
    width = channels * sections
    per = heads // 2
    count = per
    slabs = spots // (2 * count)
    spot = functools.partial(call, scalar=(per, spots))

    def turned(value, sec, shift):
        route = [
            (s * spots + c, ((s + sec) % sections) * spots + (c + shift) % spots)
            for s in range(sections)
            for c in range(spots)
        ]
        return lax.ppermute(value, ("section", "ctx"), route)

    def swapped(value, distance):
        return lax.ppermute(value, "ctx", [(i, i ^ distance) for i in range(spots)])

    def moved(value, shift):
        return lax.ppermute(
            value, "ctx", [(i, i + shift) for i in range(spots) if 0 <= i + shift < spots]
        )

    payload, sums, x, go, kern, decay, rates = call(
        prelude_kernel,
        (
            array(RIM, channels + length), array(RIM, length), array(*inputs.shape, dtype=bf16),
            array(*inputs.shape, dtype=bf16), array(*conv_weight.shape), array(*inputs.shape), array(heads, length),
        ),
        *[pltpu.with_memory_space_constraint(a, pltpu.HBM) for a in (inputs, out_grads, conv_weight, log_decay, beta.T)],
        name="prelude", far_in=True, scratch=[pltpu.SemaphoreType.DMA((5,))],
    )
    total = sums
    rim_total = 0.0
    for sec in range(1, sections):
        total = total + turned(sums, sec, 0)
        rim_total = rim_total + turned(sums, sec, 1)
    rim = turned(payload, 0, 1)
    e1, e2, edge, rate = call(
        gates_kernel,
        (array(length, channels), array(length, channels), array(24, channels), array(length, channels)),
        decay, rates, name="gates", cost=BESIDE,
    )
    scale = lax.rsqrt(total / width + norm_eps)
    rim_scale = lax.rsqrt((rim_total + rim[:, channels:]) / width + norm_eps)

    shared = (x, go, kern, e1, e2, edge, rate, rim)
    tile = (HEAD_DIM, HEAD_DIM)

    def local(slots, name):
        n = len(slots)
        return spot(
            functools.partial(local_kernel, slots),
            (array(n, 384, HEAD_DIM), array(n, WIDE, *tile), array(n, NARROW, *tile, dtype=bf16)),
            *shared, scale, rim_scale, name=name,
        )

    def prepared(slots, saved, name):
        n = len(slots)
        return spot(
            functools.partial(ready_kernel, slots),
            (array(n, MORE, *tile), array(n, PAIRS, *tile, dtype=bf16)),
            x, kern, e2, edge, rim, scale, rim_scale, *saved, name=name, cost=BESIDE,
        )

    inner_slots, outer_slots = range(per), range(per, 2 * per)
    outer, *outer_saved = local(outer_slots, "local_outer")
    outer_recv = swapped(outer, 1)
    inner, *inner_saved = local(inner_slots, "local_inner")
    pairs = spot(join_kernel, (array(384, HEAD_DIM),) * per, inner, outer_recv, name="join")
    parts = [pairs[0]] + [swapped(pairs[n], 2 * n) for n in range(1, count)]
    outer_saved += prepared(outer_slots, outer_saved, "ready_outer")
    inner_saved += prepared(inner_slots, inner_saved, "ready_inner")
    ahead = [outer_saved[-1], inner_saved[-1]]

    held = pltpu.VMEM((count, 384, HEAD_DIM), f32)
    square = array(*tile)
    step = 2 * count

    def returned(values):
        return [values[0]] + [swapped(values[n], 2 * n) for n in range(1, count)]

    if slabs == 2 and count == 4:
        found = pltpu.VMEM((count, *tile), f32)
        total, known, products, sure = spot(
            functools.partial(two_gather_kernel, len(ahead)),
            (square, array(4, *tile), array(2, *tile), array(4, *tile)),
            *parts, name="gather", scratch=[held], unread=ahead,
        )
        other = swapped(total, step)
        reach, *early = spot(
            reach_kernel, (array(6, *tile, dtype=bf16),) + (square,) * 4,
            *parts, products, sure, name="reach", scratch=[held], cost=BESIDE,
        )
        early = returned(early)
        late = spot(late_kernel, (square,) * 4, other, known, reach, name="late", scratch=[found])
        states = early + returned(late)
    else:
        gathered = spot(
            functools.partial(gather_kernel, count, len(ahead)), (square,) * 3,
            *parts, name="gather", scratch=[held], unread=ahead,
        )
        ends = (jnp.zeros(tile, f32),) * 2
        for hop in range(slabs - 1):
            if hop == 0:
                ends = gathered[1:]
            else:
                ends = spot(hop_kernel, (square,) * 2, *gathered, *ends, name=f"hop{hop}")
            ends = (moved(ends[0], step), moved(ends[1], -step))
        states = returned(
            spot(
                functools.partial(spread_kernel, count), (array(256, HEAD_DIM),) * count,
                *parts, *ends, name="spread", scratch=[held, pltpu.VMEM((count, 256, HEAD_DIM), f32)],
            )
        )
    mine, send = spot(
        part_kernel, (array(per, 256, HEAD_DIM),) * 2, inner, outer_recv, *states, name="part"
    )
    far = swapped(send, 1)

    def backward(slots, saved, states, chain, name):
        n = len(slots)
        last = chain is not None
        before = (chain[2], chain[3]) if last else ()
        return spot(
            functools.partial(back_kernel, slots, len(states), last, last),
            (
                array(*inputs.shape, dtype=bf16), array(n, length, HEAD_DIM), array(RIM, length),
                array(RIM, channels + HEAD_DIM),
            )
            + (array(RIM, HEAD_DIM),) * last,
            *shared, *saved, *states, *before, name=name, far_out=(0,),
            alias=None if chain is None else chain[0],
            scratch=[pltpu.VMEM((n, length, HEAD_DIM), bf16), pltpu.SemaphoreType.DMA((n,))],
        )

    chain = backward(inner_slots, inner_saved, (mine,), None, "back_inner")
    grads = [chain[1]]
    chain = backward(outer_slots, outer_saved, (far,), chain, "back_outer")
    grads.append(chain[1])
    slots = [*inner_slots, *outer_slots]
    stream_out, _, inner_sum, rim_grad, rim_sums = chain

    inner_total, next_sums = inner_sum, 0.0
    for sec in range(1, sections):
        inner_total = inner_total + turned(inner_sum, sec, 0)
        next_sums = next_sums + turned(rim_sums, sec, -1)
    next_rim = turned(rim_grad, 0, -1)
    (input_grad,) = spot(
        functools.partial(finish_kernel, slots, width), (array(*inputs.shape, dtype=bf16),),
        x, go, scale, inner_total, next_sums + next_rim[:, channels:], next_rim, *grads, name="finish",
        far_out=(0,), scratch=[pltpu.VMEM((heads, length, HEAD_DIM), bf16), pltpu.SemaphoreType.DMA((heads,))],
    )
    return (stream_out, input_grad)


def solution(mesh):
    in_specs = (
        P("ctx", "section"),
        P("ctx", "section"),
        P(None, None, "section"),
        P("ctx", "section"),
        P("ctx", "section"),
    )
    out_specs = (P("ctx", "section"), P("ctx", "section"))
    return jax.shard_map(shards, mesh=mesh, in_specs=in_specs, out_specs=out_specs, check_vma=False)
```

```python
import functools

import jax
import jax.numpy as jnp
from jax import lax
from jax.experimental import pallas as pl
from jax.experimental.pallas import tpu as pltpu
from jax.sharding import PartitionSpec as P

HEAD_DIM = 128
RIM = 8
epsilon = 1e-06
norm_eps = 1e-05
f32 = jnp.float32
bf16 = jnp.bfloat16
VMEM_LIMIT = 24 * 1024 * 1024

DIMS = {
    "nn": (((1,), (0,)), ((), ())),
    "nt": (((1,), (1,)), ((), ())),
    "tn": (((0,), (0,)), ((), ())),
}


def split(a):
    high = a.astype(bf16)
    return high, (a - high.astype(f32)).astype(bf16)


def exact(a):
    return a, None


def rows_of(*parts):
    highs = jnp.concatenate([p[0] for p in parts], axis=0)
    lows = [jnp.zeros_like(p[0]) if p[1] is None else p[1] for p in parts]
    return highs, jnp.concatenate(lows, axis=0)


def cols_of(*parts):
    return tuple(jnp.concatenate([p[i] for p in parts], axis=1) for i in range(2))


def mm(a, b, form):
    width = b[0].shape[1]
    if form != "nt" and a[1] is not None and b[1] is not None and width == HEAD_DIM:
        right = jnp.concatenate(b, axis=1)
        left = jnp.concatenate(a, axis=0 if form == "tn" else 1)
        out = lax.dot_general(left, jnp.concatenate([right, right], axis=0), DIMS[form], preferred_element_type=f32)
        return out[:, :width] + out[:, width:]
    pairs = [(a[0], b[0])]
    if a[1] is not None:
        pairs.append((a[1], b[0]))
    if b[1] is not None:
        pairs.append((a[0], b[1]))
    left = jnp.concatenate([p[0] for p in pairs], axis=0 if form == "tn" else 1)
    right = jnp.concatenate([p[1] for p in pairs], axis=1 if form == "nt" else 0)
    return lax.dot_general(left, right, DIMS[form], preferred_element_type=f32)


def row_sums(a):
    high = a.astype(bf16)
    rest = a - high.astype(f32)
    mid = rest.astype(bf16)
    low = (rest - mid.astype(f32)).astype(bf16)
    terms = jnp.concatenate([high, mid, low], axis=1)
    ones = jnp.ones((RIM, terms.shape[1]), bf16)
    return lax.dot_general(ones, terms, DIMS["nt"], preferred_element_type=f32)


def down_rows(row):
    return jnp.transpose(jnp.broadcast_to(row[0:1], (HEAD_DIM, row.shape[1])))


def iotas(n=HEAD_DIM):
    return (
        lax.broadcasted_iota(jnp.int32, (n, n), 0),
        lax.broadcasted_iota(jnp.int32, (n, n), 1),
    )


def lane_slice(place):
    return pl.ds(pl.multiple_of(place * HEAD_DIM, HEAD_DIM), HEAD_DIM)


def prelude_kernel(
    x_hbm, go_hbm, kern_hbm, decay_hbm, beta_hbm, payload_ref, sums_ref, x_ref, go_ref, kern_ref, decay_ref, beta_ref, sems
):
    pairs = ((x_hbm, x_ref), (go_hbm, go_ref), (kern_hbm, kern_ref), (decay_hbm, decay_ref), (beta_hbm, beta_ref))
    copies = [pltpu.make_async_copy(src, dst, sems.at[n]) for n, (src, dst) in enumerate(pairs)]
    for copy in copies:
        copy.start()
    copies[0].wait()
    x = x_ref[...].astype(f32)
    channels = x.shape[1]
    sums = row_sums(x * x)
    sums_ref[...] = sums
    payload_ref[:, :channels] = x[x.shape[0] - RIM :]
    payload_ref[:, channels:] = sums
    for copy in copies[1:]:
        copy.wait()


BASE = 5


def inverse_all(systems):
    row, col = iotas()
    size = 1 << BASE
    own = row >> BASE == col >> BASE
    row8 = lax.broadcasted_iota(jnp.int32, (RIM, HEAD_DIM), 0)
    col8 = lax.broadcasted_iota(jnp.int32, (RIM, HEAD_DIM), 1)
    first = (col8 >> BASE) << BASE
    found = []
    for n in systems:
        blocks = jnp.sum(jnp.where(own, n, 0.0).reshape(-1, size, HEAD_DIM), axis=0)
        tiles = [jnp.where(row8 + RIM * t == (col8 & (size - 1)), 1.0, 0.0) for t in range(size // RIM)]
        for s in range(size - 1):
            done = tiles[s // RIM][s % RIM : s % RIM + 1]
            for t in range(s // RIM, size // RIM):
                column = jnp.take_along_axis(
                    blocks[RIM * t : RIM * (t + 1)], first + s, axis=1, mode="promise_in_bounds"
                )
                tiles[t] = tiles[t] - column * done
        found.append(jnp.where(own, jnp.concatenate(tiles * (HEAD_DIM // size), axis=0), 0.0))
    level = BASE
    while (1 << level) < HEAD_DIM:
        mask = (row >> (level + 2) == col >> (level + 2)) & (row >> level != col >> level)
        parts = [split(d) for d in found]
        cross = [split(jnp.where(mask, n, 0.0)) for n in systems]
        maps = [split(mm(p, c, "nn")) for p, c in zip(parts, cross)]
        twice = [mm(m, cols_of(m, p), "nn") for m, p in zip(maps, parts)]
        less = [d - t[:, HEAD_DIM:] for d, t in zip(found, twice)]
        found = [y + mm(split(t[:, :HEAD_DIM]), split(y), "nn") for y, t in zip(less, twice)]
        level += 2
    return found


def mixes_of(normed, rim, kern):
    row8 = lax.broadcasted_iota(jnp.int32, (RIM, HEAD_DIM), 0)
    taps = kern.shape[1]
    shifted = [normed]
    for s in range(1, taps):
        moved = pltpu.roll(normed, s, 0)
        first = jnp.where(row8 < s, pltpu.roll(rim, s, 0), moved[:RIM])
        shifted.append(jnp.concatenate([first, moved[RIM:]], axis=0))
    return [
        sum(kern[j, i : i + 1] * shifted[taps - 1 - i] for i in range(taps)) for j in range(3)
    ]


def gates_kernel(decay_ref, beta_ref, e1_ref, e2_ref, edge_ref, rate_ref):
    length = decay_ref.shape[0]
    row, col = iotas()
    tril = jnp.where(row >= col, 1.0, 0.0).astype(bf16)
    tril = jnp.concatenate([tril] * 3, axis=1)
    for head in range(decay_ref.shape[1] // HEAD_DIM):
        here = slice(head * HEAD_DIM, (head + 1) * HEAD_DIM)
        decay = decay_ref[:, here]
        high = decay.astype(bf16)
        rest = decay - high.astype(f32)
        mid = rest.astype(bf16)
        low = (rest - mid.astype(f32)).astype(bf16)
        cumulative = lax.dot_general(
            tril, jnp.concatenate([high, mid, low], axis=0), DIMS["nn"], preferred_element_type=f32
        )
        middle = cumulative[length // 2 : length // 2 + 1]
        final = cumulative[length - 1 : length]
        e1_ref[:, here] = jnp.exp(cumulative - middle)
        e2_ref[:, here] = jnp.exp(middle - cumulative)
        edge_ref[0:8, here] = jnp.broadcast_to(jnp.exp(middle), (8, HEAD_DIM))
        edge_ref[8:16, here] = jnp.broadcast_to(jnp.exp(final - middle), (8, HEAD_DIM))
        edge_ref[16:24, here] = jnp.broadcast_to(jnp.exp(final), (8, HEAD_DIM))
        rate_ref[:, here] = down_rows(beta_ref[head : head + 1])


def scaled(x_ref, rim_ref, kern_ref, scale, rim_scale, at):
    x = x_ref[:, at].astype(f32)
    return mixes_of(x * scale, rim_ref[:, at] * rim_scale, kern_ref[:, :, at])


def scales(flags, scale_ref, rim_scale_ref):
    rim_scale = down_rows(rim_scale_ref[...])
    rim_scale = jnp.where(flags[4] != 0, rim_scale[rim_scale.shape[0] - RIM :], 0.0)
    return down_rows(scale_ref[...]), rim_scale


def keep_split(ref, j, n, parts):
    ref[j, n] = parts[0]
    ref[j, n + 1] = parts[1]


def kept(ref, j, n):
    return ref[j, n], ref[j, n + 1]


def local_kernel(
    slots, flags, x_ref, go_ref, kern_ref, e1_ref, e2_ref, edge_ref, rate_ref, rim_ref, scale_ref, rim_scale_ref,
    *rest,
):
    comp_ref, wide_ref, narrow_ref = rest[-3:]
    length = x_ref.shape[0]
    row, col = iotas()
    strict, full = row > col, row >= col
    scale, rim_scale = scales(flags, scale_ref, rim_scale_ref)
    data = []
    for j, slot in enumerate(slots):
        at = lane_slice(slot ^ flags[0])
        mixes = scaled(x_ref, rim_ref, kern_ref, scale, rim_scale, at)
        act = [m / (1.0 + jnp.exp(-m)) for m in mixes]
        q, k = [a * lax.rsqrt(jnp.sum(a * a, axis=1, keepdims=True) + epsilon) for a in act[:2]]
        rate, e1, e2 = rate_ref[:, at], e1_ref[:, at], e2_ref[:, at]
        em, ecm, ef = [edge_ref[n : n + 1, at] for n in (0, 8, 16)]
        qf, kf, kb = q * e1, k * e1, k * e2
        skf, sqf, skb = split(kf), split(qf), split(kb)
        products = mm(rows_of(skf, sqf), skb, "nt")
        system = jnp.where(strict, rate * products[:length], 0.0)
        scores = split(jnp.where(full, products[length:], 0.0))
        go = exact(go_ref[:, at])
        fresh_grad = split(mm(scores, go, "tn"))
        wide_ref[j, 0], wide_ref[j, 1] = q, k
        for n, parts in enumerate((skf, sqf, skb, scores, fresh_grad)):
            keep_split(narrow_ref, j, 2 * n, parts)
        data.append(
            dict(system=system, go=go, rhs=cols_of(split(rate * kf * em), split(rate * act[2])), ke=split(kb * ecm),
                 qg=qf * em, fresh_grad=fresh_grad, ef=ef)
        )
    inverses = inverse_all([d["system"] for d in data])
    for j, (d, inverse) in enumerate(zip(data, inverses)):
        inverse = split(inverse)
        keep_split(narrow_ref, j, 14, inverse)
        solved = mm(inverse, d["rhs"], "nn")
        wide_ref[j, 2] = solved[:, HEAD_DIM:]
        d["solved"] = split(solved)
    for j, d in enumerate(data):
        solved = d["solved"]
        keep_split(narrow_ref, j, 10, (solved[0][:, :HEAD_DIM], solved[1][:, :HEAD_DIM]))
        keep_split(narrow_ref, j, 12, (solved[0][:, HEAD_DIM:], solved[1][:, HEAD_DIM:]))
        maps = mm(d["ke"], solved, "tn")
        comp_ref[j, 0:128] = jnp.where(row == col, d["ef"], 0.0) - maps[:, :HEAD_DIM]
        comp_ref[j, 128:256] = maps[:, HEAD_DIM:]
        w = (solved[0][:, :HEAD_DIM], solved[1][:, :HEAD_DIM])
        comp_ref[j, 256:384] = mm(split(d["qg"]), d["go"], "tn") - mm(w, d["fresh_grad"], "tn")


WIDE, NARROW = 3, 16


def ready_kernel(
    slots, flags, x_ref, kern_ref, e2_ref, edge_ref, rim_ref, scale_ref, rim_scale_ref, wide_ref, narrow_ref,
    more_ref, pairs_ref,
):
    scale, rim_scale = scales(flags, scale_ref, rim_scale_ref)
    for j, slot in enumerate(slots):
        at = lane_slice(slot ^ flags[0])
        mixes = scaled(x_ref, rim_ref, kern_ref, scale, rim_scale, at)
        sig = [1.0 / (1.0 + jnp.exp(-m)) for m in mixes]
        slope = [s * (1.0 + m * (1.0 - s)) for m, s in zip(mixes, sig)]
        act = [m * s for m, s in zip(mixes[:2], sig)]
        inv = [lax.rsqrt(jnp.sum(a * a, axis=1, keepdims=True) + epsilon) for a in act]
        em, ecm = edge_ref[0:1, at], edge_ref[8:9, at]
        scores, fresh_grad, inverse = [kept(narrow_ref, j, n) for n in (6, 8, 14)]
        solved = cols_of(kept(narrow_ref, j, 10), kept(narrow_ref, j, 12))
        seen = mm(scores, solved, "nn")
        ke = split(wide_ref[j, 1] * e2_ref[:, at] * ecm)
        back = mm(inverse, cols_of(fresh_grad, ke), "tn")
        more_ref[j, 0] = slope[0] * inv[0]
        more_ref[j, 1] = slope[1] * inv[1]
        more_ref[j, 2] = slope[2]
        more_ref[j, 3] = seen[:, HEAD_DIM:]
        more_ref[j, 4] = back[:, :HEAD_DIM]
        qf = narrow_ref[j, 2].astype(f32) + narrow_ref[j, 3].astype(f32)
        keep_split(pairs_ref, j, 0, split(qf * em - seen[:, :HEAD_DIM]))
        keep_split(pairs_ref, j, 2, split(back[:, HEAD_DIM:]))


MORE, PAIRS = 5, 4


def join_kernel(flags, keep_ref, recv_ref, *outs):
    later = flags[1] != 0
    outs = outs[-keep_ref.shape[0] :]
    for j, out in enumerate(outs):
        keep, recv = keep_ref[j], recv_ref[j]
        lo = jnp.where(later, recv, keep)
        hi = jnp.where(later, keep, recv)
        lo_map, hi_map = split(lo[0:128]), split(hi[0:128])
        forward = mm(hi_map, cols_of(lo_map, split(lo[128:256])), "nn")
        back = mm(lo_map, split(hi[256:384]), "tn")
        out[0:128] = forward[:, :HEAD_DIM]
        out[128:256] = forward[:, HEAD_DIM:] + hi[128:256]
        out[256:384] = back + lo[256:384]


def collect(place, parts, held):
    for n, part in enumerate(parts):
        held[place ^ n] = part[...]


def gather_kernel(count, waits, flags, *refs):
    parts, outs, held = refs[:count], refs[count + waits : -1], refs[-1]
    collect(flags[2], parts, held)
    maps = [split(held[p, 0:128]) for p in range(count)]
    state, grad = held[0, 128:256], held[count - 1, 256:384]
    whole = held[0, 0:128]
    for p in range(1, count):
        state = mm(maps[p], split(state), "nn") + held[p, 128:256]
        grad = mm(maps[count - 1 - p], split(grad), "tn") + held[count - 1 - p, 256:384]
        whole = mm(maps[p], split(whole), "nn")
    outs[0][...], outs[1][...], outs[2][...] = whole, state, grad


def hop_kernel(flags, t_ref, u_ref, g_ref, s_ref, e_ref, s_out, e_out):
    t = split(t_ref[...])
    s_out[...] = mm(t, split(s_ref[...]), "nn") + u_ref[...]
    e_out[...] = mm(t, split(e_ref[...]), "tn") + g_ref[...]


def spread_kernel(count, flags, *refs):
    parts, ins, outs, held, found = refs[:count], refs[count : -2 - count], refs[-2 - count : -2], refs[-2], refs[-1]
    collect(flags[2], parts, held)
    state, grad = ins[0][...], ins[1][...]
    for p in range(count):
        back = count - 1 - p
        found[p, 0:128] = state
        found[back, 128:256] = grad
        if p + 1 < count:
            state = mm(split(held[p, 0:128]), split(state), "nn") + held[p, 128:256]
            grad = mm(split(held[back, 0:128]), split(grad), "tn") + held[back, 256:384]
    for n, out in enumerate(outs):
        out[...] = found[flags[2] ^ n]


def two_gather_kernel(waits, flags, *refs):
    parts, outs = refs[:4], refs[4 + waits : -1]
    held = refs[-1]
    total_ref, known_ref, pairs_ref, found_ref = outs
    upper = flags[3] != 0
    collect(flags[2], parts, held)
    t = [split(held[p, 0:128]) for p in range(4)]
    u = [held[p, 128:256] for p in range(4)]
    g = [held[p, 256:384] for p in range(4)]
    last = mm(t[3], cols_of(t[2], split(u[2])), "nn")
    first = mm(t[1], cols_of(t[0], split(u[0])), "nn")
    second = first[:, HEAD_DIM:] + u[1]
    first, last, last_u = first[:, :HEAD_DIM], last[:, :HEAD_DIM], last[:, HEAD_DIM:]
    third = mm(t[2], split(g[3]), "tn") + g[2]
    low = mm(t[0], split(g[1]), "tn")
    s_second, s_third = split(second), split(third)
    forward = [jnp.zeros_like(second), u[0], second, mm(t[2], s_second, "nn") + u[2]]
    back = [mm(t[1], s_third, "tn") + g[1], third, g[3], jnp.zeros_like(third)]
    state = mm(split(last), s_second, "nn") + (last_u + u[3])
    grad = mm(split(first), s_third, "tn") + (low + g[0])
    total_ref[...] = jnp.where(upper, grad, state)
    pairs_ref[0], pairs_ref[1] = first, last
    for p in range(4):
        found_ref[p] = jnp.where(upper, back[p], forward[p])
        known_ref[p] = jnp.where(upper, forward[p], back[3 - p])


def reach_kernel(flags, *refs):
    parts, pairs_ref, found_ref, out_ref, early, held = refs[:4], refs[4], refs[5], refs[6], refs[7:11], refs[11]
    for n, out in enumerate(early):
        out[...] = found_ref[flags[2] ^ n]
    upper = flags[3] != 0
    collect(flags[2], parts, held)
    first, last = pairs_ref[0], pairs_ref[1]
    far_up = mm(split(held[2, 0:128]), split(first), "nn")
    far_down = mm(split(last), split(held[1, 0:128]), "nn")
    ups, downs = (held[0, 0:128], first, far_up), (held[3, 0:128], last, far_down)
    for n in range(3):
        high, low = split(jnp.where(upper, ups[n], jnp.transpose(downs[n])))
        out_ref[2 * n], out_ref[2 * n + 1] = high, low


def late_kernel(flags, recv_ref, known_ref, reach_ref, *refs):
    outs, found = refs[:-1], refs[-1]
    from_end = jnp.where(flags[3] != 0, 0, 3)
    recv = recv_ref[...]
    parts = split(recv)
    found[from_end] = recv
    for n in range(3):
        found[from_end ^ (n + 1)] = mm((reach_ref[2 * n], reach_ref[2 * n + 1]), parts, "nn") + known_ref[n + 1]
    for n, out in enumerate(outs):
        out[...] = found[flags[2] ^ n]


def part_kernel(sets, per_head, flags, *refs):
    maps = [(keep, recv, n) for keep, recv in zip(refs[:sets], refs[sets : 2 * sets]) for n in range(keep.shape[0])]
    ins, (mine_ref, send_ref) = refs[2 * sets : -2], refs[-2:]
    later, upper = flags[1] != 0, flags[3] != 0
    for j, (keep_ref, recv_ref, n) in enumerate(maps):
        if per_head == 1:
            start, end = ins[j][0:128], ins[j][128:256]
        else:
            early, late = ins[2 * j][...], ins[2 * j + 1][...]
            start, end = jnp.where(upper, late, early), jnp.where(upper, early, late)
        keep, recv = keep_ref[n], recv_ref[n]
        lo = jnp.where(later, recv, keep)
        hi = jnp.where(later, keep, recv)
        start_hi = mm(split(lo[0:128]), split(start), "nn") + lo[128:256]
        end_lo = mm(split(hi[0:128]), split(end), "tn") + hi[256:384]
        mine_ref[j, 0:128] = jnp.where(later, start_hi, start)
        mine_ref[j, 128:256] = jnp.where(later, end, end_lo)
        send_ref[j, 0:128] = jnp.where(later, start, start_hi)
        send_ref[j, 128:256] = jnp.where(later, end_lo, end)


def back_kernel(
    slots, homes, chained, flags, x_ref, go_ref, kern_ref, e1_ref, e2_ref, edge_ref, rate_ref, rim_ref, state_ref,
    *rest,
):
    sets = 1 + max(n for n, _ in homes)
    saved, rest = [rest[4 * n : 4 * n + 4] for n in range(sets)], rest[4 * sets :]
    if chained:
        sums_in, rim_grad_in, rest = rest[0], rest[1], rest[3:]
    out_hbm, grad_ref, sums_ref, rim_grad_ref, out_ref, sems = rest[:4] + rest[-2:]
    length = x_ref.shape[0]
    channels = x_ref.shape[1]
    row, col = iotas()
    row8 = lax.broadcasted_iota(jnp.int32, (RIM, HEAD_DIM), 0)
    strict, full = row > col, row >= col
    taps = kern_ref.shape[1]
    if chained:
        rim_grad_ref[...] = rim_grad_in[...]
    dot_all = rim_dot = 0.0
    data, copies = [], []
    for j, (slot, (n, i)) in enumerate(zip(slots, homes)):
        at = lane_slice(slot ^ flags[0])
        wide_ref, narrow_ref, more_ref, pairs_ref = saved[n]
        start, end = split(state_ref[j, 0:128]), split(state_ref[j, 128:256])
        first = mm(rows_of(kept(pairs_ref, i, 0), kept(narrow_ref, i, 10)), start, "nn")
        z = more_ref[i, 4] + mm(kept(pairs_ref, i, 2), end, "nn")
        x = x_ref[:, at].astype(f32)
        out_ref[j] = (x + (more_ref[i, 3] + first[:length])).astype(bf16)
        copies.append(pltpu.make_async_copy(out_ref.at[j], out_hbm.at[:, at], sems.at[j]))
        copies[-1].start()
        data.append(dict(at=at, x=x, start=start, end=end, z=z, fresh=split(wide_ref[i, 2] - first[length:])))
    for j, (d, (n, i)) in enumerate(zip(data, homes)):
        at = d["at"]
        wide_ref, narrow_ref, more_ref, _ = saved[n]
        q, k = wide_ref[i, 0], wide_ref[i, 1]
        gq, gk, gv = [more_ref[i, n] for n in range(3)]
        skf, sqf, skb = [kept(narrow_ref, i, n) for n in (0, 2, 4)]
        e1, e2, rate = e1_ref[:, at], e2_ref[:, at], rate_ref[:, at]
        em, ecm = edge_ref[0:1, at], edge_ref[8:9, at]
        go = exact(go_ref[:, at])
        second = mm(rows_of(go, split(d["z"])), rows_of(d["fresh"], d["start"]), "nt")
        score_grad = split(jnp.where(full, second[:length, :HEAD_DIM], 0.0))
        product_grad = split(jnp.where(strict, -rate * second[length:, :HEAD_DIM], 0.0))
        qg_grad = second[:length, HEAD_DIM:]
        kg_grad = -rate * second[length:, HEAD_DIM:]
        ke_grad = mm(d["fresh"], d["end"], "nt")
        pair = rows_of(score_grad, product_grad)
        third = mm(pair, skb, "nn")
        kb_grad = mm(pair, rows_of(sqf, skf), "tn")
        q_grad = e1 * (third[:length] + em * qg_grad)
        k_grad = e1 * (third[length:] + em * kg_grad) + e2 * (kb_grad + ecm * ke_grad)
        mix_grads = [
            gq * (q_grad - q * jnp.sum(q * q_grad, axis=1, keepdims=True)),
            gk * (k_grad - k * jnp.sum(k * k_grad, axis=1, keepdims=True)),
            gv * (rate * d["z"]),
        ]
        kern = kern_ref[:, :, at]
        normed_grad = rim_grad = 0.0
        for i in range(taps):
            each = sum(kern[n, i : i + 1] * mix_grads[n] for n in range(3))
            s = taps - 1 - i
            if s == 0:
                normed_grad = normed_grad + each
            else:
                moved = pltpu.roll(each, length - s, 0)
                normed_grad = normed_grad + jnp.where(row < length - s, moved, 0.0)
                rim_grad = rim_grad + jnp.where(row8 >= RIM - s, moved[length - RIM :], 0.0)
        grad_ref[j] = normed_grad
        rim_grad_ref[:, at] = rim_grad
        dot_all = dot_all + normed_grad * d["x"]
        rim_dot = rim_dot + rim_grad * rim_ref[:, at]
    sums = row_sums(dot_all)
    rim_sums = jnp.broadcast_to(jnp.sum(rim_dot, axis=1, keepdims=True), rim_dot.shape)
    if chained:
        sums, rim_sums = sums + sums_in[...], rim_sums + rim_grad_in[:, channels:]
    sums_ref[...] = sums
    rim_grad_ref[:, channels:] = rim_sums
    if chained:
        rest[4][...] = rim_sums
    for copy in copies:
        copy.wait()


def finish_kernel(slots, width, flags, x_ref, go_ref, scale_ref, inner_ref, next_sums_ref, next_ref, *refs):
    grads, (out_hbm, out_ref, sems) = refs[:-3], refs[-3:]
    length = x_ref.shape[0]
    scale = down_rows(scale_ref[...])
    inner = down_rows(inner_ref[...])
    last = flags[5] == 0
    next_sums = jnp.where(last, 0.0, next_sums_ref[...])
    inner = jnp.concatenate([inner[: length - RIM], inner[length - RIM :] + next_sums], axis=0)
    cubed = scale * scale * scale * inner * (1.0 / width)
    copies = []
    places = [(ref, n) for ref in grads for n in range(ref.shape[0])]
    for j, (slot, (grad_ref, n)) in enumerate(zip(slots, places)):
        at = lane_slice(slot ^ flags[0])
        grad = grad_ref[n]
        next_grad = jnp.where(last, 0.0, next_ref[:, at])
        grad = jnp.concatenate([grad[: length - RIM], grad[length - RIM :] + next_grad], axis=0)
        total = go_ref[:, at].astype(f32) + grad * scale - x_ref[:, at].astype(f32) * cubed
        out_ref[j] = total.astype(bf16)
        copies.append(pltpu.make_async_copy(out_ref.at[j], out_hbm.at[:, at], sems.at[j]))
        copies[-1].start()
    for copy in copies:
        copy.wait()


def call(kernel, outs, *args, name=None, scratch=(), scalar=(), cost=None, far_in=False, far_out=(), unread=(), alias=None):
    spec, hbm = pl.BlockSpec(memory_space=pltpu.VMEM), pl.BlockSpec(memory_space=pltpu.HBM)
    in_specs = [hbm if far_in else spec] * len(args)
    in_specs += [pl.BlockSpec(memory_space=pl.ANY)] * len(unread)
    args = args + tuple(unread)
    aliases = {}
    if alias is not None:
        args, in_specs, aliases = args + (alias,), in_specs + [hbm], {len(args): 0}
    return pl.pallas_call(
        (lambda *refs: kernel(placed(*scalar), *refs)) if scalar else kernel,
        out_shape=list(outs),
        in_specs=in_specs,
        out_specs=[hbm if n in far_out else spec for n in range(len(outs))],
        scratch_shapes=scratch,
        input_output_aliases=aliases,
        compiler_params=pltpu.CompilerParams(vmem_limit_bytes=VMEM_LIMIT),
        cost_estimate=cost,
        name=name,
    )(*args)


BESIDE = pl.CostEstimate(flops=10**9, bytes_accessed=10**7, transcendentals=0)


def array(*shape, dtype=f32):
    return jax.ShapeDtypeStruct(shape, dtype)


def placed(per, spots):
    me = lax.axis_index("ctx")
    place, later = lax.rem(lax.shift_right_logical(me, 1), per), lax.rem(me, 2)
    row = lax.rem(lax.div(me, 2 * per), 2)
    return [later * per + place, later, place, row, me, spots - 1 - me]


def shards(inputs, out_grads, conv_weight, log_decay, beta):
    length, channels = inputs.shape
    heads = channels // HEAD_DIM
    sections, spots = lax.axis_size("section"), lax.axis_size("ctx")
    width = channels * sections
    per = heads // 2
    count = per
    slabs = spots // (2 * count)
    spot = functools.partial(call, scalar=(per, spots))

    def turned(value, sec, shift):
        route = [
            (s * spots + c, ((s + sec) % sections) * spots + (c + shift) % spots)
            for s in range(sections)
            for c in range(spots)
        ]
        return lax.ppermute(value, ("section", "ctx"), route)

    def swapped(value, distance):
        return lax.ppermute(value, "ctx", [(i, i ^ distance) for i in range(spots)])

    def moved(value, shift):
        return lax.ppermute(
            value, "ctx", [(i, i + shift) for i in range(spots) if 0 <= i + shift < spots]
        )

    payload, sums, x, go, kern, decay, rates = call(
        prelude_kernel,
        (
            array(RIM, channels + length), array(RIM, length), array(*inputs.shape, dtype=bf16),
            array(*inputs.shape, dtype=bf16), array(*conv_weight.shape), array(*inputs.shape), array(heads, length),
        ),
        *[pltpu.with_memory_space_constraint(a, pltpu.HBM) for a in (inputs, out_grads, conv_weight, log_decay, beta.T)],
        name="prelude", far_in=True, scratch=[pltpu.SemaphoreType.DMA((5,))],
    )
    total = sums
    rim_total = 0.0
    for sec in range(1, sections):
        total = total + turned(sums, sec, 0)
        rim_total = rim_total + turned(sums, sec, 1)
    rim = turned(payload, 0, 1)
    e1, e2, edge, rate = call(
        gates_kernel,
        (array(length, channels), array(length, channels), array(24, channels), array(length, channels)),
        decay, rates, name="gates", cost=BESIDE,
    )
    scale = lax.rsqrt(total / width + norm_eps)
    rim_scale = lax.rsqrt((rim_total + rim[:, channels:]) / width + norm_eps)

    shared = (x, go, kern, e1, e2, edge, rate, rim)
    tile = (HEAD_DIM, HEAD_DIM)

    def local(slots, name, unread=()):
        n = len(slots)
        return spot(
            functools.partial(local_kernel, slots),
            (array(n, 384, HEAD_DIM), array(n, WIDE, *tile), array(n, NARROW, *tile, dtype=bf16)),
            *shared, scale, rim_scale, name=name, unread=unread,
        )

    def prepared(slots, saved, name):
        n = len(slots)
        return spot(
            functools.partial(ready_kernel, slots),
            (array(n, MORE, *tile), array(n, PAIRS, *tile, dtype=bf16)),
            x, kern, e2, edge, rim, scale, rim_scale, *saved, name=name, cost=BESIDE,
        )

    inner_slots, outer_slots, rest_slots = range(1, per), range(per + 1, 2 * per), (0, per)
    some = per > 1
    parts, ahead, pairs = [None], [], ()
    if some:
        outer, *outer_saved = local(outer_slots, "local_outer")
        outer_recv = swapped(outer, 1)
        inner, *inner_saved = local(inner_slots, "local_inner")
        pairs = spot(join_kernel, (array(384, HEAD_DIM),) * (per - 1), inner, outer_recv, name="join_inner")
        parts += [swapped(pairs[n - 1], 2 * n) for n in range(1, count)]
    rest, *rest_saved = local(rest_slots, "local_rest", pairs)
    rest_recv = swapped(rest[1:], 1)
    rest = rest[:1]
    (parts[0],) = spot(join_kernel, (array(384, HEAD_DIM),), rest, rest_recv, name="join_rest")
    rest_saved += prepared(rest_slots, rest_saved, "ready_rest")
    ahead = [rest_saved[-1]]
    if some:
        outer_saved += prepared(outer_slots, outer_saved, "ready_outer")
        inner_saved += prepared(inner_slots, inner_saved, "ready_inner")
        ahead += [outer_saved[-1], inner_saved[-1]]

    held = pltpu.VMEM((count, 384, HEAD_DIM), f32)
    square = array(*tile)
    step = 2 * count

    def returned(values):
        return [values[0]] + [swapped(values[n], 2 * n) for n in range(1, count)]

    if slabs == 2 and count == 4:
        found = pltpu.VMEM((count, *tile), f32)
        total, known, products, sure = spot(
            functools.partial(two_gather_kernel, len(ahead)),
            (square, array(4, *tile), array(2, *tile), array(4, *tile)),
            *parts, name="gather", scratch=[held], unread=ahead,
        )
        other = swapped(total, step)
        reach, *early = spot(
            reach_kernel, (array(6, *tile, dtype=bf16),) + (square,) * 4,
            *parts, products, sure, name="reach", scratch=[held], cost=BESIDE,
        )
        early = returned(early)
        late = spot(late_kernel, (square,) * 4, other, known, reach, name="late", scratch=[found])
        states = list(zip(early, returned(late)))
    else:
        gathered = spot(
            functools.partial(gather_kernel, count, len(ahead)), (square,) * 3,
            *parts, name="gather", scratch=[held], unread=ahead,
        )
        ends = (jnp.zeros(tile, f32),) * 2
        for hop in range(slabs - 1):
            if hop == 0:
                ends = gathered[1:]
            else:
                ends = spot(hop_kernel, (square,) * 2, *gathered, *ends, name=f"hop{hop}")
            ends = (moved(ends[0], step), moved(ends[1], -step))
        spread = returned(
            spot(
                functools.partial(spread_kernel, count), (array(256, HEAD_DIM),) * count,
                *parts, *ends, name="spread", scratch=[held, pltpu.VMEM((count, 256, HEAD_DIM), f32)],
            )
        )
        states = [(a,) for a in spread]

    keeps, recvs = ((rest, inner), (rest_recv, outer_recv)) if some else ((rest,), (rest_recv,))
    mine, send = spot(
        functools.partial(part_kernel, len(keeps), len(states[0])), (array(per, 256, HEAD_DIM),) * 2,
        *keeps, *recvs, *(a for pair in states for a in pair), name="part",
    )
    far = swapped(send, 1)

    def backward(slots, saved, homes, states, chain, name):
        n = len(slots)
        chained = chain is not None
        before = (chain[2], chain[3]) if chained else ()
        return spot(
            functools.partial(back_kernel, slots, homes, chained),
            (
                array(*inputs.shape, dtype=bf16), array(n, length, HEAD_DIM), array(RIM, length),
                array(RIM, channels + HEAD_DIM),
            )
            + (array(RIM, HEAD_DIM),) * chained,
            *shared, states, *(a for group in saved for a in group), *before, name=name, far_out=(0,),
            alias=chain[0] if chained else None,
            scratch=[pltpu.VMEM((n, length, HEAD_DIM), bf16), pltpu.SemaphoreType.DMA((n,))],
        )

    slots = range(heads)
    homes = [[(0, n)] + [(1, i) for i in range(per - 1)] for n in range(2)]
    chain = backward(
        slots[:per], [rest_saved] + ([inner_saved] if some else []), homes[0], mine, None, "back_inner"
    )
    grads = [chain[1]]
    chain = backward(
        slots[per:], [rest_saved] + ([outer_saved] if some else []), homes[1], far, chain, "back_outer"
    )
    grads.append(chain[1])
    stream_out, _, inner_sum, rim_grad, rim_sums = chain

    inner_total, next_sums = inner_sum, 0.0
    for sec in range(1, sections):
        inner_total = inner_total + turned(inner_sum, sec, 0)
        next_sums = next_sums + turned(rim_sums, sec, -1)
    next_rim = turned(rim_grad, 0, -1)
    (input_grad,) = spot(
        functools.partial(finish_kernel, slots, width), (array(*inputs.shape, dtype=bf16),),
        x, go, scale, inner_total, next_sums + next_rim[:, channels:], next_rim, *grads, name="finish",
        far_out=(0,), scratch=[pltpu.VMEM((heads, length, HEAD_DIM), bf16), pltpu.SemaphoreType.DMA((heads,))],
    )
    return (stream_out, input_grad)


def solution(mesh):
    in_specs = (
        P("ctx", "section"),
        P("ctx", "section"),
        P(None, None, "section"),
        P("ctx", "section"),
        P("ctx", "section"),
    )
    out_specs = (P("ctx", "section"), P("ctx", "section"))
    return jax.shard_map(shards, mesh=mesh, in_specs=in_specs, out_specs=out_specs, check_vma=False)
```

```python
import functools

import jax
import jax.numpy as jnp
from jax import lax
from jax.experimental import pallas as pl
from jax.experimental.pallas import tpu as pltpu
from jax.sharding import PartitionSpec as P

HEAD_DIM = 128
RIM = 8
epsilon = 1e-06
norm_eps = 1e-05
f32 = jnp.float32
bf16 = jnp.bfloat16
VMEM_LIMIT = 24 * 1024 * 1024

DIMS = {
    "nn": (((1,), (0,)), ((), ())),
    "nt": (((1,), (1,)), ((), ())),
    "tn": (((0,), (0,)), ((), ())),
}


def split(a):
    high = a.astype(bf16)
    return high, (a - high.astype(f32)).astype(bf16)


def exact(a):
    return a, None


def rows_of(*parts):
    highs = jnp.concatenate([p[0] for p in parts], axis=0)
    lows = [jnp.zeros_like(p[0]) if p[1] is None else p[1] for p in parts]
    return highs, jnp.concatenate(lows, axis=0)


def cols_of(*parts):
    return tuple(jnp.concatenate([p[i] for p in parts], axis=1) for i in range(2))


def mm(a, b, form):
    width = b[0].shape[1]
    if form != "nt" and a[1] is not None and b[1] is not None and width == HEAD_DIM:
        right = jnp.concatenate(b, axis=1)
        left = jnp.concatenate(a, axis=0 if form == "tn" else 1)
        out = lax.dot_general(left, jnp.concatenate([right, right], axis=0), DIMS[form], preferred_element_type=f32)
        return out[:, :width] + out[:, width:]
    pairs = [(a[0], b[0])]
    if a[1] is not None:
        pairs.append((a[1], b[0]))
    if b[1] is not None:
        pairs.append((a[0], b[1]))
    left = jnp.concatenate([p[0] for p in pairs], axis=0 if form == "tn" else 1)
    right = jnp.concatenate([p[1] for p in pairs], axis=1 if form == "nt" else 0)
    return lax.dot_general(left, right, DIMS[form], preferred_element_type=f32)


def row_sums(a):
    high = a.astype(bf16)
    rest = a - high.astype(f32)
    mid = rest.astype(bf16)
    low = (rest - mid.astype(f32)).astype(bf16)
    terms = jnp.concatenate([high, mid, low], axis=1)
    ones = jnp.ones((RIM, terms.shape[1]), bf16)
    return lax.dot_general(ones, terms, DIMS["nt"], preferred_element_type=f32)


def down_rows(row):
    return jnp.transpose(jnp.broadcast_to(row[0:1], (HEAD_DIM, row.shape[1])))


def iotas(n=HEAD_DIM):
    return (
        lax.broadcasted_iota(jnp.int32, (n, n), 0),
        lax.broadcasted_iota(jnp.int32, (n, n), 1),
    )


def lane_slice(place):
    return pl.ds(pl.multiple_of(place * HEAD_DIM, HEAD_DIM), HEAD_DIM)


def prelude_kernel(
    x_hbm, go_hbm, kern_hbm, decay_hbm, beta_hbm, payload_ref, sums_ref, last_sums_ref, x_ref, go_ref, kern_ref,
    decay_ref, beta_ref, sems,
):
    pairs = ((x_hbm, x_ref), (go_hbm, go_ref), (kern_hbm, kern_ref), (decay_hbm, decay_ref), (beta_hbm, beta_ref))
    copies = [pltpu.make_async_copy(src, dst, sems.at[n]) for n, (src, dst) in enumerate(pairs)]
    for copy in copies:
        copy.start()
    copies[0].wait()
    x = x_ref[...].astype(f32)
    length, channels = x.shape
    blocks = [x[:, n : n + HEAD_DIM] for n in range(0, channels, HEAD_DIM)]
    squares = sum(block * block for block in blocks)
    sums_ref[...] = row_sums(squares)
    last = jnp.sum(squares[length - RIM :], axis=1, keepdims=True)
    last = jnp.broadcast_to(last, (RIM, HEAD_DIM))
    last_sums_ref[...] = last
    payload_ref[:, :channels] = x[length - RIM :]
    payload_ref[:, channels:] = last
    for copy in copies[1:]:
        copy.wait()


BASE = 5


def inverse_all(systems):
    row, col = iotas()
    size = 1 << BASE
    own = row >> BASE == col >> BASE
    row8 = lax.broadcasted_iota(jnp.int32, (RIM, HEAD_DIM), 0)
    col8 = lax.broadcasted_iota(jnp.int32, (RIM, HEAD_DIM), 1)
    first = (col8 >> BASE) << BASE
    found = []
    for n in systems:
        blocks = jnp.sum(jnp.where(own, n, 0.0).reshape(-1, size, HEAD_DIM), axis=0)
        tiles = [jnp.where(row8 + RIM * t == (col8 & (size - 1)), 1.0, 0.0) for t in range(size // RIM)]
        for s in range(size - 1):
            done = tiles[s // RIM][s % RIM : s % RIM + 1]
            for t in range(s // RIM, size // RIM):
                column = jnp.take_along_axis(
                    blocks[RIM * t : RIM * (t + 1)], first + s, axis=1, mode="promise_in_bounds"
                )
                tiles[t] = tiles[t] - column * done
        found.append(jnp.where(own, jnp.concatenate(tiles * (HEAD_DIM // size), axis=0), 0.0))
    level = BASE
    while (1 << level) < HEAD_DIM:
        mask = (row >> (level + 2) == col >> (level + 2)) & (row >> level != col >> level)
        parts = [split(d) for d in found]
        cross = [split(jnp.where(mask, n, 0.0)) for n in systems]
        maps = [split(mm(p, c, "nn")) for p, c in zip(parts, cross)]
        twice = [mm(m, cols_of(m, p), "nn") for m, p in zip(maps, parts)]
        less = [d - t[:, HEAD_DIM:] for d, t in zip(found, twice)]
        found = [y + mm(split(t[:, :HEAD_DIM]), split(y), "nn") for y, t in zip(less, twice)]
        level += 2
    return found


def mixes_of(normed, rim, kern):
    row8 = lax.broadcasted_iota(jnp.int32, (RIM, HEAD_DIM), 0)
    taps = kern.shape[1]
    shifted = [normed]
    for s in range(1, taps):
        moved = pltpu.roll(normed, s, 0)
        first = jnp.where(row8 < s, pltpu.roll(rim, s, 0), moved[:RIM])
        shifted.append(jnp.concatenate([first, moved[RIM:]], axis=0))
    return [
        sum(kern[j, i : i + 1] * shifted[taps - 1 - i] for i in range(taps)) for j in range(3)
    ]


def gates_kernel(width, decay_ref, beta_ref, sums_ref, e1_ref, e2_ref, edge_ref, rate_ref, scale_ref):
    scale_ref[...] = down_rows(lax.rsqrt(sums_ref[...] / width + norm_eps))
    length = decay_ref.shape[0]
    row, col = iotas()
    tril = jnp.where(row >= col, 1.0, 0.0).astype(bf16)
    tril = jnp.concatenate([tril] * 3, axis=1)
    for head in range(decay_ref.shape[1] // HEAD_DIM):
        here = slice(head * HEAD_DIM, (head + 1) * HEAD_DIM)
        decay = decay_ref[:, here]
        high = decay.astype(bf16)
        rest = decay - high.astype(f32)
        mid = rest.astype(bf16)
        low = (rest - mid.astype(f32)).astype(bf16)
        cumulative = lax.dot_general(
            tril, jnp.concatenate([high, mid, low], axis=0), DIMS["nn"], preferred_element_type=f32
        )
        middle = cumulative[length // 2 : length // 2 + 1]
        final = cumulative[length - 1 : length]
        e1_ref[:, here] = jnp.exp(cumulative - middle)
        e2_ref[:, here] = jnp.exp(middle - cumulative)
        edge_ref[0:8, here] = jnp.broadcast_to(jnp.exp(middle), (8, HEAD_DIM))
        edge_ref[8:16, here] = jnp.broadcast_to(jnp.exp(final - middle), (8, HEAD_DIM))
        edge_ref[16:24, here] = jnp.broadcast_to(jnp.exp(final), (8, HEAD_DIM))
        rate_ref[:, here] = down_rows(beta_ref[head : head + 1])


def scaled(x_ref, rim_ref, kern_ref, scale, rim_scale, at):
    x = x_ref[:, at].astype(f32)
    return mixes_of(x * scale, rim_ref[:, at] * rim_scale, kern_ref[:, :, at])


def scales(flags, scale_ref, rim_scale_ref):
    return scale_ref[...], jnp.where(flags[4] != 0, rim_scale_ref[...], 0.0)


def keep_split(ref, j, n, parts):
    ref[j, n] = parts[0]
    ref[j, n + 1] = parts[1]


def kept(ref, j, n):
    return ref[j, n], ref[j, n + 1]


def local_kernel(
    slots, flags, x_ref, go_ref, kern_ref, e1_ref, e2_ref, edge_ref, rate_ref, rim_ref, scale_ref, rim_scale_ref,
    *rest,
):
    comp_ref, wide_ref, narrow_ref = rest[-3:]
    length = x_ref.shape[0]
    row, col = iotas()
    strict, full = row > col, row >= col
    scale, rim_scale = scales(flags, scale_ref, rim_scale_ref)
    data = []
    for j, slot in enumerate(slots):
        at = lane_slice(slot ^ flags[0])
        mixes = scaled(x_ref, rim_ref, kern_ref, scale, rim_scale, at)
        act = [m / (1.0 + jnp.exp(-m)) for m in mixes]
        q, k = [a * lax.rsqrt(jnp.sum(a * a, axis=1, keepdims=True) + epsilon) for a in act[:2]]
        rate, e1, e2 = rate_ref[:, at], e1_ref[:, at], e2_ref[:, at]
        em, ecm, ef = [edge_ref[n : n + 1, at] for n in (0, 8, 16)]
        qf, kf, kb = q * e1, k * e1, k * e2
        skf, sqf, skb = split(kf), split(qf), split(kb)
        products = mm(rows_of(skf, sqf), skb, "nt")
        system = jnp.where(strict, rate * products[:length], 0.0)
        scores = split(jnp.where(full, products[length:], 0.0))
        go = exact(go_ref[:, at])
        fresh_grad = split(mm(scores, go, "tn"))
        wide_ref[j, 0], wide_ref[j, 1] = q, k
        for n, parts in enumerate((skf, sqf, skb, scores, fresh_grad)):
            keep_split(narrow_ref, j, 2 * n, parts)
        data.append(
            dict(system=system, go=go, rhs=cols_of(split(rate * kf * em), split(rate * act[2])), ke=split(kb * ecm),
                 qg=qf * em, fresh_grad=fresh_grad, ef=ef)
        )
    inverses = inverse_all([d["system"] for d in data])
    for j, (d, inverse) in enumerate(zip(data, inverses)):
        inverse = split(inverse)
        keep_split(narrow_ref, j, 14, inverse)
        solved = mm(inverse, d["rhs"], "nn")
        wide_ref[j, 2] = solved[:, HEAD_DIM:]
        d["solved"] = split(solved)
    for j, d in enumerate(data):
        solved = d["solved"]
        keep_split(narrow_ref, j, 10, (solved[0][:, :HEAD_DIM], solved[1][:, :HEAD_DIM]))
        keep_split(narrow_ref, j, 12, (solved[0][:, HEAD_DIM:], solved[1][:, HEAD_DIM:]))
        maps = mm(d["ke"], solved, "tn")
        comp_ref[j, 0:128] = jnp.where(row == col, d["ef"], 0.0) - maps[:, :HEAD_DIM]
        comp_ref[j, 128:256] = maps[:, HEAD_DIM:]
        w = (solved[0][:, :HEAD_DIM], solved[1][:, :HEAD_DIM])
        comp_ref[j, 256:384] = mm(split(d["qg"]), d["go"], "tn") - mm(w, d["fresh_grad"], "tn")


WIDE, NARROW = 3, 16


def ready_kernel(
    slots, flags, x_ref, kern_ref, e2_ref, edge_ref, rim_ref, scale_ref, rim_scale_ref, wide_ref, narrow_ref,
    more_ref, pairs_ref,
):
    scale, rim_scale = scales(flags, scale_ref, rim_scale_ref)
    for j, slot in enumerate(slots):
        at = lane_slice(slot ^ flags[0])
        mixes = scaled(x_ref, rim_ref, kern_ref, scale, rim_scale, at)
        sig = [1.0 / (1.0 + jnp.exp(-m)) for m in mixes]
        slope = [s * (1.0 + m * (1.0 - s)) for m, s in zip(mixes, sig)]
        act = [m * s for m, s in zip(mixes[:2], sig)]
        inv = [lax.rsqrt(jnp.sum(a * a, axis=1, keepdims=True) + epsilon) for a in act]
        em, ecm = edge_ref[0:1, at], edge_ref[8:9, at]
        scores, fresh_grad, inverse = [kept(narrow_ref, j, n) for n in (6, 8, 14)]
        solved = cols_of(kept(narrow_ref, j, 10), kept(narrow_ref, j, 12))
        seen = mm(scores, solved, "nn")
        ke = split(wide_ref[j, 1] * e2_ref[:, at] * ecm)
        back = mm(inverse, cols_of(fresh_grad, ke), "tn")
        more_ref[j, 0] = slope[0] * inv[0]
        more_ref[j, 1] = slope[1] * inv[1]
        more_ref[j, 2] = slope[2]
        more_ref[j, 3] = seen[:, HEAD_DIM:]
        more_ref[j, 4] = back[:, :HEAD_DIM]
        qf = narrow_ref[j, 2].astype(f32) + narrow_ref[j, 3].astype(f32)
        keep_split(pairs_ref, j, 0, split(qf * em - seen[:, :HEAD_DIM]))
        keep_split(pairs_ref, j, 2, split(back[:, HEAD_DIM:]))


MORE, PAIRS = 5, 4


def join_kernel(flags, keep_ref, recv_ref, *outs):
    later = flags[1] != 0
    outs = outs[-keep_ref.shape[0] :]
    for j, out in enumerate(outs):
        keep, recv = keep_ref[j], recv_ref[j]
        lo = jnp.where(later, recv, keep)
        hi = jnp.where(later, keep, recv)
        lo_map, hi_map = split(lo[0:128]), split(hi[0:128])
        forward = mm(hi_map, cols_of(lo_map, split(lo[128:256])), "nn")
        back = mm(lo_map, split(hi[256:384]), "tn")
        out[0:128] = forward[:, :HEAD_DIM]
        out[128:256] = forward[:, HEAD_DIM:] + hi[128:256]
        out[256:384] = back + lo[256:384]


def collect(place, parts, held):
    for n, part in enumerate(parts):
        held[place ^ n] = part[...]


def gather_kernel(count, waits, flags, *refs):
    parts, outs, held = refs[:count], refs[count + waits : -1], refs[-1]
    collect(flags[2], parts, held)
    maps = [split(held[p, 0:128]) for p in range(count)]
    state, grad = held[0, 128:256], held[count - 1, 256:384]
    whole = held[0, 0:128]
    for p in range(1, count):
        state = mm(maps[p], split(state), "nn") + held[p, 128:256]
        grad = mm(maps[count - 1 - p], split(grad), "tn") + held[count - 1 - p, 256:384]
        whole = mm(maps[p], split(whole), "nn")
    outs[0][...], outs[1][...], outs[2][...] = whole, state, grad


def hop_kernel(flags, t_ref, u_ref, g_ref, s_ref, e_ref, s_out, e_out):
    t = split(t_ref[...])
    s_out[...] = mm(t, split(s_ref[...]), "nn") + u_ref[...]
    e_out[...] = mm(t, split(e_ref[...]), "tn") + g_ref[...]


def spread_kernel(count, flags, *refs):
    parts, ins, outs, held, found = refs[:count], refs[count : -2 - count], refs[-2 - count : -2], refs[-2], refs[-1]
    collect(flags[2], parts, held)
    state, grad = ins[0][...], ins[1][...]
    for p in range(count):
        back = count - 1 - p
        found[p, 0:128] = state
        found[back, 128:256] = grad
        if p + 1 < count:
            state = mm(split(held[p, 0:128]), split(state), "nn") + held[p, 128:256]
            grad = mm(split(held[back, 0:128]), split(grad), "tn") + held[back, 256:384]
    for n, out in enumerate(outs):
        out[...] = found[flags[2] ^ n]


def two_gather_kernel(waits, flags, *refs):
    parts, outs = refs[:4], refs[4 + waits : -1]
    held = refs[-1]
    total_ref, known_ref, pairs_ref, found_ref = outs
    upper = flags[3] != 0
    collect(flags[2], parts, held)
    t = [split(held[p, 0:128]) for p in range(4)]
    u = [held[p, 128:256] for p in range(4)]
    g = [held[p, 256:384] for p in range(4)]
    last = mm(t[3], cols_of(t[2], split(u[2])), "nn")
    first = mm(t[1], cols_of(t[0], split(u[0])), "nn")
    second = first[:, HEAD_DIM:] + u[1]
    first, last, last_u = first[:, :HEAD_DIM], last[:, :HEAD_DIM], last[:, HEAD_DIM:]
    third = mm(t[2], split(g[3]), "tn") + g[2]
    low = mm(t[0], split(g[1]), "tn")
    s_second, s_third = split(second), split(third)
    forward = [jnp.zeros_like(second), u[0], second, mm(t[2], s_second, "nn") + u[2]]
    back = [mm(t[1], s_third, "tn") + g[1], third, g[3], jnp.zeros_like(third)]
    state = mm(split(last), s_second, "nn") + (last_u + u[3])
    grad = mm(split(first), s_third, "tn") + (low + g[0])
    total_ref[...] = jnp.where(upper, grad, state)
    pairs_ref[0], pairs_ref[1] = first, last
    for p in range(4):
        found_ref[p] = jnp.where(upper, back[p], forward[p])
        known_ref[p] = jnp.where(upper, forward[p], back[3 - p])


def reach_kernel(flags, *refs):
    parts, pairs_ref, found_ref, out_ref, early, held = refs[:4], refs[4], refs[5], refs[6], refs[7:11], refs[11]
    for n, out in enumerate(early):
        out[...] = found_ref[flags[2] ^ n]
    upper = flags[3] != 0
    collect(flags[2], parts, held)
    first, last = pairs_ref[0], pairs_ref[1]
    far_up = mm(split(held[2, 0:128]), split(first), "nn")
    far_down = mm(split(last), split(held[1, 0:128]), "nn")
    ups, downs = (held[0, 0:128], first, far_up), (held[3, 0:128], last, far_down)
    for n in range(3):
        high, low = split(jnp.where(upper, ups[n], jnp.transpose(downs[n])))
        out_ref[2 * n], out_ref[2 * n + 1] = high, low


def late_kernel(flags, recv_ref, known_ref, reach_ref, *refs):
    outs, found = refs[:-1], refs[-1]
    from_end = jnp.where(flags[3] != 0, 0, 3)
    recv = recv_ref[...]
    parts = split(recv)
    found[from_end] = recv
    for n in range(3):
        found[from_end ^ (n + 1)] = mm((reach_ref[2 * n], reach_ref[2 * n + 1]), parts, "nn") + known_ref[n + 1]
    for n, out in enumerate(outs):
        out[...] = found[flags[2] ^ n]


def part_kernel(sets, per_head, flags, *refs):
    maps = [(keep, recv, n) for keep, recv in zip(refs[:sets], refs[sets : 2 * sets]) for n in range(keep.shape[0])]
    ins, (mine_ref, send_ref) = refs[2 * sets : -2], refs[-2:]
    later, upper = flags[1] != 0, flags[3] != 0
    for j, (keep_ref, recv_ref, n) in enumerate(maps):
        if per_head == 1:
            start, end = ins[j][0:128], ins[j][128:256]
        else:
            early, late = ins[2 * j][...], ins[2 * j + 1][...]
            start, end = jnp.where(upper, late, early), jnp.where(upper, early, late)
        keep, recv = keep_ref[n], recv_ref[n]
        lo = jnp.where(later, recv, keep)
        hi = jnp.where(later, keep, recv)
        start_hi = mm(split(lo[0:128]), split(start), "nn") + lo[128:256]
        end_lo = mm(split(hi[0:128]), split(end), "tn") + hi[256:384]
        mine_ref[j, 0:128] = jnp.where(later, start_hi, start)
        mine_ref[j, 128:256] = jnp.where(later, end, end_lo)
        send_ref[j, 0:128] = jnp.where(later, start, start_hi)
        send_ref[j, 128:256] = jnp.where(later, end_lo, end)


def back_kernel(
    slots, homes, chained, flags, x_ref, go_ref, kern_ref, e1_ref, e2_ref, edge_ref, rate_ref, rim_ref, state_ref,
    *rest,
):
    sets = 1 + max(n for n, _ in homes)
    saved, rest = [rest[4 * n : 4 * n + 4] for n in range(sets)], rest[4 * sets :]
    if chained:
        sums_in, rim_grad_in, rest = rest[0], rest[1], rest[3:]
    out_hbm, grad_ref, sums_ref, rim_grad_ref, out_ref, sems = rest[:4] + rest[-2:]
    length = x_ref.shape[0]
    channels = x_ref.shape[1]
    row, col = iotas()
    row8 = lax.broadcasted_iota(jnp.int32, (RIM, HEAD_DIM), 0)
    strict, full = row > col, row >= col
    taps = kern_ref.shape[1]
    if chained:
        rim_grad_ref[...] = rim_grad_in[...]
    dot_all = rim_dot = 0.0
    data, copies = [], []
    for j, (slot, (n, i)) in enumerate(zip(slots, homes)):
        at = lane_slice(slot ^ flags[0])
        wide_ref, narrow_ref, more_ref, pairs_ref = saved[n]
        start, end = split(state_ref[j, 0:128]), split(state_ref[j, 128:256])
        first = mm(rows_of(kept(pairs_ref, i, 0), kept(narrow_ref, i, 10)), start, "nn")
        z = more_ref[i, 4] + mm(kept(pairs_ref, i, 2), end, "nn")
        x = x_ref[:, at].astype(f32)
        out_ref[j] = (x + (more_ref[i, 3] + first[:length])).astype(bf16)
        copies.append(pltpu.make_async_copy(out_ref.at[j], out_hbm.at[:, at], sems.at[j]))
        copies[-1].start()
        data.append(dict(at=at, x=x, start=start, end=end, z=z, fresh=split(wide_ref[i, 2] - first[length:])))
    for j, (d, (n, i)) in enumerate(zip(data, homes)):
        at = d["at"]
        wide_ref, narrow_ref, more_ref, _ = saved[n]
        q, k = wide_ref[i, 0], wide_ref[i, 1]
        gq, gk, gv = [more_ref[i, n] for n in range(3)]
        skf, sqf, skb = [kept(narrow_ref, i, n) for n in (0, 2, 4)]
        e1, e2, rate = e1_ref[:, at], e2_ref[:, at], rate_ref[:, at]
        em, ecm = edge_ref[0:1, at], edge_ref[8:9, at]
        go = exact(go_ref[:, at])
        second = mm(rows_of(go, split(d["z"])), rows_of(d["fresh"], d["start"]), "nt")
        score_grad = split(jnp.where(full, second[:length, :HEAD_DIM], 0.0))
        product_grad = split(jnp.where(strict, -rate * second[length:, :HEAD_DIM], 0.0))
        qg_grad = second[:length, HEAD_DIM:]
        kg_grad = -rate * second[length:, HEAD_DIM:]
        ke_grad = mm(d["fresh"], d["end"], "nt")
        pair = rows_of(score_grad, product_grad)
        third = mm(pair, skb, "nn")
        kb_grad = mm(pair, rows_of(sqf, skf), "tn")
        q_grad = e1 * (third[:length] + em * qg_grad)
        k_grad = e1 * (third[length:] + em * kg_grad) + e2 * (kb_grad + ecm * ke_grad)
        mix_grads = [
            gq * (q_grad - q * jnp.sum(q * q_grad, axis=1, keepdims=True)),
            gk * (k_grad - k * jnp.sum(k * k_grad, axis=1, keepdims=True)),
            gv * (rate * d["z"]),
        ]
        kern = kern_ref[:, :, at]
        normed_grad = rim_grad = 0.0
        for i in range(taps):
            each = sum(kern[n, i : i + 1] * mix_grads[n] for n in range(3))
            s = taps - 1 - i
            if s == 0:
                normed_grad = normed_grad + each
            else:
                moved = pltpu.roll(each, length - s, 0)
                normed_grad = normed_grad + jnp.where(row < length - s, moved, 0.0)
                rim_grad = rim_grad + jnp.where(row8 >= RIM - s, moved[length - RIM :], 0.0)
        grad_ref[j] = normed_grad
        rim_grad_ref[:, at] = rim_grad
        dot_all = dot_all + normed_grad * d["x"]
        rim_dot = rim_dot + rim_grad * rim_ref[:, at]
    sums = row_sums(dot_all)
    rim_sums = jnp.broadcast_to(jnp.sum(rim_dot, axis=1, keepdims=True), rim_dot.shape)
    if chained:
        sums, rim_sums = sums + sums_in[...], rim_sums + rim_grad_in[:, channels:]
    sums_ref[...] = sums
    rim_grad_ref[:, channels:] = rim_sums
    if chained:
        rest[4][...] = rim_sums
    for copy in copies:
        copy.wait()


def finish_kernel(slots, width, flags, x_ref, go_ref, scale_ref, inner_ref, next_sums_ref, next_ref, *refs):
    grads, (out_hbm, out_ref, sems) = refs[:-3], refs[-3:]
    length = x_ref.shape[0]
    scale = scale_ref[...]
    inner = down_rows(inner_ref[...])
    last = flags[5] == 0
    next_sums = jnp.where(last, 0.0, next_sums_ref[...])
    inner = jnp.concatenate([inner[: length - RIM], inner[length - RIM :] + next_sums], axis=0)
    cubed = scale * scale * scale * inner * (1.0 / width)
    copies = []
    places = [(ref, n) for ref in grads for n in range(ref.shape[0])]
    for j, (slot, (grad_ref, n)) in enumerate(zip(slots, places)):
        at = lane_slice(slot ^ flags[0])
        grad = grad_ref[n]
        next_grad = jnp.where(last, 0.0, next_ref[:, at])
        grad = jnp.concatenate([grad[: length - RIM], grad[length - RIM :] + next_grad], axis=0)
        total = go_ref[:, at].astype(f32) + grad * scale - x_ref[:, at].astype(f32) * cubed
        out_ref[j] = total.astype(bf16)
        copies.append(pltpu.make_async_copy(out_ref.at[j], out_hbm.at[:, at], sems.at[j]))
        copies[-1].start()
    for copy in copies:
        copy.wait()


def call(kernel, outs, *args, name=None, scratch=(), scalar=(), cost=None, far_in=False, far_out=(), unread=(), alias=None):
    spec, hbm = pl.BlockSpec(memory_space=pltpu.VMEM), pl.BlockSpec(memory_space=pltpu.HBM)
    in_specs = [hbm if far_in else spec] * len(args)
    in_specs += [pl.BlockSpec(memory_space=pl.ANY)] * len(unread)
    args = args + tuple(unread)
    aliases = {}
    if alias is not None:
        args, in_specs, aliases = args + (alias,), in_specs + [hbm], {len(args): 0}
    return pl.pallas_call(
        (lambda *refs: kernel(placed(*scalar), *refs)) if scalar else kernel,
        out_shape=list(outs),
        in_specs=in_specs,
        out_specs=[hbm if n in far_out else spec for n in range(len(outs))],
        scratch_shapes=scratch,
        input_output_aliases=aliases,
        compiler_params=pltpu.CompilerParams(vmem_limit_bytes=VMEM_LIMIT),
        cost_estimate=cost,
        name=name,
    )(*args)


BESIDE = pl.CostEstimate(flops=10**9, bytes_accessed=10**7, transcendentals=0)


def array(*shape, dtype=f32):
    return jax.ShapeDtypeStruct(shape, dtype)


def placed(per, spots):
    me = lax.axis_index("ctx")
    place, later = lax.rem(lax.shift_right_logical(me, 1), per), lax.rem(me, 2)
    row = lax.rem(lax.div(me, 2 * per), 2)
    return [later * per + place, later, place, row, me, spots - 1 - me]


def shards(inputs, out_grads, conv_weight, log_decay, beta):
    length, channels = inputs.shape
    heads = channels // HEAD_DIM
    sections, spots = lax.axis_size("section"), lax.axis_size("ctx")
    width = channels * sections
    per = heads // 2
    count = per
    slabs = spots // (2 * count)
    spot = functools.partial(call, scalar=(per, spots))

    def turned(value, sec, shift):
        route = [
            (s * spots + c, ((s + sec) % sections) * spots + (c + shift) % spots)
            for s in range(sections)
            for c in range(spots)
        ]
        return lax.ppermute(value, ("section", "ctx"), route)

    def swapped(value, distance):
        return lax.ppermute(value, "ctx", [(i, i ^ distance) for i in range(spots)])

    def moved(value, shift):
        return lax.ppermute(
            value, "ctx", [(i, i + shift) for i in range(spots) if 0 <= i + shift < spots]
        )

    payload, sums, last_sums, x, go, kern, decay, rates = call(
        prelude_kernel,
        (
            array(RIM, channels + HEAD_DIM), array(RIM, length), array(RIM, HEAD_DIM), array(*inputs.shape, dtype=bf16),
            array(*inputs.shape, dtype=bf16), array(*conv_weight.shape), array(*inputs.shape), array(heads, length),
        ),
        *[pltpu.with_memory_space_constraint(a, pltpu.HBM) for a in (inputs, out_grads, conv_weight, log_decay, beta.T)],
        name="prelude", far_in=True, scratch=[pltpu.SemaphoreType.DMA((5,))],
    )
    total = sums
    rim_total = 0.0
    for sec in range(1, sections):
        total = total + turned(sums, sec, 0)
        rim_total = rim_total + turned(last_sums, sec, 1)
    rim = turned(payload, 0, 1)
    e1, e2, edge, rate, scale = call(
        functools.partial(gates_kernel, width),
        (array(length, channels), array(length, channels), array(24, channels), array(length, channels),
         array(length, HEAD_DIM)),
        decay, rates, total, name="gates", cost=BESIDE,
    )
    rim_scale = lax.rsqrt((rim_total + rim[:, channels:]) / width + norm_eps)

    shared = (x, go, kern, e1, e2, edge, rate, rim)
    tile = (HEAD_DIM, HEAD_DIM)

    def local(slots, name, unread=()):
        n = len(slots)
        return spot(
            functools.partial(local_kernel, slots),
            (array(n, 384, HEAD_DIM), array(n, WIDE, *tile), array(n, NARROW, *tile, dtype=bf16)),
            *shared, scale, rim_scale, name=name, unread=unread,
        )

    def prepared(slots, saved, name):
        n = len(slots)
        return spot(
            functools.partial(ready_kernel, slots),
            (array(n, MORE, *tile), array(n, PAIRS, *tile, dtype=bf16)),
            x, kern, e2, edge, rim, scale, rim_scale, *saved, name=name, cost=BESIDE,
        )

    inner_slots, outer_slots, rest_slots = range(1, per), range(per + 1, 2 * per), (0, per)
    some = per > 1
    parts, ahead, pairs = [None], [], ()
    if some:
        outer, *outer_saved = local(outer_slots, "local_outer")
        outer_recv = swapped(outer, 1)
        inner, *inner_saved = local(inner_slots, "local_inner")
        pairs = spot(join_kernel, (array(384, HEAD_DIM),) * (per - 1), inner, outer_recv, name="join_inner")
        parts += [swapped(pairs[n - 1], 2 * n) for n in range(1, count)]
    rest, *rest_saved = local(rest_slots, "local_rest", pairs)
    rest_recv = swapped(rest[1:], 1)
    rest = rest[:1]
    (parts[0],) = spot(join_kernel, (array(384, HEAD_DIM),), rest, rest_recv, name="join_rest")
    rest_saved += prepared(rest_slots, rest_saved, "ready_rest")
    ahead = [rest_saved[-1]]
    if some:
        outer_saved += prepared(outer_slots, outer_saved, "ready_outer")
        inner_saved += prepared(inner_slots, inner_saved, "ready_inner")
        ahead += [outer_saved[-1], inner_saved[-1]]

    held = pltpu.VMEM((count, 384, HEAD_DIM), f32)
    square = array(*tile)
    step = 2 * count

    def returned(values):
        return [values[0]] + [swapped(values[n], 2 * n) for n in range(1, count)]

    if slabs == 2 and count == 4:
        found = pltpu.VMEM((count, *tile), f32)
        total, known, products, sure = spot(
            functools.partial(two_gather_kernel, len(ahead)),
            (square, array(4, *tile), array(2, *tile), array(4, *tile)),
            *parts, name="gather", scratch=[held], unread=ahead,
        )
        other = swapped(total, step)
        reach, *early = spot(
            reach_kernel, (array(6, *tile, dtype=bf16),) + (square,) * 4,
            *parts, products, sure, name="reach", scratch=[held], cost=BESIDE,
        )
        early = returned(early)
        late = spot(late_kernel, (square,) * 4, other, known, reach, name="late", scratch=[found])
        states = list(zip(early, returned(late)))
    else:
        gathered = spot(
            functools.partial(gather_kernel, count, len(ahead)), (square,) * 3,
            *parts, name="gather", scratch=[held], unread=ahead,
        )
        ends = (jnp.zeros(tile, f32),) * 2
        for hop in range(slabs - 1):
            if hop == 0:
                ends = gathered[1:]
            else:
                ends = spot(hop_kernel, (square,) * 2, *gathered, *ends, name=f"hop{hop}")
            ends = (moved(ends[0], step), moved(ends[1], -step))
        spread = returned(
            spot(
                functools.partial(spread_kernel, count), (array(256, HEAD_DIM),) * count,
                *parts, *ends, name="spread", scratch=[held, pltpu.VMEM((count, 256, HEAD_DIM), f32)],
            )
        )
        states = [(a,) for a in spread]

    keeps, recvs = ((rest, inner), (rest_recv, outer_recv)) if some else ((rest,), (rest_recv,))
    mine, send = spot(
        functools.partial(part_kernel, len(keeps), len(states[0])), (array(per, 256, HEAD_DIM),) * 2,
        *keeps, *recvs, *(a for pair in states for a in pair), name="part",
    )
    far = swapped(send, 1)

    def backward(slots, saved, homes, states, chain, name):
        n = len(slots)
        chained = chain is not None
        before = (chain[2], chain[3]) if chained else ()
        return spot(
            functools.partial(back_kernel, slots, homes, chained),
            (
                array(*inputs.shape, dtype=bf16), array(n, length, HEAD_DIM), array(RIM, length),
                array(RIM, channels + HEAD_DIM),
            )
            + (array(RIM, HEAD_DIM),) * chained,
            *shared, states, *(a for group in saved for a in group), *before, name=name, far_out=(0,),
            alias=chain[0] if chained else None,
            scratch=[pltpu.VMEM((n, length, HEAD_DIM), bf16), pltpu.SemaphoreType.DMA((n,))],
        )

    slots = range(heads)
    homes = [[(0, n)] + [(1, i) for i in range(per - 1)] for n in range(2)]
    chain = backward(
        slots[:per], [rest_saved] + ([inner_saved] if some else []), homes[0], mine, None, "back_inner"
    )
    grads = [chain[1]]
    chain = backward(
        slots[per:], [rest_saved] + ([outer_saved] if some else []), homes[1], far, chain, "back_outer"
    )
    grads.append(chain[1])
    stream_out, _, inner_sum, rim_grad, rim_sums = chain

    inner_total, next_sums = inner_sum, 0.0
    for sec in range(1, sections):
        inner_total = inner_total + turned(inner_sum, sec, 0)
        next_sums = next_sums + turned(rim_sums, sec, -1)
    next_rim = turned(rim_grad, 0, -1)
    (input_grad,) = spot(
        functools.partial(finish_kernel, slots, width), (array(*inputs.shape, dtype=bf16),),
        x, go, scale, inner_total, next_sums + next_rim[:, channels:], next_rim, *grads, name="finish",
        far_out=(0,), scratch=[pltpu.VMEM((heads, length, HEAD_DIM), bf16), pltpu.SemaphoreType.DMA((heads,))],
    )
    return (stream_out, input_grad)


def solution(mesh):
    in_specs = (
        P("ctx", "section"),
        P("ctx", "section"),
        P(None, None, "section"),
        P("ctx", "section"),
        P("ctx", "section"),
    )
    out_specs = (P("ctx", "section"), P("ctx", "section"))
    return jax.shard_map(shards, mesh=mesh, in_specs=in_specs, out_specs=out_specs, check_vma=False)
```

```python
import functools

import jax
import jax.numpy as jnp
from jax import lax
from jax.experimental import pallas as pl
from jax.experimental.pallas import tpu as pltpu
from jax.sharding import PartitionSpec as P

HEAD_DIM = 128
RIM = 8
epsilon = 1e-06
norm_eps = 1e-05
f32 = jnp.float32
bf16 = jnp.bfloat16
VMEM_LIMIT = 24 * 1024 * 1024

DIMS = {
    "nn": (((1,), (0,)), ((), ())),
    "nt": (((1,), (1,)), ((), ())),
    "tn": (((0,), (0,)), ((), ())),
}


def split(a):
    high = a.astype(bf16)
    return high, (a - high.astype(f32)).astype(bf16)


def exact(a):
    return a, None


def rows_of(*parts):
    highs = jnp.concatenate([p[0] for p in parts], axis=0)
    lows = [jnp.zeros_like(p[0]) if p[1] is None else p[1] for p in parts]
    return highs, jnp.concatenate(lows, axis=0)


def cols_of(*parts):
    return tuple(jnp.concatenate([p[i] for p in parts], axis=1) for i in range(2))


def mm(a, b, form):
    width = b[0].shape[1]
    if form != "nt" and a[1] is not None and b[1] is not None and width == HEAD_DIM:
        right = jnp.concatenate(b, axis=1)
        left = jnp.concatenate(a, axis=0 if form == "tn" else 1)
        out = lax.dot_general(left, jnp.concatenate([right, right], axis=0), DIMS[form], preferred_element_type=f32)
        return out[:, :width] + out[:, width:]
    pairs = [(a[0], b[0])]
    if a[1] is not None:
        pairs.append((a[1], b[0]))
    if b[1] is not None:
        pairs.append((a[0], b[1]))
    left = jnp.concatenate([p[0] for p in pairs], axis=0 if form == "tn" else 1)
    right = jnp.concatenate([p[1] for p in pairs], axis=1 if form == "nt" else 0)
    return lax.dot_general(left, right, DIMS[form], preferred_element_type=f32)


def row_sums(a):
    high = a.astype(bf16)
    rest = a - high.astype(f32)
    mid = rest.astype(bf16)
    low = (rest - mid.astype(f32)).astype(bf16)
    terms = jnp.concatenate([high, mid, low], axis=1)
    ones = jnp.ones((RIM, terms.shape[1]), bf16)
    return lax.dot_general(ones, terms, DIMS["nt"], preferred_element_type=f32)


def down_rows(row):
    return jnp.transpose(jnp.broadcast_to(row[0:1], (HEAD_DIM, row.shape[1])))


def iotas(n=HEAD_DIM):
    return (
        lax.broadcasted_iota(jnp.int32, (n, n), 0),
        lax.broadcasted_iota(jnp.int32, (n, n), 1),
    )


def lane_slice(place):
    return pl.ds(pl.multiple_of(place * HEAD_DIM, HEAD_DIM), HEAD_DIM)


def prelude_kernel(
    x_hbm, go_hbm, kern_hbm, decay_hbm, beta_hbm, payload_ref, sums_ref, last_sums_ref, x_ref, go_ref, kern_ref,
    decay_ref, beta_ref, sems,
):
    pairs = ((x_hbm, x_ref), (go_hbm, go_ref), (kern_hbm, kern_ref), (decay_hbm, decay_ref), (beta_hbm, beta_ref))
    copies = [pltpu.make_async_copy(src, dst, sems.at[n]) for n, (src, dst) in enumerate(pairs)]
    for copy in copies:
        copy.start()
    copies[0].wait()
    x = x_ref[...].astype(f32)
    length, channels = x.shape
    blocks = [x[:, n : n + HEAD_DIM] for n in range(0, channels, HEAD_DIM)]
    squares = sum(block * block for block in blocks)
    sums_ref[...] = row_sums(squares)
    last = jnp.sum(squares[length - RIM :], axis=1, keepdims=True)
    last = jnp.broadcast_to(last, (RIM, HEAD_DIM))
    last_sums_ref[...] = last
    payload_ref[:, :channels] = x[length - RIM :]
    payload_ref[:, channels:] = last
    for copy in copies[1:]:
        copy.wait()


BASE = 5


def inverse_all(systems):
    row, col = iotas()
    size = 1 << BASE
    own = row >> BASE == col >> BASE
    row8 = lax.broadcasted_iota(jnp.int32, (RIM, HEAD_DIM), 0)
    col8 = lax.broadcasted_iota(jnp.int32, (RIM, HEAD_DIM), 1)
    first = (col8 >> BASE) << BASE
    found = []
    for n in systems:
        blocks = jnp.sum(jnp.where(own, n, 0.0).reshape(-1, size, HEAD_DIM), axis=0)
        tiles = [jnp.where(row8 + RIM * t == (col8 & (size - 1)), 1.0, 0.0) for t in range(size // RIM)]
        for s in range(size - 1):
            done = tiles[s // RIM][s % RIM : s % RIM + 1]
            for t in range(s // RIM, size // RIM):
                column = jnp.take_along_axis(
                    blocks[RIM * t : RIM * (t + 1)], first + s, axis=1, mode="promise_in_bounds"
                )
                tiles[t] = tiles[t] - column * done
        found.append(jnp.where(own, jnp.concatenate(tiles * (HEAD_DIM // size), axis=0), 0.0))
    level = BASE
    while (1 << level) < HEAD_DIM:
        mask = (row >> (level + 2) == col >> (level + 2)) & (row >> level != col >> level)
        parts = [split(d) for d in found]
        cross = [split(jnp.where(mask, n, 0.0)) for n in systems]
        maps = [split(mm(p, c, "nn")) for p, c in zip(parts, cross)]
        twice = [mm(m, cols_of(m, p), "nn") for m, p in zip(maps, parts)]
        less = [d - t[:, HEAD_DIM:] for d, t in zip(found, twice)]
        found = [y + mm(split(t[:, :HEAD_DIM]), split(y), "nn") for y, t in zip(less, twice)]
        level += 2
    return found


def mixes_of(normed, rim, kern):
    row8 = lax.broadcasted_iota(jnp.int32, (RIM, HEAD_DIM), 0)
    taps = kern.shape[1]
    shifted = [normed]
    for s in range(1, taps):
        moved = pltpu.roll(normed, s, 0)
        first = jnp.where(row8 < s, pltpu.roll(rim, s, 0), moved[:RIM])
        shifted.append(jnp.concatenate([first, moved[RIM:]], axis=0))
    return [
        sum(kern[j, i : i + 1] * shifted[taps - 1 - i] for i in range(taps)) for j in range(3)
    ]


def gates_kernel(width, decay_ref, beta_ref, sums_ref, e1_ref, e2_ref, edge_ref, rate_ref, scale_ref):
    scale_ref[...] = down_rows(lax.rsqrt(sums_ref[...] / width + norm_eps))
    length = decay_ref.shape[0]
    row, col = iotas()
    tril = jnp.where(row >= col, 1.0, 0.0).astype(bf16)
    tril = jnp.concatenate([tril] * 3, axis=1)
    for head in range(decay_ref.shape[1] // HEAD_DIM):
        here = slice(head * HEAD_DIM, (head + 1) * HEAD_DIM)
        decay = decay_ref[:, here]
        high = decay.astype(bf16)
        rest = decay - high.astype(f32)
        mid = rest.astype(bf16)
        low = (rest - mid.astype(f32)).astype(bf16)
        cumulative = lax.dot_general(
            tril, jnp.concatenate([high, mid, low], axis=0), DIMS["nn"], preferred_element_type=f32
        )
        middle = cumulative[length // 2 : length // 2 + 1]
        final = cumulative[length - 1 : length]
        e1_ref[:, here] = jnp.exp(cumulative - middle)
        e2_ref[:, here] = jnp.exp(middle - cumulative)
        edge_ref[0:8, here] = jnp.broadcast_to(jnp.exp(middle), (8, HEAD_DIM))
        edge_ref[8:16, here] = jnp.broadcast_to(jnp.exp(final - middle), (8, HEAD_DIM))
        edge_ref[16:24, here] = jnp.broadcast_to(jnp.exp(final), (8, HEAD_DIM))
        rate_ref[:, here] = down_rows(beta_ref[head : head + 1])


def scaled(x_ref, rim_ref, kern_ref, scale, rim_scale, at):
    x = x_ref[:, at].astype(f32)
    return mixes_of(x * scale, rim_ref[:, at] * rim_scale, kern_ref[:, :, at])


def scales(flags, scale_ref, rim_scale_ref):
    return scale_ref[...], jnp.where(flags[4] != 0, rim_scale_ref[...], 0.0)


def keep_split(ref, j, n, parts):
    ref[j, n] = parts[0]
    ref[j, n + 1] = parts[1]


def kept(ref, j, n):
    return ref[j, n], ref[j, n + 1]


def local_kernel(
    slots, flags, x_ref, go_ref, kern_ref, e1_ref, e2_ref, edge_ref, rate_ref, rim_ref, scale_ref, rim_scale_ref,
    *rest,
):
    comp_ref, wide_ref, narrow_ref = rest[-3:]
    length = x_ref.shape[0]
    row, col = iotas()
    strict, full = row > col, row >= col
    scale, rim_scale = scales(flags, scale_ref, rim_scale_ref)
    data = []
    for j, slot in enumerate(slots):
        at = lane_slice(slot ^ flags[0])
        mixes = scaled(x_ref, rim_ref, kern_ref, scale, rim_scale, at)
        act = [m / (1.0 + jnp.exp(-m)) for m in mixes]
        q, k = [a * lax.rsqrt(jnp.sum(a * a, axis=1, keepdims=True) + epsilon) for a in act[:2]]
        rate, e1, e2 = rate_ref[:, at], e1_ref[:, at], e2_ref[:, at]
        em, ecm, ef = [edge_ref[n : n + 1, at] for n in (0, 8, 16)]
        qf, kf, kb = q * e1, k * e1, k * e2
        skf, sqf, skb = split(kf), split(qf), split(kb)
        products = mm(rows_of(skf, sqf), skb, "nt")
        system = jnp.where(strict, rate * products[:length], 0.0)
        scores = split(jnp.where(full, products[length:], 0.0))
        go = exact(go_ref[:, at])
        fresh_grad = split(mm(scores, go, "tn"))
        wide_ref[j, 0], wide_ref[j, 1] = q, k
        for n, parts in enumerate((skf, sqf, skb, scores, fresh_grad)):
            keep_split(narrow_ref, j, 2 * n, parts)
        data.append(
            dict(system=system, go=go, rhs=cols_of(split(rate * kf * em), split(rate * act[2])), ke=split(kb * ecm),
                 qg=qf * em, fresh_grad=fresh_grad, ef=ef)
        )
    inverses = inverse_all([d["system"] for d in data])
    for j, (d, inverse) in enumerate(zip(data, inverses)):
        inverse = split(inverse)
        keep_split(narrow_ref, j, 14, inverse)
        solved = mm(inverse, d["rhs"], "nn")
        wide_ref[j, 2] = solved[:, HEAD_DIM:]
        d["solved"] = split(solved)
    for j, d in enumerate(data):
        solved = d["solved"]
        keep_split(narrow_ref, j, 10, (solved[0][:, :HEAD_DIM], solved[1][:, :HEAD_DIM]))
        keep_split(narrow_ref, j, 12, (solved[0][:, HEAD_DIM:], solved[1][:, HEAD_DIM:]))
        maps = mm(d["ke"], solved, "tn")
        comp_ref[j, 0:128] = jnp.where(row == col, d["ef"], 0.0) - maps[:, :HEAD_DIM]
        comp_ref[j, 128:256] = maps[:, HEAD_DIM:]
        w = (solved[0][:, :HEAD_DIM], solved[1][:, :HEAD_DIM])
        comp_ref[j, 256:384] = mm(split(d["qg"]), d["go"], "tn") - mm(w, d["fresh_grad"], "tn")


WIDE, NARROW = 3, 16


def ready_kernel(
    slots, flags, x_ref, kern_ref, e2_ref, edge_ref, rim_ref, scale_ref, rim_scale_ref, wide_ref, narrow_ref,
    more_ref, pairs_ref,
):
    scale, rim_scale = scales(flags, scale_ref, rim_scale_ref)
    for j, slot in enumerate(slots):
        at = lane_slice(slot ^ flags[0])
        mixes = scaled(x_ref, rim_ref, kern_ref, scale, rim_scale, at)
        sig = [1.0 / (1.0 + jnp.exp(-m)) for m in mixes]
        slope = [s * (1.0 + m * (1.0 - s)) for m, s in zip(mixes, sig)]
        act = [m * s for m, s in zip(mixes[:2], sig)]
        inv = [lax.rsqrt(jnp.sum(a * a, axis=1, keepdims=True) + epsilon) for a in act]
        em, ecm = edge_ref[0:1, at], edge_ref[8:9, at]
        scores, fresh_grad, inverse = [kept(narrow_ref, j, n) for n in (6, 8, 14)]
        solved = cols_of(kept(narrow_ref, j, 10), kept(narrow_ref, j, 12))
        seen = mm(scores, solved, "nn")
        ke = split(wide_ref[j, 1] * e2_ref[:, at] * ecm)
        back = mm(inverse, cols_of(fresh_grad, ke), "tn")
        more_ref[j, 0] = slope[0] * inv[0]
        more_ref[j, 1] = slope[1] * inv[1]
        more_ref[j, 2] = slope[2]
        more_ref[j, 3] = seen[:, HEAD_DIM:]
        more_ref[j, 4] = back[:, :HEAD_DIM]
        qf = narrow_ref[j, 2].astype(f32) + narrow_ref[j, 3].astype(f32)
        keep_split(pairs_ref, j, 0, split(qf * em - seen[:, :HEAD_DIM]))
        keep_split(pairs_ref, j, 2, split(back[:, HEAD_DIM:]))


MORE, PAIRS = 5, 4


def join_kernel(flags, keep_ref, recv_ref, *outs):
    later, upper = flags[1] != 0, flags[3] != 0
    heads = keep_ref.shape[0]
    for j in range(heads):
        keep, recv = keep_ref[j], recv_ref[j]
        lo = jnp.where(later, recv, keep)
        hi = jnp.where(later, keep, recv)
        lo_map, hi_map = split(lo[0:128]), split(hi[0:128])
        forward = mm(hi_map, cols_of(lo_map, split(lo[128:256])), "nn")
        grad = mm(lo_map, split(hi[256:384]), "tn") + lo[256:384]
        state = forward[:, HEAD_DIM:] + hi[128:256]
        out = outs[j]
        out[0:128] = forward[:, :HEAD_DIM]
        if len(outs) == heads:
            out[128:256], out[256:384] = state, grad
        else:
            out[128:256] = jnp.where(upper, grad, state)
            outs[heads + j][...] = jnp.where(upper, state, grad)


def collect(place, parts, held):
    for n, part in enumerate(parts):
        held[place ^ n] = part[...]


def gather_kernel(count, waits, flags, *refs):
    parts, outs, held = refs[:count], refs[count + waits : -1], refs[-1]
    collect(flags[2], parts, held)
    maps = [split(held[p, 0:128]) for p in range(count)]
    state, grad = held[0, 128:256], held[count - 1, 256:384]
    whole = held[0, 0:128]
    for p in range(1, count):
        state = mm(maps[p], split(state), "nn") + held[p, 128:256]
        grad = mm(maps[count - 1 - p], split(grad), "tn") + held[count - 1 - p, 256:384]
        whole = mm(maps[p], split(whole), "nn")
    outs[0][...], outs[1][...], outs[2][...] = whole, state, grad


def hop_kernel(flags, t_ref, u_ref, g_ref, s_ref, e_ref, s_out, e_out):
    t = split(t_ref[...])
    s_out[...] = mm(t, split(s_ref[...]), "nn") + u_ref[...]
    e_out[...] = mm(t, split(e_ref[...]), "tn") + g_ref[...]


def spread_kernel(count, flags, *refs):
    parts, ins, outs, held, found = refs[:count], refs[count : -2 - count], refs[-2 - count : -2], refs[-2], refs[-1]
    collect(flags[2], parts, held)
    state, grad = ins[0][...], ins[1][...]
    for p in range(count):
        back = count - 1 - p
        found[p, 0:128] = state
        found[back, 128:256] = grad
        if p + 1 < count:
            state = mm(split(held[p, 0:128]), split(state), "nn") + held[p, 128:256]
            grad = mm(split(held[back, 0:128]), split(grad), "tn") + held[back, 256:384]
    for n, out in enumerate(outs):
        out[...] = found[flags[2] ^ n]


def two_gather_kernel(waits, flags, *refs):
    parts, outs = refs[:4], refs[4 + waits : -1]
    held = refs[-1]
    total_ref, pairs_ref, found_ref = outs
    upper = flags[3] != 0
    collect(flags[2], parts, held)
    t = [split(held[p, 0:128]) for p in range(4)]
    u = [held[p, 128:256] for p in range(4)]
    su = [split(a) for a in u]
    last = mm(t[3], cols_of(t[2], su[2]), "nn")
    first = mm(t[1], cols_of(t[0], su[0]), "nn")
    second = first[:, HEAD_DIM:] + u[1]
    first, last, last_u = first[:, :HEAD_DIM], last[:, :HEAD_DIM], last[:, HEAD_DIM:]
    third = mm(t[2], su[3], "tn") + u[2]
    low = mm(t[0], su[1], "tn")
    s_second, s_third = split(second), split(third)
    forward = [jnp.zeros_like(second), u[0], second, mm(t[2], s_second, "nn") + u[2]]
    back = [mm(t[1], s_third, "tn") + u[1], third, u[3], jnp.zeros_like(third)]
    state = mm(split(last), s_second, "nn") + (last_u + u[3])
    grad = mm(split(first), s_third, "tn") + (low + u[0])
    total_ref[...] = jnp.where(upper, grad, state)
    pairs_ref[0], pairs_ref[1] = first, last
    for p in range(4):
        found_ref[p] = jnp.where(upper, back[p], forward[p])


def known_kernel(flags, *refs):
    parts, others, known_ref, held, values = refs[:4], refs[4:8], refs[8], refs[9], refs[10]
    upper = flags[3] != 0
    collect(flags[2], parts, held)
    collect(flags[2], others, values)
    t = [split(held[p, 0:128]) for p in (1, 2)]
    second = mm(t[0], split(values[0]), "nn") + values[1]
    third = mm(t[1], split(second), "nn") + values[2]
    below = mm(t[1], split(values[3]), "tn") + values[2]
    lowest = mm(t[0], split(below), "tn") + values[1]
    for n, (up, down) in enumerate(((values[0], values[3]), (second, below), (third, lowest))):
        known_ref[n + 1] = jnp.where(upper, up, down)
    known_ref[0] = jnp.zeros_like(second)


def reach_kernel(flags, *refs):
    parts, pairs_ref, found_ref, out_ref, early, held = refs[:4], refs[4], refs[5], refs[6], refs[7:11], refs[11]
    for n, out in enumerate(early):
        out[...] = found_ref[flags[2] ^ n]
    upper = flags[3] != 0
    collect(flags[2], parts, held)
    first, last = pairs_ref[0], pairs_ref[1]
    far_up = mm(split(held[2, 0:128]), split(first), "nn")
    far_down = mm(split(last), split(held[1, 0:128]), "nn")
    ups, downs = (held[0, 0:128], first, far_up), (held[3, 0:128], last, far_down)
    for n in range(3):
        high, low = split(jnp.where(upper, ups[n], jnp.transpose(downs[n])))
        out_ref[2 * n], out_ref[2 * n + 1] = high, low


def late_kernel(flags, recv_ref, known_ref, reach_ref, *refs):
    outs, found = refs[:-1], refs[-1]
    from_end = jnp.where(flags[3] != 0, 0, 3)
    recv = recv_ref[...]
    parts = split(recv)
    found[from_end] = recv
    for n in range(3):
        found[from_end ^ (n + 1)] = mm((reach_ref[2 * n], reach_ref[2 * n + 1]), parts, "nn") + known_ref[n + 1]
    for n, out in enumerate(outs):
        out[...] = found[flags[2] ^ n]


def part_kernel(sets, per_head, flags, *refs):
    maps = [(keep, recv, n) for keep, recv in zip(refs[:sets], refs[sets : 2 * sets]) for n in range(keep.shape[0])]
    ins, (mine_ref, send_ref) = refs[2 * sets : -2], refs[-2:]
    later, upper = flags[1] != 0, flags[3] != 0
    for j, (keep_ref, recv_ref, n) in enumerate(maps):
        if per_head == 1:
            start, end = ins[j][0:128], ins[j][128:256]
        else:
            early, late = ins[2 * j][...], ins[2 * j + 1][...]
            start, end = jnp.where(upper, late, early), jnp.where(upper, early, late)
        keep, recv = keep_ref[n], recv_ref[n]
        lo = jnp.where(later, recv, keep)
        hi = jnp.where(later, keep, recv)
        start_hi = mm(split(lo[0:128]), split(start), "nn") + lo[128:256]
        end_lo = mm(split(hi[0:128]), split(end), "tn") + hi[256:384]
        mine_ref[j, 0:128] = jnp.where(later, start_hi, start)
        mine_ref[j, 128:256] = jnp.where(later, end, end_lo)
        send_ref[j, 0:128] = jnp.where(later, start, start_hi)
        send_ref[j, 128:256] = jnp.where(later, end_lo, end)


def back_kernel(
    slots, homes, chained, flags, x_ref, go_ref, kern_ref, e1_ref, e2_ref, edge_ref, rate_ref, rim_ref, state_ref,
    *rest,
):
    sets = 1 + max(n for n, _ in homes)
    saved, rest = [rest[4 * n : 4 * n + 4] for n in range(sets)], rest[4 * sets :]
    if chained:
        sums_in, rim_grad_in, rest = rest[0], rest[1], rest[3:]
    out_hbm, grad_ref, sums_ref, rim_grad_ref, out_ref, sems = rest[:4] + rest[-2:]
    length = x_ref.shape[0]
    channels = x_ref.shape[1]
    row, col = iotas()
    row8 = lax.broadcasted_iota(jnp.int32, (RIM, HEAD_DIM), 0)
    strict, full = row > col, row >= col
    taps = kern_ref.shape[1]
    if chained:
        rim_grad_ref[...] = rim_grad_in[...]
    dot_all = rim_dot = 0.0
    data, copies = [], []
    for j, (slot, (n, i)) in enumerate(zip(slots, homes)):
        at = lane_slice(slot ^ flags[0])
        wide_ref, narrow_ref, more_ref, pairs_ref = saved[n]
        start, end = split(state_ref[j, 0:128]), split(state_ref[j, 128:256])
        first = mm(rows_of(kept(pairs_ref, i, 0), kept(narrow_ref, i, 10)), start, "nn")
        z = more_ref[i, 4] + mm(kept(pairs_ref, i, 2), end, "nn")
        x = x_ref[:, at].astype(f32)
        out_ref[j] = (x + (more_ref[i, 3] + first[:length])).astype(bf16)
        copies.append(pltpu.make_async_copy(out_ref.at[j], out_hbm.at[:, at], sems.at[j]))
        copies[-1].start()
        data.append(dict(at=at, x=x, start=start, end=end, z=z, fresh=split(wide_ref[i, 2] - first[length:])))
    for j, (d, (n, i)) in enumerate(zip(data, homes)):
        at = d["at"]
        wide_ref, narrow_ref, more_ref, _ = saved[n]
        q, k = wide_ref[i, 0], wide_ref[i, 1]
        gq, gk, gv = [more_ref[i, n] for n in range(3)]
        skf, sqf, skb = [kept(narrow_ref, i, n) for n in (0, 2, 4)]
        e1, e2, rate = e1_ref[:, at], e2_ref[:, at], rate_ref[:, at]
        em, ecm = edge_ref[0:1, at], edge_ref[8:9, at]
        go = exact(go_ref[:, at])
        second = mm(rows_of(go, split(d["z"])), rows_of(d["fresh"], d["start"]), "nt")
        score_grad = split(jnp.where(full, second[:length, :HEAD_DIM], 0.0))
        product_grad = split(jnp.where(strict, -rate * second[length:, :HEAD_DIM], 0.0))
        qg_grad = second[:length, HEAD_DIM:]
        kg_grad = -rate * second[length:, HEAD_DIM:]
        ke_grad = mm(d["fresh"], d["end"], "nt")
        pair = rows_of(score_grad, product_grad)
        third = mm(pair, skb, "nn")
        kb_grad = mm(pair, rows_of(sqf, skf), "tn")
        q_grad = e1 * (third[:length] + em * qg_grad)
        k_grad = e1 * (third[length:] + em * kg_grad) + e2 * (kb_grad + ecm * ke_grad)
        mix_grads = [
            gq * (q_grad - q * jnp.sum(q * q_grad, axis=1, keepdims=True)),
            gk * (k_grad - k * jnp.sum(k * k_grad, axis=1, keepdims=True)),
            gv * (rate * d["z"]),
        ]
        kern = kern_ref[:, :, at]
        normed_grad = rim_grad = 0.0
        for i in range(taps):
            each = sum(kern[n, i : i + 1] * mix_grads[n] for n in range(3))
            s = taps - 1 - i
            if s == 0:
                normed_grad = normed_grad + each
            else:
                moved = pltpu.roll(each, length - s, 0)
                normed_grad = normed_grad + jnp.where(row < length - s, moved, 0.0)
                rim_grad = rim_grad + jnp.where(row8 >= RIM - s, moved[length - RIM :], 0.0)
        grad_ref[j] = normed_grad
        rim_grad_ref[:, at] = rim_grad
        dot_all = dot_all + normed_grad * d["x"]
        rim_dot = rim_dot + rim_grad * rim_ref[:, at]
    sums = row_sums(dot_all)
    rim_sums = jnp.broadcast_to(jnp.sum(rim_dot, axis=1, keepdims=True), rim_dot.shape)
    if chained:
        sums, rim_sums = sums + sums_in[...], rim_sums + rim_grad_in[:, channels:]
    sums_ref[...] = sums
    rim_grad_ref[:, channels:] = rim_sums
    if chained:
        rest[4][...] = rim_sums
    for copy in copies:
        copy.wait()


def finish_kernel(slots, width, flags, x_ref, go_ref, scale_ref, inner_ref, next_sums_ref, next_ref, *refs):
    grads, (out_hbm, out_ref, sems) = refs[:-3], refs[-3:]
    length = x_ref.shape[0]
    scale = scale_ref[...]
    inner = down_rows(inner_ref[...])
    last = flags[5] == 0
    next_sums = jnp.where(last, 0.0, next_sums_ref[...])
    inner = jnp.concatenate([inner[: length - RIM], inner[length - RIM :] + next_sums], axis=0)
    cubed = scale * scale * scale * inner * (1.0 / width)
    copies = []
    places = [(ref, n) for ref in grads for n in range(ref.shape[0])]
    for j, (slot, (grad_ref, n)) in enumerate(zip(slots, places)):
        at = lane_slice(slot ^ flags[0])
        grad = grad_ref[n]
        next_grad = jnp.where(last, 0.0, next_ref[:, at])
        grad = jnp.concatenate([grad[: length - RIM], grad[length - RIM :] + next_grad], axis=0)
        total = go_ref[:, at].astype(f32) + grad * scale - x_ref[:, at].astype(f32) * cubed
        out_ref[j] = total.astype(bf16)
        copies.append(pltpu.make_async_copy(out_ref.at[j], out_hbm.at[:, at], sems.at[j]))
        copies[-1].start()
    for copy in copies:
        copy.wait()


def call(kernel, outs, *args, name=None, scratch=(), scalar=(), cost=None, far_in=False, far_out=(), unread=(), alias=None):
    spec, hbm = pl.BlockSpec(memory_space=pltpu.VMEM), pl.BlockSpec(memory_space=pltpu.HBM)
    in_specs = [hbm if far_in else spec] * len(args)
    in_specs += [pl.BlockSpec(memory_space=pl.ANY)] * len(unread)
    args = args + tuple(unread)
    aliases = {}
    if alias is not None:
        args, in_specs, aliases = args + (alias,), in_specs + [hbm], {len(args): 0}
    return pl.pallas_call(
        (lambda *refs: kernel(placed(*scalar), *refs)) if scalar else kernel,
        out_shape=list(outs),
        in_specs=in_specs,
        out_specs=[hbm if n in far_out else spec for n in range(len(outs))],
        scratch_shapes=scratch,
        input_output_aliases=aliases,
        compiler_params=pltpu.CompilerParams(vmem_limit_bytes=VMEM_LIMIT),
        cost_estimate=cost,
        name=name,
    )(*args)


BESIDE = pl.CostEstimate(flops=0, bytes_accessed=0, transcendentals=0)


def array(*shape, dtype=f32):
    return jax.ShapeDtypeStruct(shape, dtype)


def placed(per, spots):
    me = lax.axis_index("ctx")
    place, later = lax.rem(lax.shift_right_logical(me, 1), per), lax.rem(me, 2)
    row = lax.rem(lax.div(me, 2 * per), 2)
    return [later * per + place, later, place, row, me, spots - 1 - me]


def shards(inputs, out_grads, conv_weight, log_decay, beta):
    length, channels = inputs.shape
    heads = channels // HEAD_DIM
    sections, spots = lax.axis_size("section"), lax.axis_size("ctx")
    width = channels * sections
    per = heads // 2
    count = per
    slabs = spots // (2 * count)
    rows = slabs == 2 and count == 4
    spot = functools.partial(call, scalar=(per, spots))

    def turned(value, sec, shift):
        route = [
            (s * spots + c, ((s + sec) % sections) * spots + (c + shift) % spots)
            for s in range(sections)
            for c in range(spots)
        ]
        return lax.ppermute(value, ("section", "ctx"), route)

    def swapped(value, distance):
        return lax.ppermute(value, "ctx", [(i, i ^ distance) for i in range(spots)])

    def moved(value, shift):
        return lax.ppermute(
            value, "ctx", [(i, i + shift) for i in range(spots) if 0 <= i + shift < spots]
        )

    payload, sums, last_sums, x, go, kern, decay, rates = call(
        prelude_kernel,
        (
            array(RIM, channels + HEAD_DIM), array(RIM, length), array(RIM, HEAD_DIM), array(*inputs.shape, dtype=bf16),
            array(*inputs.shape, dtype=bf16), array(*conv_weight.shape), array(*inputs.shape), array(heads, length),
        ),
        *[pltpu.with_memory_space_constraint(a, pltpu.HBM) for a in (inputs, out_grads, conv_weight, log_decay, beta.T)],
        name="prelude", far_in=True, scratch=[pltpu.SemaphoreType.DMA((5,))],
    )
    total = sums
    rim_total = 0.0
    for sec in range(1, sections):
        total = total + turned(sums, sec, 0)
        rim_total = rim_total + turned(last_sums, sec, 1)
    rim = turned(payload, 0, 1)
    e1, e2, edge, rate, scale = call(
        functools.partial(gates_kernel, width),
        (array(length, channels), array(length, channels), array(24, channels), array(length, channels),
         array(length, HEAD_DIM)),
        decay, rates, total, name="gates", cost=BESIDE,
    )
    rim_scale = lax.rsqrt((rim_total + rim[:, channels:]) / width + norm_eps)

    shared = (x, go, kern, e1, e2, edge, rate, rim)
    tile = (HEAD_DIM, HEAD_DIM)

    def local(slots, name, unread=()):
        n = len(slots)
        return spot(
            functools.partial(local_kernel, slots),
            (array(n, 384, HEAD_DIM), array(n, WIDE, *tile), array(n, NARROW, *tile, dtype=bf16)),
            *shared, scale, rim_scale, name=name, unread=unread, cost=BESIDE,
        )

    def prepared(slots, saved, name):
        n = len(slots)
        return spot(
            functools.partial(ready_kernel, slots),
            (array(n, MORE, *tile), array(n, PAIRS, *tile, dtype=bf16)),
            x, kern, e2, edge, rim, scale, rim_scale, *saved, name=name, cost=BESIDE,
        )

    inner_slots, outer_slots = range(per), range(per, 2 * per)
    joined, others = ((array(256, HEAD_DIM),), (array(*tile),)) if rows else ((array(384, HEAD_DIM),), ())
    outer, *outer_saved = local(outer_slots, "local_outer")
    outer_recv = swapped(outer, 1)
    inner, *inner_saved = local(inner_slots, "local_inner")
    pairs = spot(join_kernel, joined * per + others * per, inner, outer_recv, name="join")
    parts = [pairs[0]] + [swapped(pairs[n], 2 * n) for n in range(1, count)]
    second = [pairs[per]] + [swapped(pairs[per + n], 2 * n) for n in range(1, count)] if rows else []
    outer_saved += prepared(outer_slots, outer_saved, "ready_outer")
    inner_saved += prepared(inner_slots, inner_saved, "ready_inner")
    ahead = [outer_saved[-1], inner_saved[-1]]

    held = pltpu.VMEM((count, 256 if rows else 384, HEAD_DIM), f32)
    square = array(*tile)
    step = 2 * count

    def returned(values):
        return [values[0]] + [swapped(values[n], 2 * n) for n in range(1, count)]

    if rows:
        found = pltpu.VMEM((count, *tile), f32)
        total, products, sure = spot(
            functools.partial(two_gather_kernel, len(ahead)),
            (square, array(2, *tile), array(4, *tile)),
            *parts, name="gather", scratch=[held], unread=ahead,
        )
        other = swapped(total, step)
        reach, *early = spot(
            reach_kernel, (array(6, *tile, dtype=bf16),) + (square,) * 4,
            *parts, products, sure, name="reach", scratch=[held], cost=BESIDE,
        )
        early = returned(early)
        (known,) = spot(
            known_kernel, (array(4, *tile),), *parts, *second, name="known", scratch=[held, found], cost=BESIDE
        )
        late = spot(late_kernel, (square,) * 4, other, known, reach, name="late", scratch=[found])
        states = list(zip(early, returned(late)))
    else:
        gathered = spot(
            functools.partial(gather_kernel, count, len(ahead)), (square,) * 3,
            *parts, name="gather", scratch=[held], unread=ahead,
        )
        ends = (jnp.zeros(tile, f32),) * 2
        for hop in range(slabs - 1):
            if hop == 0:
                ends = gathered[1:]
            else:
                ends = spot(hop_kernel, (square,) * 2, *gathered, *ends, name=f"hop{hop}")
            ends = (moved(ends[0], step), moved(ends[1], -step))
        spread = returned(
            spot(
                functools.partial(spread_kernel, count), (array(256, HEAD_DIM),) * count,
                *parts, *ends, name="spread", scratch=[held, pltpu.VMEM((count, 256, HEAD_DIM), f32)],
            )
        )
        states = [(a,) for a in spread]

    keeps, recvs = (inner,), (outer_recv,)
    mine, send = spot(
        functools.partial(part_kernel, len(keeps), len(states[0])), (array(per, 256, HEAD_DIM),) * 2,
        *keeps, *recvs, *(a for pair in states for a in pair), name="part",
    )
    far = swapped(send, 1)

    def backward(slots, saved, homes, states, chain, name):
        n = len(slots)
        chained = chain is not None
        before = (chain[2], chain[3]) if chained else ()
        return spot(
            functools.partial(back_kernel, slots, homes, chained),
            (
                array(*inputs.shape, dtype=bf16), array(n, length, HEAD_DIM), array(RIM, length),
                array(RIM, channels + HEAD_DIM),
            )
            + (array(RIM, HEAD_DIM),) * chained,
            *shared, states, *(a for group in saved for a in group), *before, name=name, far_out=(0,),
            alias=chain[0] if chained else None,
            scratch=[pltpu.VMEM((n, length, HEAD_DIM), bf16), pltpu.SemaphoreType.DMA((n,))],
        )

    slots = range(heads)
    homes = [(0, n) for n in range(per)]
    chain = backward(slots[:per], [inner_saved], homes, mine, None, "back_inner")
    grads = [chain[1]]
    chain = backward(slots[per:], [outer_saved], homes, far, chain, "back_outer")
    grads.append(chain[1])
    stream_out, _, inner_sum, rim_grad, rim_sums = chain

    inner_total, next_sums = inner_sum, 0.0
    for sec in range(1, sections):
        inner_total = inner_total + turned(inner_sum, sec, 0)
        next_sums = next_sums + turned(rim_sums, sec, -1)
    next_rim = turned(rim_grad, 0, -1)
    (input_grad,) = spot(
        functools.partial(finish_kernel, slots, width), (array(*inputs.shape, dtype=bf16),),
        x, go, scale, inner_total, next_sums + next_rim[:, channels:], next_rim, *grads, name="finish",
        far_out=(0,), scratch=[pltpu.VMEM((heads, length, HEAD_DIM), bf16), pltpu.SemaphoreType.DMA((heads,))],
    )
    return (stream_out, input_grad)


def solution(mesh):
    in_specs = (
        P("ctx", "section"),
        P("ctx", "section"),
        P(None, None, "section"),
        P("ctx", "section"),
        P("ctx", "section"),
    )
    out_specs = (P("ctx", "section"), P("ctx", "section"))
    return jax.shard_map(shards, mesh=mesh, in_specs=in_specs, out_specs=out_specs, check_vma=False)
```

```python
import functools

import jax
import jax.numpy as jnp
from jax import lax
from jax.experimental import pallas as pl
from jax.experimental.pallas import tpu as pltpu
from jax.sharding import PartitionSpec as P

HEAD_DIM = 128
RIM = 8
epsilon = 1e-06
norm_eps = 1e-05
f32 = jnp.float32
bf16 = jnp.bfloat16
VMEM_LIMIT = 24 * 1024 * 1024

DIMS = {
    "nn": (((1,), (0,)), ((), ())),
    "nt": (((1,), (1,)), ((), ())),
    "tn": (((0,), (0,)), ((), ())),
}


def split(a):
    high = a.astype(bf16)
    return high, (a - high.astype(f32)).astype(bf16)


def exact(a):
    return a, None


def rows_of(*parts):
    highs = jnp.concatenate([p[0] for p in parts], axis=0)
    lows = [jnp.zeros_like(p[0]) if p[1] is None else p[1] for p in parts]
    return highs, jnp.concatenate(lows, axis=0)


def cols_of(*parts):
    return tuple(jnp.concatenate([p[i] for p in parts], axis=1) for i in range(2))


def mm(a, b, form):
    width = b[0].shape[1]
    if form != "nt" and a[1] is not None and b[1] is not None and width == HEAD_DIM:
        right = jnp.concatenate(b, axis=1)
        left = jnp.concatenate(a, axis=0 if form == "tn" else 1)
        out = lax.dot_general(left, jnp.concatenate([right, right], axis=0), DIMS[form], preferred_element_type=f32)
        return out[:, :width] + out[:, width:]
    pairs = [(a[0], b[0])]
    if a[1] is not None:
        pairs.append((a[1], b[0]))
    if b[1] is not None:
        pairs.append((a[0], b[1]))
    left = jnp.concatenate([p[0] for p in pairs], axis=0 if form == "tn" else 1)
    right = jnp.concatenate([p[1] for p in pairs], axis=1 if form == "nt" else 0)
    return lax.dot_general(left, right, DIMS[form], preferred_element_type=f32)


def row_sums(a):
    high = a.astype(bf16)
    rest = a - high.astype(f32)
    mid = rest.astype(bf16)
    low = (rest - mid.astype(f32)).astype(bf16)
    terms = jnp.concatenate([high, mid, low], axis=1)
    ones = jnp.ones((RIM, terms.shape[1]), bf16)
    return lax.dot_general(ones, terms, DIMS["nt"], preferred_element_type=f32)


def down_rows(row):
    return jnp.transpose(jnp.broadcast_to(row[0:1], (HEAD_DIM, row.shape[1])))


def iotas(n=HEAD_DIM):
    return (
        lax.broadcasted_iota(jnp.int32, (n, n), 0),
        lax.broadcasted_iota(jnp.int32, (n, n), 1),
    )


def lane_slice(place):
    return pl.ds(pl.multiple_of(place * HEAD_DIM, HEAD_DIM), HEAD_DIM)


def prelude_kernel(
    x_hbm, go_hbm, kern_hbm, decay_hbm, beta_hbm, payload_ref, sums_ref, last_sums_ref, x_ref, go_ref, kern_ref,
    decay_ref, beta_ref, sems,
):
    pairs = ((x_hbm, x_ref), (go_hbm, go_ref), (kern_hbm, kern_ref), (decay_hbm, decay_ref), (beta_hbm, beta_ref))
    copies = [pltpu.make_async_copy(src, dst, sems.at[n]) for n, (src, dst) in enumerate(pairs)]
    for copy in copies:
        copy.start()
    copies[0].wait()
    x = x_ref[...].astype(f32)
    length, channels = x.shape
    blocks = [x[:, n : n + HEAD_DIM] for n in range(0, channels, HEAD_DIM)]
    squares = sum(block * block for block in blocks)
    sums_ref[...] = row_sums(squares)
    last = jnp.sum(squares[length - RIM :], axis=1, keepdims=True)
    last = jnp.broadcast_to(last, (RIM, HEAD_DIM))
    last_sums_ref[...] = last
    payload_ref[:, :channels] = x[length - RIM :]
    payload_ref[:, channels:] = last
    for copy in copies[1:]:
        copy.wait()


BASE = 5


def inverse_all(systems):
    row, col = iotas()
    size = 1 << BASE
    own = row >> BASE == col >> BASE
    row8 = lax.broadcasted_iota(jnp.int32, (RIM, HEAD_DIM), 0)
    col8 = lax.broadcasted_iota(jnp.int32, (RIM, HEAD_DIM), 1)
    first = (col8 >> BASE) << BASE
    found = []
    for n in systems:
        blocks = jnp.sum(jnp.where(own, n, 0.0).reshape(-1, size, HEAD_DIM), axis=0)
        tiles = [jnp.where(row8 + RIM * t == (col8 & (size - 1)), 1.0, 0.0) for t in range(size // RIM)]
        for s in range(size - 1):
            done = tiles[s // RIM][s % RIM : s % RIM + 1]
            for t in range(s // RIM, size // RIM):
                column = jnp.take_along_axis(
                    blocks[RIM * t : RIM * (t + 1)], first + s, axis=1, mode="promise_in_bounds"
                )
                tiles[t] = tiles[t] - column * done
        found.append(jnp.where(own, jnp.concatenate(tiles * (HEAD_DIM // size), axis=0), 0.0))
    level = BASE
    while (1 << level) < HEAD_DIM:
        mask = (row >> (level + 2) == col >> (level + 2)) & (row >> level != col >> level)
        parts = [split(d) for d in found]
        cross = [split(jnp.where(mask, n, 0.0)) for n in systems]
        maps = [split(mm(p, c, "nn")) for p, c in zip(parts, cross)]
        twice = [mm(m, cols_of(m, p), "nn") for m, p in zip(maps, parts)]
        less = [d - t[:, HEAD_DIM:] for d, t in zip(found, twice)]
        found = [y + mm(split(t[:, :HEAD_DIM]), split(y), "nn") for y, t in zip(less, twice)]
        level += 2
    return found


def mixes_of(normed, rim, kern):
    row8 = lax.broadcasted_iota(jnp.int32, (RIM, HEAD_DIM), 0)
    taps = kern.shape[1]
    shifted = [normed]
    for s in range(1, taps):
        moved = pltpu.roll(normed, s, 0)
        first = jnp.where(row8 < s, pltpu.roll(rim, s, 0), moved[:RIM])
        shifted.append(jnp.concatenate([first, moved[RIM:]], axis=0))
    return [
        sum(kern[j, i : i + 1] * shifted[taps - 1 - i] for i in range(taps)) for j in range(3)
    ]


def gates_kernel(width, decay_ref, beta_ref, sums_ref, e1_ref, e2_ref, edge_ref, rate_ref, scale_ref):
    scale_ref[...] = down_rows(lax.rsqrt(sums_ref[...] / width + norm_eps))
    length = decay_ref.shape[0]
    row, col = iotas()
    tril = jnp.where(row >= col, 1.0, 0.0).astype(bf16)
    tril = jnp.concatenate([tril] * 3, axis=1)
    for head in range(decay_ref.shape[1] // HEAD_DIM):
        here = slice(head * HEAD_DIM, (head + 1) * HEAD_DIM)
        decay = decay_ref[:, here]
        high = decay.astype(bf16)
        rest = decay - high.astype(f32)
        mid = rest.astype(bf16)
        low = (rest - mid.astype(f32)).astype(bf16)
        cumulative = lax.dot_general(
            tril, jnp.concatenate([high, mid, low], axis=0), DIMS["nn"], preferred_element_type=f32
        )
        middle = cumulative[length // 2 : length // 2 + 1]
        final = cumulative[length - 1 : length]
        e1_ref[:, here] = jnp.exp(cumulative - middle)
        e2_ref[:, here] = jnp.exp(middle - cumulative)
        edge_ref[0:8, here] = jnp.broadcast_to(jnp.exp(middle), (8, HEAD_DIM))
        edge_ref[8:16, here] = jnp.broadcast_to(jnp.exp(final - middle), (8, HEAD_DIM))
        edge_ref[16:24, here] = jnp.broadcast_to(jnp.exp(final), (8, HEAD_DIM))
        rate_ref[:, here] = down_rows(beta_ref[head : head + 1])


def scaled(x_ref, rim_ref, kern_ref, scale, rim_scale, at):
    x = x_ref[:, at].astype(f32)
    return mixes_of(x * scale, rim_ref[:, at] * rim_scale, kern_ref[:, :, at])


def scales(flags, scale_ref, rim_scale_ref):
    return scale_ref[...], jnp.where(flags[4] != 0, rim_scale_ref[...], 0.0)


def keep_split(ref, j, n, parts):
    ref[j, n] = parts[0]
    ref[j, n + 1] = parts[1]


def kept(ref, j, n):
    return ref[j, n], ref[j, n + 1]


def local_kernel(
    slots, flags, x_ref, go_ref, kern_ref, e1_ref, e2_ref, edge_ref, rate_ref, rim_ref, scale_ref, rim_scale_ref,
    *rest,
):
    comp_ref, wide_ref, narrow_ref = rest[-3:]
    length = x_ref.shape[0]
    row, col = iotas()
    strict, full = row > col, row >= col
    scale, rim_scale = scales(flags, scale_ref, rim_scale_ref)
    data = []
    for j, slot in enumerate(slots):
        at = lane_slice(slot ^ flags[0])
        mixes = scaled(x_ref, rim_ref, kern_ref, scale, rim_scale, at)
        act = [m / (1.0 + jnp.exp(-m)) for m in mixes]
        q, k = [a * lax.rsqrt(jnp.sum(a * a, axis=1, keepdims=True) + epsilon) for a in act[:2]]
        rate, e1, e2 = rate_ref[:, at], e1_ref[:, at], e2_ref[:, at]
        em, ecm, ef = [edge_ref[n : n + 1, at] for n in (0, 8, 16)]
        qf, kf, kb = q * e1, k * e1, k * e2
        skf, sqf, skb = split(kf), split(qf), split(kb)
        products = mm(rows_of(skf, sqf), skb, "nt")
        system = jnp.where(strict, rate * products[:length], 0.0)
        scores = split(jnp.where(full, products[length:], 0.0))
        go = exact(go_ref[:, at])
        wide_ref[j, 0], wide_ref[j, 1] = q, k
        for n, parts in enumerate((skf, sqf, skb, scores)):
            keep_split(narrow_ref, j, 2 * n, parts)
        data.append(
            dict(system=system, go=go, rhs=cols_of(split(rate * kf * em), split(rate * act[2])), ke=split(kb * ecm),
                 qg=qf * em, scores=scores, ef=ef)
        )
    inverses = inverse_all([d["system"] for d in data])
    for j, d in enumerate(data):
        d["fresh_grad"] = split(mm(d["scores"], d["go"], "tn"))
        keep_split(narrow_ref, j, 8, d["fresh_grad"])
    for j, (d, inverse) in enumerate(zip(data, inverses)):
        inverse = split(inverse)
        keep_split(narrow_ref, j, 14, inverse)
        solved = mm(inverse, d["rhs"], "nn")
        wide_ref[j, 2] = solved[:, HEAD_DIM:]
        d["solved"] = split(solved)
    for j, d in enumerate(data):
        solved = d["solved"]
        keep_split(narrow_ref, j, 10, (solved[0][:, :HEAD_DIM], solved[1][:, :HEAD_DIM]))
        keep_split(narrow_ref, j, 12, (solved[0][:, HEAD_DIM:], solved[1][:, HEAD_DIM:]))
        maps = mm(d["ke"], solved, "tn")
        comp_ref[j, 0:128] = jnp.where(row == col, d["ef"], 0.0) - maps[:, :HEAD_DIM]
        comp_ref[j, 128:256] = maps[:, HEAD_DIM:]
        w = (solved[0][:, :HEAD_DIM], solved[1][:, :HEAD_DIM])
        comp_ref[j, 256:384] = mm(split(d["qg"]), d["go"], "tn") - mm(w, d["fresh_grad"], "tn")


WIDE, NARROW = 3, 16


def ready_kernel(
    slots, flags, x_ref, kern_ref, e2_ref, edge_ref, rim_ref, scale_ref, rim_scale_ref, wide_ref, narrow_ref,
    more_ref, pairs_ref,
):
    scale, rim_scale = scales(flags, scale_ref, rim_scale_ref)
    for j, slot in enumerate(slots):
        at = lane_slice(slot ^ flags[0])
        mixes = scaled(x_ref, rim_ref, kern_ref, scale, rim_scale, at)
        sig = [1.0 / (1.0 + jnp.exp(-m)) for m in mixes]
        slope = [s * (1.0 + m * (1.0 - s)) for m, s in zip(mixes, sig)]
        act = [m * s for m, s in zip(mixes[:2], sig)]
        inv = [lax.rsqrt(jnp.sum(a * a, axis=1, keepdims=True) + epsilon) for a in act]
        em, ecm = edge_ref[0:1, at], edge_ref[8:9, at]
        scores, fresh_grad, inverse = [kept(narrow_ref, j, n) for n in (6, 8, 14)]
        solved = cols_of(kept(narrow_ref, j, 10), kept(narrow_ref, j, 12))
        seen = mm(scores, solved, "nn")
        ke = split(wide_ref[j, 1] * e2_ref[:, at] * ecm)
        back = mm(inverse, cols_of(fresh_grad, ke), "tn")
        more_ref[j, 0] = slope[0] * inv[0]
        more_ref[j, 1] = slope[1] * inv[1]
        more_ref[j, 2] = slope[2]
        more_ref[j, 3] = seen[:, HEAD_DIM:]
        more_ref[j, 4] = back[:, :HEAD_DIM]
        qf = narrow_ref[j, 2].astype(f32) + narrow_ref[j, 3].astype(f32)
        keep_split(pairs_ref, j, 0, split(qf * em - seen[:, :HEAD_DIM]))
        keep_split(pairs_ref, j, 2, split(back[:, HEAD_DIM:]))


MORE, PAIRS = 5, 4


def join_kernel(flags, keep_ref, recv_ref, *outs):
    later, upper = flags[1] != 0, flags[3] != 0
    heads = keep_ref.shape[0]
    for j in range(heads):
        keep, recv = keep_ref[j], recv_ref[j]
        lo = jnp.where(later, recv, keep)
        hi = jnp.where(later, keep, recv)
        lo_map, hi_map = split(lo[0:128]), split(hi[0:128])
        forward = mm(hi_map, cols_of(lo_map, split(lo[128:256])), "nn")
        grad = mm(lo_map, split(hi[256:384]), "tn") + lo[256:384]
        state = forward[:, HEAD_DIM:] + hi[128:256]
        out = outs[j]
        out[0:128] = forward[:, :HEAD_DIM]
        if len(outs) == heads:
            out[128:256], out[256:384] = state, grad
        else:
            out[128:256] = jnp.where(upper, grad, state)
            outs[heads + j][...] = jnp.where(upper, state, grad)


def collect(place, parts, held):
    for n, part in enumerate(parts):
        held[place ^ n] = part[...]


def gather_kernel(count, waits, flags, *refs):
    parts, outs, held = refs[:count], refs[count + waits : -1], refs[-1]
    collect(flags[2], parts, held)
    maps = [split(held[p, 0:128]) for p in range(count)]
    state, grad = held[0, 128:256], held[count - 1, 256:384]
    whole = held[0, 0:128]
    for p in range(1, count):
        state = mm(maps[p], split(state), "nn") + held[p, 128:256]
        grad = mm(maps[count - 1 - p], split(grad), "tn") + held[count - 1 - p, 256:384]
        whole = mm(maps[p], split(whole), "nn")
    outs[0][...], outs[1][...], outs[2][...] = whole, state, grad


def hop_kernel(flags, t_ref, u_ref, g_ref, s_ref, e_ref, s_out, e_out):
    t = split(t_ref[...])
    s_out[...] = mm(t, split(s_ref[...]), "nn") + u_ref[...]
    e_out[...] = mm(t, split(e_ref[...]), "tn") + g_ref[...]


def spread_kernel(count, flags, *refs):
    parts, ins, outs, held, found = refs[:count], refs[count : -2 - count], refs[-2 - count : -2], refs[-2], refs[-1]
    collect(flags[2], parts, held)
    state, grad = ins[0][...], ins[1][...]
    for p in range(count):
        back = count - 1 - p
        found[p, 0:128] = state
        found[back, 128:256] = grad
        if p + 1 < count:
            state = mm(split(held[p, 0:128]), split(state), "nn") + held[p, 128:256]
            grad = mm(split(held[back, 0:128]), split(grad), "tn") + held[back, 256:384]
    for n, out in enumerate(outs):
        out[...] = found[flags[2] ^ n]


def two_gather_kernel(waits, flags, *refs):
    parts, outs = refs[:4], refs[4 + waits : -1]
    held = refs[-1]
    total_ref, pairs_ref, found_ref = outs
    upper = flags[3] != 0
    collect(flags[2], parts, held)
    t = [split(held[p, 0:128]) for p in range(4)]
    u = [held[p, 128:256] for p in range(4)]
    su = [split(a) for a in u]
    last = mm(t[3], cols_of(t[2], su[2]), "nn")
    first = mm(t[1], cols_of(t[0], su[0]), "nn")
    second = first[:, HEAD_DIM:] + u[1]
    first, last, last_u = first[:, :HEAD_DIM], last[:, :HEAD_DIM], last[:, HEAD_DIM:]
    third = mm(t[2], su[3], "tn") + u[2]
    low = mm(t[0], su[1], "tn")
    s_second, s_third = split(second), split(third)
    forward = [jnp.zeros_like(second), u[0], second, mm(t[2], s_second, "nn") + u[2]]
    back = [mm(t[1], s_third, "tn") + u[1], third, u[3], jnp.zeros_like(third)]
    state = mm(split(last), s_second, "nn") + (last_u + u[3])
    grad = mm(split(first), s_third, "tn") + (low + u[0])
    total_ref[...] = jnp.where(upper, grad, state)
    pairs_ref[0], pairs_ref[1] = first, last
    for p in range(4):
        found_ref[p] = jnp.where(upper, back[p], forward[p])


def known_kernel(flags, *refs):
    parts, others, known_ref, held, values = refs[:4], refs[4:8], refs[8], refs[9], refs[10]
    upper = flags[3] != 0
    collect(flags[2], parts, held)
    collect(flags[2], others, values)
    t = [split(held[p, 0:128]) for p in (1, 2)]
    second = mm(t[0], split(values[0]), "nn") + values[1]
    third = mm(t[1], split(second), "nn") + values[2]
    below = mm(t[1], split(values[3]), "tn") + values[2]
    lowest = mm(t[0], split(below), "tn") + values[1]
    for n, (up, down) in enumerate(((values[0], values[3]), (second, below), (third, lowest))):
        known_ref[n + 1] = jnp.where(upper, up, down)
    known_ref[0] = jnp.zeros_like(second)


def reach_kernel(flags, *refs):
    parts, pairs_ref, found_ref, out_ref, early, held = refs[:4], refs[4], refs[5], refs[6], refs[7:11], refs[11]
    for n, out in enumerate(early):
        out[...] = found_ref[flags[2] ^ n]
    upper = flags[3] != 0
    collect(flags[2], parts, held)
    first, last = pairs_ref[0], pairs_ref[1]
    far_up = mm(split(held[2, 0:128]), split(first), "nn")
    far_down = mm(split(last), split(held[1, 0:128]), "nn")
    ups, downs = (held[0, 0:128], first, far_up), (held[3, 0:128], last, far_down)
    for n in range(3):
        high, low = split(jnp.where(upper, ups[n], jnp.transpose(downs[n])))
        out_ref[2 * n], out_ref[2 * n + 1] = high, low


def late_kernel(flags, recv_ref, known_ref, reach_ref, *refs):
    outs, found = refs[:-1], refs[-1]
    from_end = jnp.where(flags[3] != 0, 0, 3)
    recv = recv_ref[...]
    parts = split(recv)
    found[from_end] = recv
    for n in range(3):
        found[from_end ^ (n + 1)] = mm((reach_ref[2 * n], reach_ref[2 * n + 1]), parts, "nn") + known_ref[n + 1]
    for n, out in enumerate(outs):
        out[...] = found[flags[2] ^ n]


def part_kernel(sets, per_head, flags, *refs):
    maps = [(keep, recv, n) for keep, recv in zip(refs[:sets], refs[sets : 2 * sets]) for n in range(keep.shape[0])]
    ins, (mine_ref, send_ref) = refs[2 * sets : -2], refs[-2:]
    later, upper = flags[1] != 0, flags[3] != 0
    for j, (keep_ref, recv_ref, n) in enumerate(maps):
        if per_head == 1:
            start, end = ins[j][0:128], ins[j][128:256]
        else:
            early, late = ins[2 * j][...], ins[2 * j + 1][...]
            start, end = jnp.where(upper, late, early), jnp.where(upper, early, late)
        keep, recv = keep_ref[n], recv_ref[n]
        lo = jnp.where(later, recv, keep)
        hi = jnp.where(later, keep, recv)
        start_hi = mm(split(lo[0:128]), split(start), "nn") + lo[128:256]
        end_lo = mm(split(hi[0:128]), split(end), "tn") + hi[256:384]
        mine_ref[j, 0:128] = jnp.where(later, start_hi, start)
        mine_ref[j, 128:256] = jnp.where(later, end, end_lo)
        send_ref[j, 0:128] = jnp.where(later, start, start_hi)
        send_ref[j, 128:256] = jnp.where(later, end_lo, end)


def back_kernel(
    slots, homes, chained, flags, x_ref, go_ref, kern_ref, e1_ref, e2_ref, edge_ref, rate_ref, rim_ref, state_ref,
    *rest,
):
    sets = 1 + max(n for n, _ in homes)
    saved, rest = [rest[4 * n : 4 * n + 4] for n in range(sets)], rest[4 * sets :]
    if chained:
        sums_in, rim_grad_in, rest = rest[0], rest[1], rest[3:]
    out_hbm, grad_ref, sums_ref, rim_grad_ref, out_ref, sems = rest[:4] + rest[-2:]
    length = x_ref.shape[0]
    channels = x_ref.shape[1]
    row, col = iotas()
    row8 = lax.broadcasted_iota(jnp.int32, (RIM, HEAD_DIM), 0)
    strict, full = row > col, row >= col
    taps = kern_ref.shape[1]
    if chained:
        rim_grad_ref[...] = rim_grad_in[...]
    dot_all = rim_dot = 0.0
    data, copies = [], []
    for j, (slot, (n, i)) in enumerate(zip(slots, homes)):
        at = lane_slice(slot ^ flags[0])
        wide_ref, narrow_ref, more_ref, pairs_ref = saved[n]
        start, end = split(state_ref[j, 0:128]), split(state_ref[j, 128:256])
        first = mm(rows_of(kept(pairs_ref, i, 0), kept(narrow_ref, i, 10)), start, "nn")
        z = more_ref[i, 4] + mm(kept(pairs_ref, i, 2), end, "nn")
        x = x_ref[:, at].astype(f32)
        out_ref[j] = (x + (more_ref[i, 3] + first[:length])).astype(bf16)
        copies.append(pltpu.make_async_copy(out_ref.at[j], out_hbm.at[:, at], sems.at[j]))
        copies[-1].start()
        data.append(dict(at=at, x=x, start=start, end=end, z=z, fresh=split(wide_ref[i, 2] - first[length:])))
    for j, (d, (n, i)) in enumerate(zip(data, homes)):
        at = d["at"]
        wide_ref, narrow_ref, more_ref, _ = saved[n]
        q, k = wide_ref[i, 0], wide_ref[i, 1]
        gq, gk, gv = [more_ref[i, n] for n in range(3)]
        skf, sqf, skb = [kept(narrow_ref, i, n) for n in (0, 2, 4)]
        e1, e2, rate = e1_ref[:, at], e2_ref[:, at], rate_ref[:, at]
        em, ecm = edge_ref[0:1, at], edge_ref[8:9, at]
        go = exact(go_ref[:, at])
        second = mm(rows_of(go, split(d["z"])), rows_of(d["fresh"], d["start"]), "nt")
        score_grad = split(jnp.where(full, second[:length, :HEAD_DIM], 0.0))
        product_grad = split(jnp.where(strict, -rate * second[length:, :HEAD_DIM], 0.0))
        qg_grad = second[:length, HEAD_DIM:]
        kg_grad = -rate * second[length:, HEAD_DIM:]
        ke_grad = mm(d["fresh"], d["end"], "nt")
        pair = rows_of(score_grad, product_grad)
        third = mm(pair, skb, "nn")
        kb_grad = mm(pair, rows_of(sqf, skf), "tn")
        q_grad = e1 * (third[:length] + em * qg_grad)
        k_grad = e1 * (third[length:] + em * kg_grad) + e2 * (kb_grad + ecm * ke_grad)
        mix_grads = [
            gq * (q_grad - q * jnp.sum(q * q_grad, axis=1, keepdims=True)),
            gk * (k_grad - k * jnp.sum(k * k_grad, axis=1, keepdims=True)),
            gv * (rate * d["z"]),
        ]
        kern = kern_ref[:, :, at]
        normed_grad = rim_grad = 0.0
        for i in range(taps):
            each = sum(kern[n, i : i + 1] * mix_grads[n] for n in range(3))
            s = taps - 1 - i
            if s == 0:
                normed_grad = normed_grad + each
            else:
                moved = pltpu.roll(each, length - s, 0)
                normed_grad = normed_grad + jnp.where(row < length - s, moved, 0.0)
                rim_grad = rim_grad + jnp.where(row8 >= RIM - s, moved[length - RIM :], 0.0)
        grad_ref[j] = normed_grad
        rim_grad_ref[:, at] = rim_grad
        dot_all = dot_all + normed_grad * d["x"]
        rim_dot = rim_dot + rim_grad * rim_ref[:, at]
    sums = row_sums(dot_all)
    rim_sums = jnp.broadcast_to(jnp.sum(rim_dot, axis=1, keepdims=True), rim_dot.shape)
    if chained:
        sums, rim_sums = sums + sums_in[...], rim_sums + rim_grad_in[:, channels:]
    sums_ref[...] = sums
    rim_grad_ref[:, channels:] = rim_sums
    if chained:
        rest[4][...] = rim_sums
    for copy in copies:
        copy.wait()


def finish_kernel(slots, width, flags, x_ref, go_ref, scale_ref, inner_ref, next_sums_ref, next_ref, *refs):
    grads, (out_hbm, out_ref, sems) = refs[:-3], refs[-3:]
    length = x_ref.shape[0]
    scale = scale_ref[...]
    inner = down_rows(inner_ref[...])
    last = flags[5] == 0
    next_sums = jnp.where(last, 0.0, next_sums_ref[...])
    inner = jnp.concatenate([inner[: length - RIM], inner[length - RIM :] + next_sums], axis=0)
    cubed = scale * scale * scale * inner * (1.0 / width)
    copies = []
    places = [(ref, n) for ref in grads for n in range(ref.shape[0])]
    for j, (slot, (grad_ref, n)) in enumerate(zip(slots, places)):
        at = lane_slice(slot ^ flags[0])
        grad = grad_ref[n]
        next_grad = jnp.where(last, 0.0, next_ref[:, at])
        grad = jnp.concatenate([grad[: length - RIM], grad[length - RIM :] + next_grad], axis=0)
        total = go_ref[:, at].astype(f32) + grad * scale - x_ref[:, at].astype(f32) * cubed
        out_ref[j] = total.astype(bf16)
        copies.append(pltpu.make_async_copy(out_ref.at[j], out_hbm.at[:, at], sems.at[j]))
        copies[-1].start()
    for copy in copies:
        copy.wait()


def call(kernel, outs, *args, name=None, scratch=(), scalar=(), cost=None, far_in=False, far_out=(), unread=(), alias=None):
    spec, hbm = pl.BlockSpec(memory_space=pltpu.VMEM), pl.BlockSpec(memory_space=pltpu.HBM)
    in_specs = [hbm if far_in else spec] * len(args)
    in_specs += [pl.BlockSpec(memory_space=pl.ANY)] * len(unread)
    args = args + tuple(unread)
    aliases = {}
    if alias is not None:
        args, in_specs, aliases = args + (alias,), in_specs + [hbm], {len(args): 0}
    return pl.pallas_call(
        (lambda *refs: kernel(placed(*scalar), *refs)) if scalar else kernel,
        out_shape=list(outs),
        in_specs=in_specs,
        out_specs=[hbm if n in far_out else spec for n in range(len(outs))],
        scratch_shapes=scratch,
        input_output_aliases=aliases,
        compiler_params=pltpu.CompilerParams(vmem_limit_bytes=VMEM_LIMIT),
        cost_estimate=cost,
        name=name,
    )(*args)


BESIDE = pl.CostEstimate(flops=0, bytes_accessed=0, transcendentals=0)


def array(*shape, dtype=f32):
    return jax.ShapeDtypeStruct(shape, dtype)


def placed(per, spots):
    me = lax.axis_index("ctx")
    place, later = lax.rem(lax.shift_right_logical(me, 1), per), lax.rem(me, 2)
    row = lax.rem(lax.div(me, 2 * per), 2)
    return [later * per + place, later, place, row, me, spots - 1 - me]


def shards(inputs, out_grads, conv_weight, log_decay, beta):
    length, channels = inputs.shape
    heads = channels // HEAD_DIM
    sections, spots = lax.axis_size("section"), lax.axis_size("ctx")
    width = channels * sections
    per = heads // 2
    count = per
    slabs = spots // (2 * count)
    rows = slabs == 2 and count == 4
    spot = functools.partial(call, scalar=(per, spots))

    def turned(value, sec, shift):
        route = [
            (s * spots + c, ((s + sec) % sections) * spots + (c + shift) % spots)
            for s in range(sections)
            for c in range(spots)
        ]
        return lax.ppermute(value, ("section", "ctx"), route)

    def swapped(value, distance):
        return lax.ppermute(value, "ctx", [(i, i ^ distance) for i in range(spots)])

    def moved(value, shift):
        return lax.ppermute(
            value, "ctx", [(i, i + shift) for i in range(spots) if 0 <= i + shift < spots]
        )

    payload, sums, last_sums, x, go, kern, decay, rates = call(
        prelude_kernel,
        (
            array(RIM, channels + HEAD_DIM), array(RIM, length), array(RIM, HEAD_DIM), array(*inputs.shape, dtype=bf16),
            array(*inputs.shape, dtype=bf16), array(*conv_weight.shape), array(*inputs.shape), array(heads, length),
        ),
        *[pltpu.with_memory_space_constraint(a, pltpu.HBM) for a in (inputs, out_grads, conv_weight, log_decay, beta.T)],
        name="prelude", far_in=True, scratch=[pltpu.SemaphoreType.DMA((5,))],
    )
    total = sums
    rim_total = 0.0
    for sec in range(1, sections):
        total = total + turned(sums, sec, 0)
        rim_total = rim_total + turned(last_sums, sec, 1)
    rim = turned(payload, 0, 1)
    e1, e2, edge, rate, scale = call(
        functools.partial(gates_kernel, width),
        (array(length, channels), array(length, channels), array(24, channels), array(length, channels),
         array(length, HEAD_DIM)),
        decay, rates, total, name="gates", cost=BESIDE,
    )
    rim_scale = lax.rsqrt((rim_total + rim[:, channels:]) / width + norm_eps)

    shared = (x, go, kern, e1, e2, edge, rate, rim)
    tile = (HEAD_DIM, HEAD_DIM)

    def local(slots, name, unread=()):
        n = len(slots)
        return spot(
            functools.partial(local_kernel, slots),
            (array(n, 384, HEAD_DIM), array(n, WIDE, *tile), array(n, NARROW, *tile, dtype=bf16)),
            *shared, scale, rim_scale, name=name, unread=unread, cost=BESIDE,
        )

    def prepared(slots, saved, name):
        n = len(slots)
        return spot(
            functools.partial(ready_kernel, slots),
            (array(n, MORE, *tile), array(n, PAIRS, *tile, dtype=bf16)),
            x, kern, e2, edge, rim, scale, rim_scale, *saved, name=name, cost=BESIDE,
        )

    inner_slots, outer_slots = range(per), range(per, 2 * per)
    joined, others = ((array(256, HEAD_DIM),), (array(*tile),)) if rows else ((array(384, HEAD_DIM),), ())
    outer, *outer_saved = local(outer_slots, "local_outer")
    outer_recv = swapped(outer, 1)
    inner, *inner_saved = local(inner_slots, "local_inner")
    pairs = spot(join_kernel, joined * per + others * per, inner, outer_recv, name="join")
    parts = [pairs[0]] + [swapped(pairs[n], 2 * n) for n in range(1, count)]
    second = [pairs[per]] + [swapped(pairs[per + n], 2 * n) for n in range(1, count)] if rows else []
    outer_saved += prepared(outer_slots, outer_saved, "ready_outer")
    inner_saved += prepared(inner_slots, inner_saved, "ready_inner")
    ahead = [outer_saved[-1], inner_saved[-1]]

    held = pltpu.VMEM((count, 256 if rows else 384, HEAD_DIM), f32)
    square = array(*tile)
    step = 2 * count

    def returned(values):
        return [values[0]] + [swapped(values[n], 2 * n) for n in range(1, count)]

    if rows:
        found = pltpu.VMEM((count, *tile), f32)
        total, products, sure = spot(
            functools.partial(two_gather_kernel, len(ahead)),
            (square, array(2, *tile), array(4, *tile)),
            *parts, name="gather", scratch=[held], unread=ahead,
        )
        other = swapped(total, step)
        reach, *early = spot(
            reach_kernel, (array(6, *tile, dtype=bf16),) + (square,) * 4,
            *parts, products, sure, name="reach", scratch=[held], cost=BESIDE,
        )
        early = returned(early)
        (known,) = spot(
            known_kernel, (array(4, *tile),), *parts, *second, name="known", scratch=[held, found], cost=BESIDE
        )
        late = spot(late_kernel, (square,) * 4, other, known, reach, name="late", scratch=[found])
        states = list(zip(early, returned(late)))
    else:
        gathered = spot(
            functools.partial(gather_kernel, count, len(ahead)), (square,) * 3,
            *parts, name="gather", scratch=[held], unread=ahead,
        )
        ends = (jnp.zeros(tile, f32),) * 2
        for hop in range(slabs - 1):
            if hop == 0:
                ends = gathered[1:]
            else:
                ends = spot(hop_kernel, (square,) * 2, *gathered, *ends, name=f"hop{hop}")
            ends = (moved(ends[0], step), moved(ends[1], -step))
        spread = returned(
            spot(
                functools.partial(spread_kernel, count), (array(256, HEAD_DIM),) * count,
                *parts, *ends, name="spread", scratch=[held, pltpu.VMEM((count, 256, HEAD_DIM), f32)],
            )
        )
        states = [(a,) for a in spread]

    keeps, recvs = (inner,), (outer_recv,)
    mine, send = spot(
        functools.partial(part_kernel, len(keeps), len(states[0])), (array(per, 256, HEAD_DIM),) * 2,
        *keeps, *recvs, *(a for pair in states for a in pair), name="part",
    )
    far = swapped(send, 1)

    def backward(slots, saved, homes, states, chain, name):
        n = len(slots)
        chained = chain is not None
        before = (chain[2], chain[3]) if chained else ()
        return spot(
            functools.partial(back_kernel, slots, homes, chained),
            (
                array(*inputs.shape, dtype=bf16), array(n, length, HEAD_DIM), array(RIM, length),
                array(RIM, channels + HEAD_DIM),
            )
            + (array(RIM, HEAD_DIM),) * chained,
            *shared, states, *(a for group in saved for a in group), *before, name=name, far_out=(0,),
            alias=chain[0] if chained else None,
            scratch=[pltpu.VMEM((n, length, HEAD_DIM), bf16), pltpu.SemaphoreType.DMA((n,))],
        )

    slots = range(heads)
    homes = [(0, n) for n in range(per)]
    chain = backward(slots[:per], [inner_saved], homes, mine, None, "back_inner")
    grads = [chain[1]]
    chain = backward(slots[per:], [outer_saved], homes, far, chain, "back_outer")
    grads.append(chain[1])
    stream_out, _, inner_sum, rim_grad, rim_sums = chain

    inner_total, next_sums = inner_sum, 0.0
    for sec in range(1, sections):
        inner_total = inner_total + turned(inner_sum, sec, 0)
        next_sums = next_sums + turned(rim_sums, sec, -1)
    next_rim = turned(rim_grad, 0, -1)
    (input_grad,) = spot(
        functools.partial(finish_kernel, slots, width), (array(*inputs.shape, dtype=bf16),),
        x, go, scale, inner_total, next_sums + next_rim[:, channels:], next_rim, *grads, name="finish",
        far_out=(0,), scratch=[pltpu.VMEM((heads, length, HEAD_DIM), bf16), pltpu.SemaphoreType.DMA((heads,))],
    )
    return (stream_out, input_grad)


def solution(mesh):
    in_specs = (
        P("ctx", "section"),
        P("ctx", "section"),
        P(None, None, "section"),
        P("ctx", "section"),
        P("ctx", "section"),
    )
    out_specs = (P("ctx", "section"), P("ctx", "section"))
    return jax.shard_map(shards, mesh=mesh, in_specs=in_specs, out_specs=out_specs, check_vma=False)
```

```python
import functools

import jax
import jax.numpy as jnp
from jax import lax
from jax.experimental import pallas as pl
from jax.experimental.pallas import tpu as pltpu
from jax.sharding import PartitionSpec as P

HEAD_DIM = 128
RIM = 8
epsilon = 1e-06
norm_eps = 1e-05
f32 = jnp.float32
bf16 = jnp.bfloat16
VMEM_LIMIT = 24 * 1024 * 1024

DIMS = {
    "nn": (((1,), (0,)), ((), ())),
    "nt": (((1,), (1,)), ((), ())),
    "tn": (((0,), (0,)), ((), ())),
}


def split(a):
    high = a.astype(bf16)
    return high, (a - high.astype(f32)).astype(bf16)


def exact(a):
    return a, None


def rows_of(*parts):
    highs = jnp.concatenate([p[0] for p in parts], axis=0)
    lows = [jnp.zeros_like(p[0]) if p[1] is None else p[1] for p in parts]
    return highs, jnp.concatenate(lows, axis=0)


def cols_of(*parts):
    return tuple(jnp.concatenate([p[i] for p in parts], axis=1) for i in range(2))


def mm(a, b, form):
    width = b[0].shape[1]
    if form != "nt" and a[1] is not None and b[1] is not None and width == HEAD_DIM:
        right = jnp.concatenate(b, axis=1)
        left = jnp.concatenate(a, axis=0 if form == "tn" else 1)
        out = lax.dot_general(left, jnp.concatenate([right, right], axis=0), DIMS[form], preferred_element_type=f32)
        return out[:, :width] + out[:, width:]
    pairs = [(a[0], b[0])]
    if a[1] is not None:
        pairs.append((a[1], b[0]))
    if b[1] is not None:
        pairs.append((a[0], b[1]))
    left = jnp.concatenate([p[0] for p in pairs], axis=0 if form == "tn" else 1)
    right = jnp.concatenate([p[1] for p in pairs], axis=1 if form == "nt" else 0)
    return lax.dot_general(left, right, DIMS[form], preferred_element_type=f32)


def row_sums(a):
    terms = jnp.concatenate(split(a), axis=1)
    ones = jnp.ones((RIM, terms.shape[1]), bf16)
    return lax.dot_general(ones, terms, DIMS["nt"], preferred_element_type=f32)


def down_rows(row):
    return jnp.transpose(jnp.broadcast_to(row[0:1], (HEAD_DIM, row.shape[1])))


def iotas(n=HEAD_DIM):
    return (
        lax.broadcasted_iota(jnp.int32, (n, n), 0),
        lax.broadcasted_iota(jnp.int32, (n, n), 1),
    )


def lane_slice(place):
    return pl.ds(pl.multiple_of(place * HEAD_DIM, HEAD_DIM), HEAD_DIM)


def prelude_kernel(
    x_hbm, go_hbm, kern_hbm, decay_hbm, beta_hbm, payload_ref, sums_ref, last_sums_ref, x_ref, go_ref, kern_ref,
    decay_ref, beta_ref, sems,
):
    pairs = ((x_hbm, x_ref), (go_hbm, go_ref), (kern_hbm, kern_ref), (decay_hbm, decay_ref), (beta_hbm, beta_ref))
    copies = [pltpu.make_async_copy(src, dst, sems.at[n]) for n, (src, dst) in enumerate(pairs)]
    for copy in copies:
        copy.start()
    copies[0].wait()
    x = x_ref[...].astype(f32)
    length, channels = x.shape
    blocks = [x[:, n : n + HEAD_DIM] for n in range(0, channels, HEAD_DIM)]
    squares = sum(block * block for block in blocks)
    sums_ref[...] = row_sums(squares)
    last = jnp.sum(squares[length - RIM :], axis=1, keepdims=True)
    last = jnp.broadcast_to(last, (RIM, HEAD_DIM))
    last_sums_ref[...] = last
    payload_ref[:, :channels] = x[length - RIM :]
    payload_ref[:, channels:] = last
    for copy in copies[1:]:
        copy.wait()


BASE = 5


def inverse_all(systems):
    row, col = iotas()
    size = 1 << BASE
    own = row >> BASE == col >> BASE
    row8 = lax.broadcasted_iota(jnp.int32, (RIM, HEAD_DIM), 0)
    col8 = lax.broadcasted_iota(jnp.int32, (RIM, HEAD_DIM), 1)
    first = (col8 >> BASE) << BASE
    found = []
    for n in systems:
        blocks = jnp.sum(jnp.where(own, n, 0.0).reshape(-1, size, HEAD_DIM), axis=0)
        tiles = [jnp.where(row8 + RIM * t == (col8 & (size - 1)), 1.0, 0.0) for t in range(size // RIM)]
        for s in range(size - 1):
            done = tiles[s // RIM][s % RIM : s % RIM + 1]
            for t in range(s // RIM, size // RIM):
                column = jnp.take_along_axis(
                    blocks[RIM * t : RIM * (t + 1)], first + s, axis=1, mode="promise_in_bounds"
                )
                tiles[t] = tiles[t] - column * done
        found.append(jnp.where(own, jnp.concatenate(tiles * (HEAD_DIM // size), axis=0), 0.0))
    level = BASE
    while (1 << level) < HEAD_DIM:
        mask = (row >> (level + 2) == col >> (level + 2)) & (row >> level != col >> level)
        parts = [split(d) for d in found]
        cross = [split(jnp.where(mask, n, 0.0)) for n in systems]
        maps = [split(mm(p, c, "nn")) for p, c in zip(parts, cross)]
        twice = [mm(m, cols_of(m, p), "nn") for m, p in zip(maps, parts)]
        less = [d - t[:, HEAD_DIM:] for d, t in zip(found, twice)]
        found = [y + mm(split(t[:, :HEAD_DIM]), split(y), "nn") for y, t in zip(less, twice)]
        level += 2
    return found


def mixes_of(normed, rim, kern):
    row8 = lax.broadcasted_iota(jnp.int32, (RIM, HEAD_DIM), 0)
    taps = kern.shape[1]
    shifted = [normed]
    for s in range(1, taps):
        moved = pltpu.roll(normed, s, 0)
        first = jnp.where(row8 < s, pltpu.roll(rim, s, 0), moved[:RIM])
        shifted.append(jnp.concatenate([first, moved[RIM:]], axis=0))
    return [
        sum(kern[j, i : i + 1] * shifted[taps - 1 - i] for i in range(taps)) for j in range(3)
    ]


def gates_kernel(width, decay_ref, beta_ref, sums_ref, e1_ref, e2_ref, edge_ref, rate_ref, scale_ref):
    scale_ref[...] = down_rows(lax.rsqrt(sums_ref[...] / width + norm_eps))
    length = decay_ref.shape[0]
    row, col = iotas()
    tril = jnp.where(row >= col, 1.0, 0.0).astype(bf16)
    tril = jnp.concatenate([tril] * 3, axis=1)
    for head in range(decay_ref.shape[1] // HEAD_DIM):
        here = slice(head * HEAD_DIM, (head + 1) * HEAD_DIM)
        decay = decay_ref[:, here]
        high = decay.astype(bf16)
        rest = decay - high.astype(f32)
        mid = rest.astype(bf16)
        low = (rest - mid.astype(f32)).astype(bf16)
        cumulative = lax.dot_general(
            tril, jnp.concatenate([high, mid, low], axis=0), DIMS["nn"], preferred_element_type=f32
        )
        middle = cumulative[length // 2 : length // 2 + 1]
        final = cumulative[length - 1 : length]
        e1_ref[:, here] = jnp.exp(cumulative - middle)
        e2_ref[:, here] = jnp.exp(middle - cumulative)
        edge_ref[0:8, here] = jnp.broadcast_to(jnp.exp(middle), (8, HEAD_DIM))
        edge_ref[8:16, here] = jnp.broadcast_to(jnp.exp(final - middle), (8, HEAD_DIM))
        edge_ref[16:24, here] = jnp.broadcast_to(jnp.exp(final), (8, HEAD_DIM))
        rate_ref[:, here] = down_rows(beta_ref[head : head + 1])


def scaled(x_ref, rim_ref, kern_ref, scale, rim_scale, at):
    x = x_ref[:, at].astype(f32)
    return mixes_of(x * scale, rim_ref[:, at] * rim_scale, kern_ref[:, :, at])


def scales(flags, scale_ref, rim_scale_ref):
    return scale_ref[...], jnp.where(flags[4] != 0, rim_scale_ref[...], 0.0)


def keep_split(ref, j, n, parts):
    ref[j, n] = parts[0]
    ref[j, n + 1] = parts[1]


def kept(ref, j, n):
    return ref[j, n], ref[j, n + 1]


def local_kernel(
    slots, flags, x_ref, go_ref, kern_ref, e1_ref, e2_ref, edge_ref, rate_ref, rim_ref, scale_ref, rim_scale_ref,
    *rest,
):
    comp_ref, wide_ref, narrow_ref = rest[-3:]
    length = x_ref.shape[0]
    row, col = iotas()
    strict, full = row > col, row >= col
    scale, rim_scale = scales(flags, scale_ref, rim_scale_ref)
    data = []
    for j, slot in enumerate(slots):
        at = lane_slice(slot ^ flags[0])
        mixes = scaled(x_ref, rim_ref, kern_ref, scale, rim_scale, at)
        act = [m / (1.0 + jnp.exp(-m)) for m in mixes]
        q, k = [a * lax.rsqrt(jnp.sum(a * a, axis=1, keepdims=True) + epsilon) for a in act[:2]]
        rate, e1, e2 = rate_ref[:, at], e1_ref[:, at], e2_ref[:, at]
        em, ecm, ef = [edge_ref[n : n + 1, at] for n in (0, 8, 16)]
        qf, kf, kb = q * e1, k * e1, k * e2
        skf, sqf, skb = split(kf), split(qf), split(kb)
        products = mm(rows_of(skf, sqf), skb, "nt")
        system = jnp.where(strict, rate * products[:length], 0.0)
        scores = split(jnp.where(full, products[length:], 0.0))
        go = exact(go_ref[:, at])
        wide_ref[j, 0], wide_ref[j, 1] = q, k
        for n, parts in enumerate((skf, sqf, skb, scores)):
            keep_split(narrow_ref, j, 2 * n, parts)
        data.append(
            dict(system=system, go=go, rhs=cols_of(split(rate * kf * em), split(rate * act[2])), ke=split(kb * ecm),
                 qg=qf * em, scores=scores, ef=ef)
        )
    inverses = inverse_all([d["system"] for d in data])
    for j, d in enumerate(data):
        d["fresh_grad"] = split(mm(d["scores"], d["go"], "tn"))
        keep_split(narrow_ref, j, 8, d["fresh_grad"])
    for j, (d, inverse) in enumerate(zip(data, inverses)):
        inverse = split(inverse)
        keep_split(narrow_ref, j, 14, inverse)
        solved = mm(inverse, d["rhs"], "nn")
        wide_ref[j, 2] = solved[:, HEAD_DIM:]
        d["solved"] = split(solved)
    for j, d in enumerate(data):
        solved = d["solved"]
        keep_split(narrow_ref, j, 10, (solved[0][:, :HEAD_DIM], solved[1][:, :HEAD_DIM]))
        keep_split(narrow_ref, j, 12, (solved[0][:, HEAD_DIM:], solved[1][:, HEAD_DIM:]))
        maps = mm(d["ke"], solved, "tn")
        comp_ref[j, 0:128] = jnp.where(row == col, d["ef"], 0.0) - maps[:, :HEAD_DIM]
        comp_ref[j, 128:256] = maps[:, HEAD_DIM:]
        w = (solved[0][:, :HEAD_DIM], solved[1][:, :HEAD_DIM])
        comp_ref[j, 256:384] = mm(split(d["qg"]), d["go"], "tn") - mm(w, d["fresh_grad"], "tn")


WIDE, NARROW = 3, 16


def ready_kernel(
    slots, flags, x_ref, kern_ref, e2_ref, edge_ref, rim_ref, scale_ref, rim_scale_ref, wide_ref, narrow_ref,
    more_ref, pairs_ref,
):
    scale, rim_scale = scales(flags, scale_ref, rim_scale_ref)
    for j, slot in enumerate(slots):
        at = lane_slice(slot ^ flags[0])
        mixes = scaled(x_ref, rim_ref, kern_ref, scale, rim_scale, at)
        sig = [1.0 / (1.0 + jnp.exp(-m)) for m in mixes]
        slope = [s * (1.0 + m * (1.0 - s)) for m, s in zip(mixes, sig)]
        act = [m * s for m, s in zip(mixes[:2], sig)]
        inv = [lax.rsqrt(jnp.sum(a * a, axis=1, keepdims=True) + epsilon) for a in act]
        em, ecm = edge_ref[0:1, at], edge_ref[8:9, at]
        scores, fresh_grad, inverse = [kept(narrow_ref, j, n) for n in (6, 8, 14)]
        solved = cols_of(kept(narrow_ref, j, 10), kept(narrow_ref, j, 12))
        seen = mm(scores, solved, "nn")
        ke = split(wide_ref[j, 1] * e2_ref[:, at] * ecm)
        back = mm(inverse, cols_of(fresh_grad, ke), "tn")
        more_ref[j, 0] = slope[0] * inv[0]
        more_ref[j, 1] = slope[1] * inv[1]
        more_ref[j, 2] = slope[2]
        more_ref[j, 3] = seen[:, HEAD_DIM:]
        more_ref[j, 4] = back[:, :HEAD_DIM]
        qf = narrow_ref[j, 2].astype(f32) + narrow_ref[j, 3].astype(f32)
        keep_split(pairs_ref, j, 0, split(qf * em - seen[:, :HEAD_DIM]))
        keep_split(pairs_ref, j, 2, split(back[:, HEAD_DIM:]))


MORE, PAIRS = 5, 4


def join_kernel(flags, keep_ref, recv_ref, *outs):
    later, upper = flags[1] != 0, flags[3] != 0
    heads = keep_ref.shape[0]
    for j in range(heads):
        keep, recv = keep_ref[j], recv_ref[j]
        lo = jnp.where(later, recv, keep)
        hi = jnp.where(later, keep, recv)
        lo_map, hi_map = split(lo[0:128]), split(hi[0:128])
        forward = mm(hi_map, cols_of(lo_map, split(lo[128:256])), "nn")
        grad = mm(lo_map, split(hi[256:384]), "tn") + lo[256:384]
        state = forward[:, HEAD_DIM:] + hi[128:256]
        out = outs[j]
        out[0:128] = forward[:, :HEAD_DIM]
        if len(outs) == heads:
            out[128:256], out[256:384] = state, grad
        else:
            out[128:256] = jnp.where(upper, grad, state)
            outs[heads + j][...] = jnp.where(upper, state, grad)


def collect(place, parts, held):
    for n, part in enumerate(parts):
        held[place ^ n] = part[...]


def gather_kernel(count, waits, flags, *refs):
    parts, outs, held = refs[:count], refs[count + waits : -1], refs[-1]
    collect(flags[2], parts, held)
    maps = [split(held[p, 0:128]) for p in range(count)]
    state, grad = held[0, 128:256], held[count - 1, 256:384]
    whole = held[0, 0:128]
    for p in range(1, count):
        state = mm(maps[p], split(state), "nn") + held[p, 128:256]
        grad = mm(maps[count - 1 - p], split(grad), "tn") + held[count - 1 - p, 256:384]
        whole = mm(maps[p], split(whole), "nn")
    outs[0][...], outs[1][...], outs[2][...] = whole, state, grad


def hop_kernel(flags, t_ref, u_ref, g_ref, s_ref, e_ref, s_out, e_out):
    t = split(t_ref[...])
    s_out[...] = mm(t, split(s_ref[...]), "nn") + u_ref[...]
    e_out[...] = mm(t, split(e_ref[...]), "tn") + g_ref[...]


def spread_kernel(count, flags, *refs):
    parts, ins, outs, held, found = refs[:count], refs[count : -2 - count], refs[-2 - count : -2], refs[-2], refs[-1]
    collect(flags[2], parts, held)
    state, grad = ins[0][...], ins[1][...]
    for p in range(count):
        back = count - 1 - p
        found[p, 0:128] = state
        found[back, 128:256] = grad
        if p + 1 < count:
            state = mm(split(held[p, 0:128]), split(state), "nn") + held[p, 128:256]
            grad = mm(split(held[back, 0:128]), split(grad), "tn") + held[back, 256:384]
    for n, out in enumerate(outs):
        out[...] = found[flags[2] ^ n]


def two_gather_kernel(waits, flags, *refs):
    parts, outs = refs[:4], refs[4 + waits : -1]
    held = refs[-1]
    total_ref, pairs_ref, found_ref = outs
    upper = flags[3] != 0
    collect(flags[2], parts, held)
    t = [split(held[p, 0:128]) for p in range(4)]
    u = [held[p, 128:256] for p in range(4)]
    su = [split(a) for a in u]
    last = mm(t[3], cols_of(t[2], su[2]), "nn")
    first = mm(t[1], cols_of(t[0], su[0]), "nn")
    second = first[:, HEAD_DIM:] + u[1]
    first, last, last_u = first[:, :HEAD_DIM], last[:, :HEAD_DIM], last[:, HEAD_DIM:]
    third = mm(t[2], su[3], "tn") + u[2]
    low = mm(t[0], su[1], "tn")
    s_second, s_third = split(second), split(third)
    forward = [jnp.zeros_like(second), u[0], second, mm(t[2], s_second, "nn") + u[2]]
    back = [mm(t[1], s_third, "tn") + u[1], third, u[3], jnp.zeros_like(third)]
    state = mm(split(last), s_second, "nn") + (last_u + u[3])
    grad = mm(split(first), s_third, "tn") + (low + u[0])
    total_ref[...] = jnp.where(upper, grad, state)
    pairs_ref[0], pairs_ref[1] = first, last
    for p in range(4):
        found_ref[p] = jnp.where(upper, back[p], forward[p])


def known_kernel(flags, *refs):
    parts, others, known_ref, held, values = refs[:4], refs[4:8], refs[8], refs[9], refs[10]
    upper = flags[3] != 0
    collect(flags[2], parts, held)
    collect(flags[2], others, values)
    t = [split(held[p, 0:128]) for p in (1, 2)]
    second = mm(t[0], split(values[0]), "nn") + values[1]
    third = mm(t[1], split(second), "nn") + values[2]
    below = mm(t[1], split(values[3]), "tn") + values[2]
    lowest = mm(t[0], split(below), "tn") + values[1]
    for n, (up, down) in enumerate(((values[0], values[3]), (second, below), (third, lowest))):
        known_ref[n + 1] = jnp.where(upper, up, down)
    known_ref[0] = jnp.zeros_like(second)


def reach_kernel(flags, *refs):
    parts, pairs_ref, found_ref, out_ref, early, held = refs[:4], refs[4], refs[5], refs[6], refs[7:11], refs[11]
    for n, out in enumerate(early):
        out[...] = found_ref[flags[2] ^ n]
    upper = flags[3] != 0
    collect(flags[2], parts, held)
    first, last = pairs_ref[0], pairs_ref[1]
    far_up = mm(split(held[2, 0:128]), split(first), "nn")
    far_down = mm(split(last), split(held[1, 0:128]), "nn")
    ups, downs = (held[0, 0:128], first, far_up), (held[3, 0:128], last, far_down)
    for n in range(3):
        high, low = split(jnp.where(upper, ups[n], jnp.transpose(downs[n])))
        out_ref[2 * n], out_ref[2 * n + 1] = high, low


def late_kernel(flags, recv_ref, known_ref, reach_ref, *refs):
    outs, found = refs[:-1], refs[-1]
    from_end = jnp.where(flags[3] != 0, 0, 3)
    recv = recv_ref[...]
    parts = split(recv)
    found[from_end] = recv
    for n in range(3):
        found[from_end ^ (n + 1)] = mm((reach_ref[2 * n], reach_ref[2 * n + 1]), parts, "nn") + known_ref[n + 1]
    for n, out in enumerate(outs):
        out[...] = found[flags[2] ^ n]


def part_kernel(sets, per_head, flags, *refs):
    maps = [(keep, recv, n) for keep, recv in zip(refs[:sets], refs[sets : 2 * sets]) for n in range(keep.shape[0])]
    ins, (mine_ref, send_ref) = refs[2 * sets : -2], refs[-2:]
    later, upper = flags[1] != 0, flags[3] != 0
    for j, (keep_ref, recv_ref, n) in enumerate(maps):
        if per_head == 1:
            start, end = ins[j][0:128], ins[j][128:256]
        else:
            early, late = ins[2 * j][...], ins[2 * j + 1][...]
            start, end = jnp.where(upper, late, early), jnp.where(upper, early, late)
        keep, recv = keep_ref[n], recv_ref[n]
        lo = jnp.where(later, recv, keep)
        hi = jnp.where(later, keep, recv)
        start_hi = mm(split(lo[0:128]), split(start), "nn") + lo[128:256]
        end_lo = mm(split(hi[0:128]), split(end), "tn") + hi[256:384]
        mine_ref[j, 0:128] = jnp.where(later, start_hi, start)
        mine_ref[j, 128:256] = jnp.where(later, end, end_lo)
        send_ref[j, 0:128] = jnp.where(later, start, start_hi)
        send_ref[j, 128:256] = jnp.where(later, end_lo, end)


def back_kernel(
    slots, homes, chained, flags, x_ref, go_ref, kern_ref, e1_ref, e2_ref, edge_ref, rate_ref, rim_ref, state_ref,
    *rest,
):
    sets = 1 + max(n for n, _ in homes)
    saved, rest = [rest[4 * n : 4 * n + 4] for n in range(sets)], rest[4 * sets :]
    if chained:
        sums_in, rim_grad_in, rest = rest[0], rest[1], rest[3:]
    out_hbm, grad_ref, sums_ref, rim_grad_ref, out_ref, sems = rest[:4] + rest[-2:]
    length = x_ref.shape[0]
    channels = x_ref.shape[1]
    row, col = iotas()
    row8 = lax.broadcasted_iota(jnp.int32, (RIM, HEAD_DIM), 0)
    strict, full = row > col, row >= col
    taps = kern_ref.shape[1]
    if chained:
        rim_grad_ref[...] = rim_grad_in[...]
    dot_all = rim_dot = 0.0
    data, copies = [], []
    for j, (slot, (n, i)) in enumerate(zip(slots, homes)):
        at = lane_slice(slot ^ flags[0])
        wide_ref, narrow_ref, more_ref, pairs_ref = saved[n]
        start, end = split(state_ref[j, 0:128]), split(state_ref[j, 128:256])
        first = mm(rows_of(kept(pairs_ref, i, 0), kept(narrow_ref, i, 10)), start, "nn")
        z = more_ref[i, 4] + mm(kept(pairs_ref, i, 2), end, "nn")
        x = x_ref[:, at].astype(f32)
        out_ref[j] = (x + (more_ref[i, 3] + first[:length])).astype(bf16)
        copies.append(pltpu.make_async_copy(out_ref.at[j], out_hbm.at[:, at], sems.at[j]))
        copies[-1].start()
        data.append(dict(at=at, x=x, start=start, end=end, z=z, fresh=split(wide_ref[i, 2] - first[length:])))
    for j, (d, (n, i)) in enumerate(zip(data, homes)):
        at = d["at"]
        wide_ref, narrow_ref, more_ref, _ = saved[n]
        q, k = wide_ref[i, 0], wide_ref[i, 1]
        gq, gk, gv = [more_ref[i, n] for n in range(3)]
        skf, sqf, skb = [kept(narrow_ref, i, n) for n in (0, 2, 4)]
        e1, e2, rate = e1_ref[:, at], e2_ref[:, at], rate_ref[:, at]
        em, ecm = edge_ref[0:1, at], edge_ref[8:9, at]
        go = exact(go_ref[:, at])
        second = mm(rows_of(go, split(d["z"])), rows_of(d["fresh"], d["start"]), "nt")
        score_grad = split(jnp.where(full, second[:length, :HEAD_DIM], 0.0))
        product_grad = split(jnp.where(strict, -rate * second[length:, :HEAD_DIM], 0.0))
        qg_grad = second[:length, HEAD_DIM:]
        kg_grad = -rate * second[length:, HEAD_DIM:]
        ke_grad = mm(d["fresh"], d["end"], "nt")
        pair = rows_of(score_grad, product_grad)
        third = mm(pair, skb, "nn")
        kb_grad = mm(pair, rows_of(sqf, skf), "tn")
        q_grad = e1 * (third[:length] + em * qg_grad)
        k_grad = e1 * (third[length:] + em * kg_grad) + e2 * (kb_grad + ecm * ke_grad)
        mix_grads = [
            gq * (q_grad - q * jnp.sum(q * q_grad, axis=1, keepdims=True)),
            gk * (k_grad - k * jnp.sum(k * k_grad, axis=1, keepdims=True)),
            gv * (rate * d["z"]),
        ]
        kern = kern_ref[:, :, at]
        normed_grad = rim_grad = 0.0
        for i in range(taps):
            each = sum(kern[n, i : i + 1] * mix_grads[n] for n in range(3))
            s = taps - 1 - i
            if s == 0:
                normed_grad = normed_grad + each
            else:
                moved = pltpu.roll(each, length - s, 0)
                normed_grad = normed_grad + jnp.where(row < length - s, moved, 0.0)
                rim_grad = rim_grad + jnp.where(row8 >= RIM - s, moved[length - RIM :], 0.0)
        grad_ref[j] = normed_grad
        rim_grad_ref[:, at] = rim_grad
        dot_all = dot_all + normed_grad * d["x"]
        rim_dot = rim_dot + rim_grad * rim_ref[:, at]
    sums = row_sums(dot_all)
    rim_sums = jnp.broadcast_to(jnp.sum(rim_dot, axis=1, keepdims=True), rim_dot.shape)
    if chained:
        sums, rim_sums = sums + sums_in[...], rim_sums + rim_grad_in[:, channels:]
    sums_ref[...] = sums
    rim_grad_ref[:, channels:] = rim_sums
    if chained:
        rest[4][...] = rim_sums
    for copy in copies:
        copy.wait()


def finish_kernel(slots, width, flags, x_ref, go_ref, scale_ref, inner_ref, next_sums_ref, next_ref, *refs):
    grads, (out_hbm, out_ref, sems) = refs[:-3], refs[-3:]
    length = x_ref.shape[0]
    scale = scale_ref[...]
    inner = down_rows(inner_ref[...])
    last = flags[5] == 0
    next_sums = jnp.where(last, 0.0, next_sums_ref[...])
    inner = jnp.concatenate([inner[: length - RIM], inner[length - RIM :] + next_sums], axis=0)
    cubed = scale * scale * scale * inner * (1.0 / width)
    copies = []
    places = [(ref, n) for ref in grads for n in range(ref.shape[0])]
    for j, (slot, (grad_ref, n)) in enumerate(zip(slots, places)):
        at = lane_slice(slot ^ flags[0])
        grad = grad_ref[n]
        next_grad = jnp.where(last, 0.0, next_ref[:, at])
        grad = jnp.concatenate([grad[: length - RIM], grad[length - RIM :] + next_grad], axis=0)
        total = go_ref[:, at].astype(f32) + grad * scale - x_ref[:, at].astype(f32) * cubed
        out_ref[j] = total.astype(bf16)
        copies.append(pltpu.make_async_copy(out_ref.at[j], out_hbm.at[:, at], sems.at[j]))
        copies[-1].start()
    for copy in copies:
        copy.wait()


def call(kernel, outs, *args, name=None, scratch=(), scalar=(), cost=None, far_in=False, far_out=(), unread=(), alias=None):
    spec, hbm = pl.BlockSpec(memory_space=pltpu.VMEM), pl.BlockSpec(memory_space=pltpu.HBM)
    in_specs = [hbm if far_in else spec] * len(args)
    in_specs += [pl.BlockSpec(memory_space=pl.ANY)] * len(unread)
    args = args + tuple(unread)
    aliases = {}
    if alias is not None:
        args, in_specs, aliases = args + (alias,), in_specs + [hbm], {len(args): 0}
    return pl.pallas_call(
        (lambda *refs: kernel(placed(*scalar), *refs)) if scalar else kernel,
        out_shape=list(outs),
        in_specs=in_specs,
        out_specs=[hbm if n in far_out else spec for n in range(len(outs))],
        scratch_shapes=scratch,
        input_output_aliases=aliases,
        compiler_params=pltpu.CompilerParams(vmem_limit_bytes=VMEM_LIMIT),
        cost_estimate=cost,
        name=name,
    )(*args)


BESIDE = pl.CostEstimate(flops=0, bytes_accessed=0, transcendentals=0)


def array(*shape, dtype=f32):
    return jax.ShapeDtypeStruct(shape, dtype)


def placed(per, spots):
    me = lax.axis_index("ctx")
    place, later = lax.rem(lax.shift_right_logical(me, 1), per), lax.rem(me, 2)
    row = lax.rem(lax.div(me, 2 * per), 2)
    return [later * per + place, later, place, row, me, spots - 1 - me]


def shards(inputs, out_grads, conv_weight, log_decay, beta):
    length, channels = inputs.shape
    heads = channels // HEAD_DIM
    sections, spots = lax.axis_size("section"), lax.axis_size("ctx")
    width = channels * sections
    per = heads // 2
    count = per
    slabs = spots // (2 * count)
    rows = slabs == 2 and count == 4
    spot = functools.partial(call, scalar=(per, spots))

    def turned(value, sec, shift):
        route = [
            (s * spots + c, ((s + sec) % sections) * spots + (c + shift) % spots)
            for s in range(sections)
            for c in range(spots)
        ]
        return lax.ppermute(value, ("section", "ctx"), route)

    def swapped(value, distance):
        return lax.ppermute(value, "ctx", [(i, i ^ distance) for i in range(spots)])

    def moved(value, shift):
        return lax.ppermute(
            value, "ctx", [(i, i + shift) for i in range(spots) if 0 <= i + shift < spots]
        )

    payload, sums, last_sums, x, go, kern, decay, rates = call(
        prelude_kernel,
        (
            array(RIM, channels + HEAD_DIM), array(RIM, length), array(RIM, HEAD_DIM), array(*inputs.shape, dtype=bf16),
            array(*inputs.shape, dtype=bf16), array(*conv_weight.shape), array(*inputs.shape), array(heads, length),
        ),
        *[pltpu.with_memory_space_constraint(a, pltpu.HBM) for a in (inputs, out_grads, conv_weight, log_decay, beta.T)],
        name="prelude", far_in=True, scratch=[pltpu.SemaphoreType.DMA((5,))],
    )
    total = sums
    rim_total = 0.0
    for sec in range(1, sections):
        total = total + turned(sums, sec, 0)
        rim_total = rim_total + turned(last_sums, sec, 1)
    rim = turned(payload, 0, 1)
    e1, e2, edge, rate, scale = call(
        functools.partial(gates_kernel, width),
        (array(length, channels), array(length, channels), array(24, channels), array(length, channels),
         array(length, HEAD_DIM)),
        decay, rates, total, name="gates", cost=BESIDE,
    )
    rim_scale = lax.rsqrt((rim_total + rim[:, channels:]) / width + norm_eps)

    shared = (x, go, kern, e1, e2, edge, rate, rim)
    tile = (HEAD_DIM, HEAD_DIM)

    def local(slots, name, unread=()):
        n = len(slots)
        return spot(
            functools.partial(local_kernel, slots),
            (array(n, 384, HEAD_DIM), array(n, WIDE, *tile), array(n, NARROW, *tile, dtype=bf16)),
            *shared, scale, rim_scale, name=name, unread=unread, cost=BESIDE,
        )

    def prepared(slots, saved, name):
        n = len(slots)
        return spot(
            functools.partial(ready_kernel, slots),
            (array(n, MORE, *tile), array(n, PAIRS, *tile, dtype=bf16)),
            x, kern, e2, edge, rim, scale, rim_scale, *saved, name=name, cost=BESIDE,
        )

    inner_slots, outer_slots = range(per), range(per, 2 * per)
    joined, others = ((array(256, HEAD_DIM),), (array(*tile),)) if rows else ((array(384, HEAD_DIM),), ())
    outer, *outer_saved = local(outer_slots, "local_outer")
    outer_recv = swapped(outer, 1)
    inner, *inner_saved = local(inner_slots, "local_inner")
    pairs = spot(join_kernel, joined * per + others * per, inner, outer_recv, name="join")
    parts = [pairs[0]] + [swapped(pairs[n], 2 * n) for n in range(1, count)]
    second = [pairs[per]] + [swapped(pairs[per + n], 2 * n) for n in range(1, count)] if rows else []
    outer_saved += prepared(outer_slots, outer_saved, "ready_outer")
    inner_saved += prepared(inner_slots, inner_saved, "ready_inner")
    ahead = [outer_saved[-1], inner_saved[-1]]

    held = pltpu.VMEM((count, 256 if rows else 384, HEAD_DIM), f32)
    square = array(*tile)
    step = 2 * count

    def returned(values):
        return [values[0]] + [swapped(values[n], 2 * n) for n in range(1, count)]

    if rows:
        found = pltpu.VMEM((count, *tile), f32)
        total, products, sure = spot(
            functools.partial(two_gather_kernel, len(ahead)),
            (square, array(2, *tile), array(4, *tile)),
            *parts, name="gather", scratch=[held], unread=ahead,
        )
        other = swapped(total, step)
        reach, *early = spot(
            reach_kernel, (array(6, *tile, dtype=bf16),) + (square,) * 4,
            *parts, products, sure, name="reach", scratch=[held], cost=BESIDE,
        )
        early = returned(early)
        (known,) = spot(
            known_kernel, (array(4, *tile),), *parts, *second, name="known", scratch=[held, found], cost=BESIDE
        )
        late = spot(late_kernel, (square,) * 4, other, known, reach, name="late", scratch=[found])
        states = list(zip(early, returned(late)))
    else:
        gathered = spot(
            functools.partial(gather_kernel, count, len(ahead)), (square,) * 3,
            *parts, name="gather", scratch=[held], unread=ahead,
        )
        ends = (jnp.zeros(tile, f32),) * 2
        for hop in range(slabs - 1):
            if hop == 0:
                ends = gathered[1:]
            else:
                ends = spot(hop_kernel, (square,) * 2, *gathered, *ends, name=f"hop{hop}")
            ends = (moved(ends[0], step), moved(ends[1], -step))
        spread = returned(
            spot(
                functools.partial(spread_kernel, count), (array(256, HEAD_DIM),) * count,
                *parts, *ends, name="spread", scratch=[held, pltpu.VMEM((count, 256, HEAD_DIM), f32)],
            )
        )
        states = [(a,) for a in spread]

    keeps, recvs = (inner,), (outer_recv,)
    mine, send = spot(
        functools.partial(part_kernel, len(keeps), len(states[0])), (array(per, 256, HEAD_DIM),) * 2,
        *keeps, *recvs, *(a for pair in states for a in pair), name="part",
    )
    far = swapped(send, 1)

    def backward(slots, saved, homes, states, chain, name):
        n = len(slots)
        chained = chain is not None
        before = (chain[2], chain[3]) if chained else ()
        return spot(
            functools.partial(back_kernel, slots, homes, chained),
            (
                array(*inputs.shape, dtype=bf16), array(n, length, HEAD_DIM), array(RIM, length),
                array(RIM, channels + HEAD_DIM),
            )
            + (array(RIM, HEAD_DIM),) * chained,
            *shared, states, *(a for group in saved for a in group), *before, name=name, far_out=(0,),
            alias=chain[0] if chained else None,
            scratch=[pltpu.VMEM((n, length, HEAD_DIM), bf16), pltpu.SemaphoreType.DMA((n,))],
        )

    slots = range(heads)
    homes = [(0, n) for n in range(per)]
    chain = backward(slots[:per], [inner_saved], homes, mine, None, "back_inner")
    grads = [chain[1]]
    chain = backward(slots[per:], [outer_saved], homes, far, chain, "back_outer")
    grads.append(chain[1])
    stream_out, _, inner_sum, rim_grad, rim_sums = chain

    inner_total, next_sums = inner_sum, 0.0
    for sec in range(1, sections):
        inner_total = inner_total + turned(inner_sum, sec, 0)
        next_sums = next_sums + turned(rim_sums, sec, -1)
    next_rim = turned(rim_grad, 0, -1)
    (input_grad,) = spot(
        functools.partial(finish_kernel, slots, width), (array(*inputs.shape, dtype=bf16),),
        x, go, scale, inner_total, next_sums + next_rim[:, channels:], next_rim, *grads, name="finish",
        far_out=(0,), scratch=[pltpu.VMEM((heads, length, HEAD_DIM), bf16), pltpu.SemaphoreType.DMA((heads,))],
    )
    return (stream_out, input_grad)


def solution(mesh):
    in_specs = (
        P("ctx", "section"),
        P("ctx", "section"),
        P(None, None, "section"),
        P("ctx", "section"),
        P("ctx", "section"),
    )
    out_specs = (P("ctx", "section"), P("ctx", "section"))
    return jax.shard_map(shards, mesh=mesh, in_specs=in_specs, out_specs=out_specs, check_vma=False)
```
